32 devices in a mesh: groups: 2 (over y), wide: 8 (over z, x), heads: 2 (over core).
Axes of the slice: x: 2, y: 2, z: 4, core: 2. Of those that a mesh axis runs over, the one named last changes fastest.
Arguments:
- queries: bfloat16 [2048, 2048], P(('groups', 'wide'), 'heads'), parts along dimension 0, may hold values from -160 to 160
- encodings: bfloat16 [1024, 3584], P(('groups', 'wide')), parts along dimension 0, may hold values from -6 to 6
- w_key: bfloat16 [896, 2048], P(None, 'heads'), may hold values from -0.1875 to 0.1875
- w_value: bfloat16 [896, 2048], P(None, 'heads'), may hold values from -0.1875 to 0.1875
- block_owner: int32 [32, 64, 1], P(('groups', 'wide')), parts along dimension 0, may hold values from 0 to 7; in each aligned block of 128 rows (0 to 127, 128 to 255, ..., all dimensions but the last counted through in order) at most 32 rows name the same one
- block_row: int32 [32, 64], P(('groups', 'wide')), parts along dimension 0, may hold values from 0 to 63
Outputs:
- attended: bfloat16 [2048, 2048], P(('groups', 'wide'), 'heads'), parts along dimension 0
The draws below stay inside these ranges and needn't reach their ends.
There are 2 independent parts, one for each index of `groups`. The reference program is written for one: setup_inputs(seed, part) draws one part's arguments, and reference() takes and returns one part's arrays. A program takes and returns all parts, laid end to end along the dimension named above; an argument that names none is the same for every part. Nothing has to cross between parts.
Inputs may be any that keep to these rules, and one draw needn't show every extreme that they name: `block_owner`: within the requests of one index of wide, no owner is named more than 32 times, a bound that some block reaches.
All inputs are finite; a program needn't handle non-finite values.
Results may differ from the reference program's by a relative error of at most 0.0065.
The reference program's roundings to bfloat16 on the way count: a program that leaves them out, or rounds other values in their place, can miss the bound.
Values may be sent and summed in bfloat16 or wider, within the bound.
No kernel may reach another device: no remote copies, remote signals or barrier semaphores. Data moves between devices by JAX's collectives and lax.ppermute only.
A program may use at most 64 MiB of HBM per device.

```python
import math
import jax
import jax.numpy as jnp
import numpy as np
from jax import lax

HEADS = 16
HD = 128
DE = 896
SPAN = 64
NEIGH = 2
BLK = 4
CH_DEV = 2
ENC_DEV = 64
NBLK = 32
KEYS = 256
TOKENS = 1024
SPANS = 16
ENCODINGS = 512
REQ_DEV = 128
CAP = 32
N_WIDE = 8


def draw_queries(key, part):
    key = jax.random.fold_in(key, 11)
    first = jax.random.fold_in(key, 0)
    shape = (TOKENS, HEADS * HD)
    base = jnp.clip(jax.random.normal(first, shape, jnp.float32), -6.0, 6.0)
    return base.astype(jnp.bfloat16)


def place_ends(values, key, least, largest):
    longest = values.shape.index(max(values.shape))
    spots = []
    for shift in (0, 1):
        where = [jax.random.randint(jax.random.fold_in(key, axis), (), 0, length) for axis, length in enumerate(values.shape)]
        where[longest] = (where[longest] + shift) % values.shape[longest]
        spots.append(tuple(where))
    return values.at[spots[0]].set(least).at[spots[1]].set(largest)


def steps_of(key, extent, shards, least, top_value):
    factor_of, own = 1.0, jax.random.fold_in(key, 6)
    for axis_at, blocks in shards:
        draws = jnp.exp(jax.random.uniform(jax.random.fold_in(own, axis_at), (blocks,), jnp.float32, least / len(shards), top_value / len(shards)))
        factor_of = factor_of * jnp.repeat(draws, extent[axis_at] // blocks).reshape([-1 if axis == axis_at else 1 for axis in range(len(extent))])
    return factor_of


def routed_block(key, own, number, rows, count, top, most, skew):
    sequence = jax.random.permutation(key, count)
    packed, ordinary = load_shares(count, rows * top, most, skew, True), load_shares(count, rows * top, most, skew, False)
    places = jnp.arange(count)

    def named(lengths, offset_by):
        used = int((lengths > 0).sum())
        fixed = max(1, used // 4)
        passed = fixed + (places - fixed + offset_by * (used - fixed)) % max(1, count - fixed)
        return jnp.zeros((count,), jnp.int32).at[sequence[jnp.where(places < fixed, places, passed)]].set(jnp.asarray(lengths, jnp.int32))

    lengths = jnp.where(number % 4 == 0, named(packed, number // 4), named(ordinary, number - number // 4 - 1))
    mixed = jax.random.permutation(jax.random.fold_in(own, 3), count)
    source_of, receiver = mixed[0:count // 2 * 2:2], mixed[1:count // 2 * 2:2]
    margin = jnp.minimum(lengths[source_of] - 1, most - lengths[receiver]) // 2
    margin = jnp.where((source_of == sequence[0]) | (receiver == sequence[0]) | (lengths[receiver] == 0), 0, jnp.maximum(margin, 0))
    passed = jax.random.randint(jax.random.fold_in(own, 4), (count // 2,), 0, 1 << 20) % (margin + 1)
    lengths = lengths.at[source_of].add(-passed).at[receiver].add(passed)
    items = jnp.searchsorted(jnp.cumsum(lengths), jnp.arange(rows * top), side="right").astype(jnp.int32)
    table = items.reshape(top, rows).T
    table = table[jax.random.permutation(jax.random.fold_in(own, 1), rows)]
    offset_by = jax.random.randint(jax.random.fold_in(own, 2), (rows, 1), 0, top)
    return jnp.take_along_axis(table, (jnp.arange(top)[None, :] + offset_by) % top, axis=1)


def load_shares(amount, total, reach, slope, full):
    loads = [(1 << 20) // math.isqrt(standing ** slope) + 1 for standing in range(1, amount + 1)]
    largest = reach if full else min(reach, max(-(-total // amount), total * loads[0] // sum(loads)))
    least = 1 if total - largest >= amount - 1 else 0
    given, rest = [largest] + [least] * (amount - 1), total - largest - least * (amount - 1)
    while rest > 0:
        free = [i for i in range(1, amount) if given[i] < largest] or [i for i in range(1, amount) if given[i] < reach]
        whole, budget = sum([loads[i] for i in free]), rest
        for i in free:
            extra = min(reach - given[i], max(1, budget * loads[i] // whole), rest)
            given[i] = given[i] + extra
            rest = rest - extra
    return np.array(given)


def gaussian(own_key, extent, width, limit, cuts=(), kind=jnp.bfloat16):
    entries = width * jax.random.normal(own_key, extent, jnp.float32)
    if cuts:
        entries = entries * steps_of(own_key, extent, cuts, -0.22, 0.18)
    return jnp.clip(entries, -limit, limit).astype(kind)


def setup_inputs(seed: int = 0, part: int = 0) -> dict:
    key_list = jax.random.split(jax.random.key(seed), 7)
    part_splits = jax.random.split(jax.random.fold_in(key_list[6], part), 7)
    queries = draw_queries(jax.random.fold_in(jax.random.fold_in(key_list[6], part), 71), part)
    encodings = gaussian(part_splits[1], (ENCODINGS, BLK * DE), 1.0, 6.0, ((0, 8),))
    w_key = gaussian(key_list[2], (DE, HEADS * HD), DE ** -0.5, 0.1875, ((1, 2),))
    w_value = gaussian(key_list[3], (DE, HEADS * HD), DE ** -0.5, 0.1875, ((1, 2),))
    block_owner_keys = jax.random.split(jax.random.fold_in(part_splits[4], 1), SPANS * (NEIGH * NBLK) // REQ_DEV)
    block_owner_turns = jax.random.permutation(jax.random.fold_in(part_splits[4], 3), SPANS * (NEIGH * NBLK) // REQ_DEV)
    block_owner = jax.vmap(lambda own, number: routed_block(jax.random.fold_in(part_splits[4], 2), own, number, REQ_DEV, N_WIDE, 1, CAP, 2))(block_owner_keys, block_owner_turns).reshape((SPANS, NEIGH * NBLK, 1))
    block_row = place_ends(jax.random.randint(part_splits[5], (SPANS, NEIGH * NBLK), 0, ENC_DEV), jax.random.fold_in(part_splits[5], 1), 0, ENC_DEV - 1).astype(jnp.int32)
    return dict(queries=queries, encodings=encodings, w_key=w_key, w_value=w_value, block_owner=block_owner, block_row=block_row)


def reference(queries, encodings, w_key, w_value, block_owner, block_row):
    flat_index = (block_owner[..., 0] * ENC_DEV + block_row).astype(jnp.int32)
    grouped_q = queries.reshape(N_WIDE, CH_DEV, SPAN, HEADS, HD)
    grouped_i = flat_index.reshape(N_WIDE, CH_DEV, NEIGH * NBLK)
    scale = HD ** -0.5

    def one_group(items):
        query_part, index_part = items
        blocks = encodings[index_part]
        source = blocks.reshape(CH_DEV * KEYS, DE)
        keys = jnp.dot(source, w_key, preferred_element_type=jnp.float32).astype(jnp.bfloat16)
        values = jnp.dot(source, w_value, preferred_element_type=jnp.float32).astype(jnp.bfloat16)
        keys = keys.reshape(CH_DEV, KEYS, HEADS, HD)
        values = values.reshape(CH_DEV, KEYS, HEADS, HD)
        scores = jnp.einsum("cqhd,ckhd->chqk", query_part.astype(jnp.float32), keys.astype(jnp.float32)) * scale
        probs = jax.nn.softmax(scores, axis=-1).astype(jnp.bfloat16)
        mixed = jnp.einsum("chqk,ckhd->cqhd", probs.astype(jnp.float32), values.astype(jnp.float32))
        return mixed.astype(jnp.bfloat16)

    result = lax.map(one_group, (grouped_q, grouped_i))
    return result.reshape(TOKENS, HEADS * HD)
```

```python
import jax
import jax.numpy as jnp
from jax import lax
from jax.sharding import PartitionSpec as P

HD = 128
SPAN = 64


def exchange(encodings, owners, stored, capacity):
    wide_count = lax.axis_size("wide")
    requests = owners.shape[0]
    order = jnp.arange(requests, dtype=jnp.int32)
    earlier = (owners[:, None] == owners[None, :]) & (order[None, :] < order[:, None])
    rank = jnp.sum(earlier.astype(jnp.int32), axis=1)
    slot = owners * capacity + rank
    table = jnp.full((wide_count * capacity,), -1, jnp.int32).at[slot].set(stored)
    table = table.reshape(wide_count, capacity)
    asked = lax.all_to_all(table, "wide", split_axis=0, concat_axis=0, tiled=True)
    wanted = jnp.maximum(asked, 0)
    picked = encodings[wanted]
    returned = lax.all_to_all(picked, "wide", split_axis=0, concat_axis=0, tiled=True)
    return returned.reshape(wide_count * capacity, encodings.shape[1])[slot]


def gather(encodings, owners, stored):
    rows = encodings.shape[0]
    part = rows // lax.axis_size("heads")
    mine = lax.dynamic_slice_in_dim(encodings, lax.axis_index("heads") * part, part, 0)
    database = lax.all_gather(mine, ("wide", "heads"), axis=0, tiled=True)
    return database[owners * rows + stored]


def on_device(queries, encodings, w_key, w_value, block_owner, block_row):
    wide_count = lax.axis_size("wide")
    owners = block_owner.reshape(-1)
    stored = block_row.reshape(-1)
    requests = owners.shape[0]
    capacity = 2 * ((requests + wide_count - 1) // wide_count)
    if encodings.shape[0] <= 2 * capacity:
        fetched = gather(encodings, owners, stored)
    else:
        fetched = exchange(encodings, owners, stored, capacity)
    channels = w_key.shape[0]
    source = fetched.reshape(-1, channels)
    keys = jnp.dot(source, w_key, preferred_element_type=jnp.float32).astype(jnp.bfloat16)
    values = jnp.dot(source, w_value, preferred_element_type=jnp.float32).astype(jnp.bfloat16)
    span_count = queries.shape[0] // SPAN
    heads_local = w_key.shape[1] // HD
    keys = keys.reshape(span_count, -1, heads_local, HD)
    values = values.reshape(span_count, -1, heads_local, HD)
    query_part = queries.reshape(span_count, SPAN, heads_local, HD)
    scores = jnp.einsum(
        "cqhd,ckhd->chqk", query_part, keys, preferred_element_type=jnp.float32
    ) * HD ** (-0.5)
    probs = jax.nn.softmax(scores, axis=-1).astype(jnp.bfloat16)
    mixed = jnp.einsum("chqk,ckhd->cqhd", probs, values, preferred_element_type=jnp.float32)
    return mixed.astype(jnp.bfloat16).reshape(queries.shape)


def solution(mesh):
    placed = (
        P(("groups", "wide"), "heads"),
        P(("groups", "wide"), None),
        P(None, "heads"),
        P(None, "heads"),
        P(("groups", "wide"), None, None),
        P(("groups", "wide"), None),
    )
    return jax.shard_map(
        on_device,
        mesh=mesh,
        in_specs=placed,
        out_specs=P(("groups", "wide"), "heads"),
        check_vma=False,
    )
```

```python
import functools

import jax
import jax.numpy as jnp
from jax import lax
from jax.experimental import pallas as pl
from jax.experimental.pallas import tpu as pltpu
from jax.sharding import PartitionSpec as P

HD = 128
SPAN = 64
SIDE = 2
LIMIT = 40 * 1024 * 1024
VMEM = pl.BlockSpec(memory_space=pltpu.VMEM)
HBM = pl.BlockSpec(memory_space=pl.ANY)


def params():
    return pltpu.CompilerParams(vmem_limit_bytes=LIMIT)


def half_kernel(width, enc_ref, out_ref, sem):
    column = pl.multiple_of(lax.axis_index("heads") * width, 128)
    copy = pltpu.make_async_copy(enc_ref.at[:, pl.ds(column, width)], out_ref, sem)
    copy.start()
    copy.wait()


def half_columns(encodings):
    rows, columns = encodings.shape
    width = columns // lax.axis_size("heads")
    return pl.pallas_call(
        functools.partial(half_kernel, width),
        out_shape=jax.ShapeDtypeStruct((rows, width), encodings.dtype),
        in_specs=[HBM],
        out_specs=HBM,
        scratch_shapes=[pltpu.SemaphoreType.DMA],
        compiler_params=params(),
    )(encodings)


def pick_kernel(chunks, index_ref, *refs):
    sources, out_ref, held, sems = refs[:chunks], refs[chunks], refs[chunks + 1], refs[chunks + 2]
    rows = sources[0].shape[0]
    copies = [
        pltpu.make_async_copy(ref, held.at[pl.ds(n * rows, rows), :], sems.at[n])
        for n, ref in enumerate(sources)
    ]
    for copy in copies:
        copy.start()
    places = lax.broadcasted_iota(jnp.int32, (index_ref.shape[0], chunks * rows), 1)
    chosen = jnp.where(places == index_ref[...], 1.0, 0.0).astype(jnp.bfloat16)
    for copy in copies:
        copy.wait()
    out_ref[...] = jnp.dot(chosen, held[...], preferred_element_type=jnp.float32).astype(out_ref.dtype)


def pick(index, sources):
    chunks = len(sources)
    rows, width = sources[0].shape
    return pl.pallas_call(
        functools.partial(pick_kernel, chunks),
        out_shape=jax.ShapeDtypeStruct((index.shape[0], width), sources[0].dtype),
        in_specs=[VMEM] + [HBM] * chunks,
        out_specs=VMEM,
        scratch_shapes=[
            pltpu.VMEM((chunks * rows, width), sources[0].dtype),
            pltpu.SemaphoreType.DMA((chunks,)),
        ],
        compiler_params=params(),
    )(index, *sources)


def by_span(picked, spans, channels):
    per = picked.shape[0] // spans
    parts = []
    for c in range(spans):
        for t in range(picked.shape[1] // channels):
            parts.append(picked[c * per : (c + 1) * per, t * channels : (t + 1) * channels])
    return jnp.concatenate(parts, axis=0)


def project_kernel(spans, picked_ref, wk_ref, wv_ref, keys_ref, values_ref):
    source = by_span(picked_ref[...], spans, wk_ref.shape[0])
    keys_ref[...] = jnp.dot(source, wk_ref[...], preferred_element_type=jnp.float32).astype(keys_ref.dtype)
    values_ref[...] = jnp.dot(source, wv_ref[...], preferred_element_type=jnp.float32).astype(values_ref.dtype)


def project(picked, w_key, w_value, spans):
    rows = picked.size // w_key.shape[0]
    shape = jax.ShapeDtypeStruct((rows, w_key.shape[1]), picked.dtype)
    return pl.pallas_call(
        functools.partial(project_kernel, spans),
        out_shape=(shape, shape),
        in_specs=[VMEM] * 3,
        out_specs=(VMEM, VMEM),
        compiler_params=params(),
    )(picked, w_key, w_value)


def attend_kernel(spans, picked_ref, wk_ref, wv_ref, keys_ref, values_ref, query_ref, out_ref):
    source = by_span(picked_ref[...], spans, wk_ref.shape[0])
    keys_more = jnp.dot(source, wk_ref[...], preferred_element_type=jnp.float32).astype(jnp.bfloat16)
    values_more = jnp.dot(source, wv_ref[...], preferred_element_type=jnp.float32).astype(jnp.bfloat16)
    per = keys_more.shape[0] // spans
    for c in range(spans):
        keys = jnp.concatenate([keys_ref[c * per : (c + 1) * per, :], keys_more[c * per : (c + 1) * per]], axis=0)
        values = jnp.concatenate([values_ref[c * per : (c + 1) * per, :], values_more[c * per : (c + 1) * per]], axis=0)
        for h in range(wk_ref.shape[1] // HD):
            lanes = slice(h * HD, (h + 1) * HD)
            query = query_ref[c * SPAN : (c + 1) * SPAN, lanes]
            scores = lax.dot_general(
                query, keys[:, lanes], (((1,), (1,)), ((), ())), preferred_element_type=jnp.float32
            ) * HD ** (-0.5)
            raised = jnp.exp(scores - jnp.max(scores, axis=-1, keepdims=True))
            probs = (raised * (1.0 / jnp.sum(raised, axis=-1, keepdims=True))).astype(jnp.bfloat16)
            mixed = jnp.dot(probs, values[:, lanes], preferred_element_type=jnp.float32)
            out_ref[c * SPAN : (c + 1) * SPAN, lanes] = mixed.astype(out_ref.dtype)


def attend(picked, w_key, w_value, keys, values, queries, spans):
    return pl.pallas_call(
        functools.partial(attend_kernel, spans),
        out_shape=jax.ShapeDtypeStruct(queries.shape, queries.dtype),
        in_specs=[VMEM] * 6,
        out_specs=VMEM,
        compiler_params=params(),
    )(picked, w_key, w_value, keys, values, queries)


def spread(mine):
    wide_count = lax.axis_size("wide")
    turns = wide_count // SIDE
    ring = [(n, (n + SIDE) % wide_count) for n in range(wide_count)]
    across = [(n, n + 1 if n % SIDE == 0 else n - 1) for n in range(wide_count)]
    own, crossed = [mine], []
    for k in range(turns):
        if k + 1 < turns:
            own.append(lax.ppermute(own[k], "wide", ring))
        crossed.append(lax.ppermute(own[k], "wide", across))
    return own + crossed


def gathered_plan(queries, encodings, w_key, w_value, owners, stored):
    wide_count = lax.axis_size("wide")
    turns = wide_count // SIDE
    me = lax.axis_index("wide")
    spans = queries.shape[0] // SPAN
    mine = half_columns(encodings)
    sources = spread(mine)
    back = (me // SIDE - owners // SIDE) % turns
    place = jnp.where(owners % SIDE == me % SIDE, back, turns + back)
    index = (place * encodings.shape[0] + stored)[:, None]
    picked = pick(index, sources)
    other = lax.ppermute(picked, "heads", [(0, 1), (1, 0)])
    keys, values = project(picked, w_key, w_value, spans)
    return attend(other, w_key, w_value, keys, values, queries, spans)


def exchange(encodings, owners, stored, capacity):
    wide_count = lax.axis_size("wide")
    requests = owners.shape[0]
    order = jnp.arange(requests, dtype=jnp.int32)
    earlier = (owners[:, None] == owners[None, :]) & (order[None, :] < order[:, None])
    rank = jnp.sum(earlier.astype(jnp.int32), axis=1)
    slot = owners * capacity + rank
    table = jnp.full((wide_count * capacity,), -1, jnp.int32).at[slot].set(stored)
    table = table.reshape(wide_count, capacity)
    asked = lax.all_to_all(table, "wide", split_axis=0, concat_axis=0, tiled=True)
    wanted = jnp.maximum(asked, 0)
    picked = encodings[wanted]
    returned = lax.all_to_all(picked, "wide", split_axis=0, concat_axis=0, tiled=True)
    return returned.reshape(wide_count * capacity, encodings.shape[1])[slot]


def exchanged_plan(queries, encodings, w_key, w_value, owners, stored, capacity):
    fetched = exchange(encodings, owners, stored, capacity)
    channels = w_key.shape[0]
    source = fetched.reshape(-1, channels)
    keys = jnp.dot(source, w_key, preferred_element_type=jnp.float32).astype(jnp.bfloat16)
    values = jnp.dot(source, w_value, preferred_element_type=jnp.float32).astype(jnp.bfloat16)
    span_count = queries.shape[0] // SPAN
    heads_local = w_key.shape[1] // HD
    keys = keys.reshape(span_count, -1, heads_local, HD)
    values = values.reshape(span_count, -1, heads_local, HD)
    query_part = queries.reshape(span_count, SPAN, heads_local, HD)
    scores = jnp.einsum(
        "cqhd,ckhd->chqk", query_part, keys, preferred_element_type=jnp.float32
    ) * HD ** (-0.5)
    probs = jax.nn.softmax(scores, axis=-1).astype(jnp.bfloat16)
    mixed = jnp.einsum("chqk,ckhd->cqhd", probs, values, preferred_element_type=jnp.float32)
    return mixed.astype(jnp.bfloat16).reshape(queries.shape)


def on_device(queries, encodings, w_key, w_value, block_owner, block_row):
    wide_count = lax.axis_size("wide")
    owners = block_owner.reshape(-1)
    stored = block_row.reshape(-1)
    requests = owners.shape[0]
    capacity = 2 * ((requests + wide_count - 1) // wide_count)
    if encodings.shape[0] <= 2 * capacity:
        return gathered_plan(queries, encodings, w_key, w_value, owners, stored)
    return exchanged_plan(queries, encodings, w_key, w_value, owners, stored, capacity)


def solution(mesh):
    placed = (
        P(("groups", "wide"), "heads"),
        P(("groups", "wide"), None),
        P(None, "heads"),
        P(None, "heads"),
        P(("groups", "wide"), None, None),
        P(("groups", "wide"), None),
    )
    return jax.shard_map(
        on_device,
        mesh=mesh,
        in_specs=placed,
        out_specs=P(("groups", "wide"), "heads"),
        check_vma=False,
    )
```

```python
import functools

import jax
import jax.numpy as jnp
from jax import lax
from jax.experimental import pallas as pl
from jax.experimental.pallas import tpu as pltpu
from jax.sharding import PartitionSpec as P

HD = 128
SPAN = 64
SIDE = 2
LIMIT = 24 * 1024 * 1024
MOST = 54 * 1024 * 1024
EXPONENT = HD ** (-0.5) * 1.4426950408889634
VMEM = pl.BlockSpec(memory_space=pltpu.VMEM)
HBM = pl.BlockSpec(memory_space=pltpu.HBM)


def params(limit=LIMIT):
    return pltpu.CompilerParams(vmem_limit_bytes=limit)


def half_kernel(width, enc_ref, out_ref, sem):
    column = pl.multiple_of(lax.axis_index("heads") * width, 128)
    copy = pltpu.make_async_copy(enc_ref.at[:, pl.ds(column, width)], out_ref, sem)
    copy.start()
    copy.wait()


def half_columns(encodings):
    rows, columns = encodings.shape
    width = columns // lax.axis_size("heads")
    return pl.pallas_call(
        functools.partial(half_kernel, width),
        out_shape=jax.ShapeDtypeStruct((rows, width), encodings.dtype),
        in_specs=[HBM],
        out_specs=HBM,
        scratch_shapes=[pltpu.SemaphoreType.DMA],
        compiler_params=params(MOST),
    )(encodings)


def chosen_rows(index, sources, first):
    held = jnp.concatenate([ref[...] for ref in sources], axis=0)
    places = lax.broadcasted_iota(jnp.int32, (index.shape[0], held.shape[0]), 1) + first
    chosen = jnp.where(places == index, 1.0, 0.0).astype(held.dtype)
    return jnp.dot(chosen, held, preferred_element_type=jnp.float32)


def early_kernel(chunks, index_ref, *refs):
    refs[chunks][...] = chosen_rows(index_ref[...], refs[:chunks], 0).astype(refs[chunks].dtype)


def early(index, sources):
    chunks = len(sources)
    rows, width = sources[0].shape
    return pl.pallas_call(
        functools.partial(early_kernel, chunks),
        out_shape=jax.ShapeDtypeStruct((index.shape[0], width), sources[0].dtype),
        in_specs=[VMEM] * (1 + chunks),
        out_specs=VMEM,
        compiler_params=params(),
        cost_estimate=pl.CostEstimate(
            flops=2 * index.shape[0] * width * rows * chunks,
            bytes_accessed=2 * index.shape[0] * width,
            transcendentals=0,
        ),
    )(index, *sources)


def pick_kernel(chunks, first, index_ref, begun_ref, *refs):
    picked = chosen_rows(index_ref[...], refs[:chunks], first)
    refs[chunks][...] = (picked + begun_ref[...].astype(jnp.float32)).astype(begun_ref.dtype)


def pick(index, begun, sources, first):
    return pl.pallas_call(
        functools.partial(pick_kernel, len(sources), first),
        out_shape=jax.ShapeDtypeStruct(begun.shape, begun.dtype),
        in_specs=[VMEM] * (2 + len(sources)),
        out_specs=VMEM,
        compiler_params=params(),
    )(index, begun, *sources)


def by_span(picked, spans, channels):
    per = picked.shape[0] // spans
    parts = []
    for c in range(spans):
        for t in range(picked.shape[1] // channels):
            parts.append(picked[c * per : (c + 1) * per, t * channels : (t + 1) * channels])
    return jnp.concatenate(parts, axis=0)


def project_kernel(spans, picked_ref, wk_ref, wv_ref, keys_ref, values_ref):
    source = by_span(picked_ref[...], spans, wk_ref.shape[0])
    keys_ref[...] = jnp.dot(source, wk_ref[...], preferred_element_type=jnp.float32).astype(keys_ref.dtype)
    values_ref[...] = jnp.dot(source, wv_ref[...], preferred_element_type=jnp.float32).astype(values_ref.dtype)


def project(picked, w_key, w_value, spans):
    rows = picked.size // w_key.shape[0]
    shape = jax.ShapeDtypeStruct((rows, w_key.shape[1]), picked.dtype)
    return pl.pallas_call(
        functools.partial(project_kernel, spans),
        out_shape=(shape, shape),
        in_specs=[VMEM] * 3,
        out_specs=(VMEM, VMEM),
        compiler_params=params(),
    )(picked, w_key, w_value)


def attend_kernel(spans, picked_ref, wk_ref, wv_ref, keys_ref, values_ref, query_ref, out_ref, scores_ref, probs_ref):
    source = by_span(picked_ref[...], spans, wk_ref.shape[0])
    keys_more = jnp.dot(source, wk_ref[...], preferred_element_type=jnp.float32).astype(jnp.bfloat16)
    values_more = jnp.dot(source, wv_ref[...], preferred_element_type=jnp.float32).astype(jnp.bfloat16)
    per = keys_more.shape[0] // spans
    heads = wk_ref.shape[1] // HD
    places = [(c, slice(h * HD, (h + 1) * HD), c * heads + h) for c in range(spans) for h in range(heads)]

    def joined(ref, more, c, lanes):
        return jnp.concatenate([ref[c * per : (c + 1) * per, lanes], more[c * per : (c + 1) * per, lanes]], axis=0)

    for c, lanes, n in places:
        scores_ref[n] = lax.dot_general(
            query_ref[c * SPAN : (c + 1) * SPAN, lanes],
            joined(keys_ref, keys_more, c, lanes),
            (((1,), (1,)), ((), ())),
            preferred_element_type=jnp.float32,
        )
    for c, lanes, n in places:
        scores = scores_ref[n]
        raised = jnp.exp2((scores - jnp.max(scores, axis=-1, keepdims=True)) * EXPONENT)
        probs_ref[n] = (raised * (1.0 / jnp.sum(raised, axis=-1, keepdims=True))).astype(jnp.bfloat16)
    for c, lanes, n in places:
        mixed = jnp.dot(probs_ref[n], joined(values_ref, values_more, c, lanes), preferred_element_type=jnp.float32)
        out_ref[c * SPAN : (c + 1) * SPAN, lanes] = mixed.astype(out_ref.dtype)


def attend(picked, w_key, w_value, keys, values, queries, spans):
    each = spans * (queries.shape[1] // HD), SPAN, 2 * keys.shape[0] // spans
    return pl.pallas_call(
        functools.partial(attend_kernel, spans),
        out_shape=jax.ShapeDtypeStruct(queries.shape, queries.dtype),
        in_specs=[VMEM] * 6,
        out_specs=VMEM,
        scratch_shapes=[pltpu.VMEM(each, jnp.float32), pltpu.VMEM(each, jnp.bfloat16)],
        compiler_params=params(),
    )(picked, w_key, w_value, keys, values, queries)


def gathered_plan(queries, encodings, w_key, w_value, owners, stored):
    wide_count = lax.axis_size("wide")
    turns = wide_count // SIDE
    me = lax.axis_index("wide")
    rows = encodings.shape[0]
    spans = queries.shape[0] // SPAN
    ring = [(n, (n + SIDE) % wide_count) for n in range(wide_count)]
    across = [(n, n + 1 if n % SIDE == 0 else n - 1) for n in range(wide_count)]
    held, crossed = [half_columns(encodings)], []
    for k in range(turns - 1):
        onward = lax.ppermute(held[k], "wide", ring)
        aside = lax.ppermute(held[k], "wide", across)
        onward, aside = lax.optimization_barrier((onward, aside))
        held.append(onward)
        crossed.append(aside)
    middle = rows // 2
    last = [
        lax.ppermute(held[-1][:middle], "wide", across),
        lax.ppermute(crossed[-1][middle:], "wide", ring),
    ]
    back = (me // SIDE - owners // SIDE) % turns
    straight = jnp.where(back == 0, 0, 2 * back - 1)
    place = jnp.where(owners % SIDE == me % SIDE, straight, jnp.where(back == turns - 1, wide_count - 1, 2 * back + 2))
    index = (place * rows + stored)[:, None]
    order = [held[0]] + [chunk for pair in zip(held[1:], crossed) for chunk in pair]
    there = len(order) - 2
    begun = early(index, order[:there])
    picked = pick(index, begun, order[there:] + last, there * rows)
    other = lax.ppermute(picked, "heads", [(0, 1), (1, 0)])
    keys, values = project(picked, w_key, w_value, spans)
    return attend(other, w_key, w_value, keys, values, queries, spans)


def exchange(encodings, owners, stored, capacity):
    wide_count = lax.axis_size("wide")
    requests = owners.shape[0]
    order = jnp.arange(requests, dtype=jnp.int32)
    earlier = (owners[:, None] == owners[None, :]) & (order[None, :] < order[:, None])
    rank = jnp.sum(earlier.astype(jnp.int32), axis=1)
    slot = owners * capacity + rank
    table = jnp.full((wide_count * capacity,), -1, jnp.int32).at[slot].set(stored)
    table = table.reshape(wide_count, capacity)
    asked = lax.all_to_all(table, "wide", split_axis=0, concat_axis=0, tiled=True)
    wanted = jnp.maximum(asked, 0)
    picked = encodings[wanted]
    returned = lax.all_to_all(picked, "wide", split_axis=0, concat_axis=0, tiled=True)
    return returned.reshape(wide_count * capacity, encodings.shape[1])[slot]


def exchanged_plan(queries, encodings, w_key, w_value, owners, stored, capacity):
    fetched = exchange(encodings, owners, stored, capacity)
    channels = w_key.shape[0]
    source = fetched.reshape(-1, channels)
    keys = jnp.dot(source, w_key, preferred_element_type=jnp.float32).astype(jnp.bfloat16)
    values = jnp.dot(source, w_value, preferred_element_type=jnp.float32).astype(jnp.bfloat16)
    span_count = queries.shape[0] // SPAN
    heads_local = w_key.shape[1] // HD
    keys = keys.reshape(span_count, -1, heads_local, HD)
    values = values.reshape(span_count, -1, heads_local, HD)
    query_part = queries.reshape(span_count, SPAN, heads_local, HD)
    scores = jnp.einsum(
        "cqhd,ckhd->chqk", query_part, keys, preferred_element_type=jnp.float32
    ) * HD ** (-0.5)
    probs = jax.nn.softmax(scores, axis=-1).astype(jnp.bfloat16)
    mixed = jnp.einsum("chqk,ckhd->cqhd", probs, values, preferred_element_type=jnp.float32)
    return mixed.astype(jnp.bfloat16).reshape(queries.shape)


def on_device(queries, encodings, w_key, w_value, block_owner, block_row):
    wide_count = lax.axis_size("wide")
    owners = block_owner.reshape(-1)
    stored = block_row.reshape(-1)
    requests = owners.shape[0]
    capacity = 2 * ((requests + wide_count - 1) // wide_count)
    if encodings.shape[0] <= 2 * capacity:
        return gathered_plan(queries, encodings, w_key, w_value, owners, stored)
    return exchanged_plan(queries, encodings, w_key, w_value, owners, stored, capacity)


def solution(mesh):
    placed = (
        P(("groups", "wide"), "heads"),
        P(("groups", "wide"), None),
        P(None, "heads"),
        P(None, "heads"),
        P(("groups", "wide"), None, None),
        P(("groups", "wide"), None),
    )
    return jax.shard_map(
        on_device,
        mesh=mesh,
        in_specs=placed,
        out_specs=P(("groups", "wide"), "heads"),
        check_vma=False,
    )
```

```python
import functools

import jax
import jax.numpy as jnp
from jax import lax
from jax.experimental import pallas as pl
from jax.experimental.pallas import tpu as pltpu
from jax.sharding import PartitionSpec as P

HD = 128
SPAN = 64
SIDE = 2
LIMIT = 24 * 1024 * 1024
STREAMS = 2
EXPONENT = HD ** (-0.5) * 1.4426950408889634
VMEM = pl.BlockSpec(memory_space=pltpu.VMEM)


def params():
    return pltpu.CompilerParams(vmem_limit_bytes=LIMIT)


def half_kernel(enc_ref, *refs):
    outs, sems = refs[:-1], refs[-1]
    width = outs[0].shape[1]
    start = lax.axis_index("heads") * len(outs) * width
    copies = [
        pltpu.make_async_copy(enc_ref.at[:, pl.ds(pl.multiple_of(start + n * width, 128), width)], out, sems.at[n])
        for n, out in enumerate(outs)
    ]
    for copy in copies:
        copy.start()
    for copy in copies:
        copy.wait()


def half_columns(encodings):
    rows, columns = encodings.shape
    width = columns // lax.axis_size("heads") // STREAMS
    return pl.pallas_call(
        half_kernel,
        out_shape=[jax.ShapeDtypeStruct((rows, width), encodings.dtype)] * STREAMS,
        in_specs=[VMEM],
        out_specs=[VMEM] * STREAMS,
        scratch_shapes=[pltpu.SemaphoreType.DMA((STREAMS,))],
        compiler_params=params(),
    )(encodings)


def chosen_rows(index, sources, first):
    chunks = len(sources) // STREAMS
    rows = sources[0].shape[0]
    places = lax.broadcasted_iota(jnp.int32, (index.shape[0], chunks * rows), 1) + first
    chosen = jnp.where(places == index, 1.0, 0.0).astype(sources[0].dtype)
    parts = []
    for n in range(STREAMS):
        held = jnp.concatenate([ref[...] for ref in sources[n * chunks : (n + 1) * chunks]], axis=0)
        parts.append(jnp.dot(chosen, held, preferred_element_type=jnp.float32))
    return jnp.concatenate(parts, axis=1)


def early_kernel(index_ref, *refs):
    refs[-1][...] = chosen_rows(index_ref[...], refs[:-1], 0).astype(refs[-1].dtype)


def early(index, streams):
    sources = [chunk for stream in streams for chunk in stream]
    rows, width = sources[0].shape
    return pl.pallas_call(
        early_kernel,
        out_shape=jax.ShapeDtypeStruct((index.shape[0], STREAMS * width), sources[0].dtype),
        in_specs=[VMEM] * (1 + len(sources)),
        out_specs=VMEM,
        compiler_params=params(),
        cost_estimate=pl.CostEstimate(
            flops=2 * index.shape[0] * width * rows * len(sources),
            bytes_accessed=2 * index.shape[0] * width * STREAMS,
            transcendentals=0,
        ),
    )(index, *sources)


def pick_kernel(first, index_ref, begun_ref, *refs):
    picked = chosen_rows(index_ref[...], refs[:-1], first)
    refs[-1][...] = (picked + begun_ref[...].astype(jnp.float32)).astype(begun_ref.dtype)


def pick(index, begun, streams, first):
    sources = [chunk for stream in streams for chunk in stream]
    return pl.pallas_call(
        functools.partial(pick_kernel, first),
        out_shape=jax.ShapeDtypeStruct(begun.shape, begun.dtype),
        in_specs=[VMEM] * (2 + len(sources)),
        out_specs=VMEM,
        compiler_params=params(),
    )(index, begun, *sources)


def by_span(picked, spans, channels):
    per = picked.shape[0] // spans
    parts = []
    for c in range(spans):
        for t in range(picked.shape[1] // channels):
            parts.append(picked[c * per : (c + 1) * per, t * channels : (t + 1) * channels])
    return jnp.concatenate(parts, axis=0)


def project_kernel(spans, picked_ref, wk_ref, wv_ref, keys_ref, values_ref):
    source = by_span(picked_ref[...], spans, wk_ref.shape[0])
    keys_ref[...] = jnp.dot(source, wk_ref[...], preferred_element_type=jnp.float32).astype(keys_ref.dtype)
    values_ref[...] = jnp.dot(source, wv_ref[...], preferred_element_type=jnp.float32).astype(values_ref.dtype)


def project(picked, w_key, w_value, spans):
    rows = picked.size // w_key.shape[0]
    shape = jax.ShapeDtypeStruct((rows, w_key.shape[1]), picked.dtype)
    return pl.pallas_call(
        functools.partial(project_kernel, spans),
        out_shape=(shape, shape),
        in_specs=[VMEM] * 3,
        out_specs=(VMEM, VMEM),
        compiler_params=params(),
    )(picked, w_key, w_value)


def attend_kernel(spans, picked_ref, wk_ref, wv_ref, keys_ref, values_ref, query_ref, out_ref, scores_ref, probs_ref):
    source = by_span(picked_ref[...], spans, wk_ref.shape[0])
    keys_more = jnp.dot(source, wk_ref[...], preferred_element_type=jnp.float32).astype(jnp.bfloat16)
    values_more = jnp.dot(source, wv_ref[...], preferred_element_type=jnp.float32).astype(jnp.bfloat16)
    per = keys_more.shape[0] // spans
    heads = wk_ref.shape[1] // HD
    places = [(c, slice(h * HD, (h + 1) * HD), c * heads + h) for c in range(spans) for h in range(heads)]

    def joined(ref, more, c, lanes):
        return jnp.concatenate([ref[c * per : (c + 1) * per, lanes], more[c * per : (c + 1) * per, lanes]], axis=0)

    for c, lanes, n in places:
        scores_ref[n] = lax.dot_general(
            query_ref[c * SPAN : (c + 1) * SPAN, lanes],
            joined(keys_ref, keys_more, c, lanes),
            (((1,), (1,)), ((), ())),
            preferred_element_type=jnp.float32,
        )
    for c, lanes, n in places:
        scores = scores_ref[n]
        raised = jnp.exp2((scores - jnp.max(scores, axis=-1, keepdims=True)) * EXPONENT)
        probs_ref[n] = (raised * (1.0 / jnp.sum(raised, axis=-1, keepdims=True))).astype(jnp.bfloat16)
    for c, lanes, n in places:
        mixed = jnp.dot(probs_ref[n], joined(values_ref, values_more, c, lanes), preferred_element_type=jnp.float32)
        out_ref[c * SPAN : (c + 1) * SPAN, lanes] = mixed.astype(out_ref.dtype)


def attend(picked, w_key, w_value, keys, values, queries, spans):
    each = spans * (queries.shape[1] // HD), SPAN, 2 * keys.shape[0] // spans
    return pl.pallas_call(
        functools.partial(attend_kernel, spans),
        out_shape=jax.ShapeDtypeStruct(queries.shape, queries.dtype),
        in_specs=[VMEM] * 6,
        out_specs=VMEM,
        scratch_shapes=[pltpu.VMEM(each, jnp.float32), pltpu.VMEM(each, jnp.bfloat16)],
        compiler_params=params(),
    )(picked, w_key, w_value, keys, values, queries)


def gathered_plan(queries, encodings, w_key, w_value, owners, stored):
    wide_count = lax.axis_size("wide")
    turns = wide_count // SIDE
    me = lax.axis_index("wide")
    rows = encodings.shape[0]
    spans = queries.shape[0] // SPAN
    ring = [(n, (n + SIDE) % wide_count) for n in range(wide_count)]
    across = [(n, n + 1 if n % SIDE == 0 else n - 1) for n in range(wide_count)]
    held = [[piece] for piece in half_columns(encodings)]
    crossed = [[] for _ in held]
    for k in range(turns - 1):
        for straight, side in zip(held, crossed):
            onward = lax.ppermute(straight[k], "wide", ring)
            aside = lax.ppermute(straight[k], "wide", across)
            onward, aside = lax.optimization_barrier((onward, aside))
            straight.append(onward)
            side.append(aside)
    last = [
        lax.ppermute(held[n][-1], "wide", across) if n % 2 == 0 else lax.ppermute(crossed[n][-1], "wide", ring)
        for n in range(STREAMS)
    ]
    back = (me // SIDE - owners // SIDE) % turns
    straight = jnp.where(back == 0, 0, 2 * back - 1)
    place = jnp.where(owners % SIDE == me % SIDE, straight, jnp.where(back == turns - 1, wide_count - 1, 2 * back + 2))
    index = (place * rows + stored)[:, None]
    order = [
        [straight[0]] + [chunk for pair in zip(straight[1:], side) for chunk in pair]
        for straight, side in zip(held, crossed)
    ]
    there = len(order[0]) - 2
    begun = early(index, [chunks[:there] for chunks in order])
    picked = pick(index, begun, [chunks[there:] + [final] for chunks, final in zip(order, last)], there * rows)
    other = lax.ppermute(picked, "heads", [(0, 1), (1, 0)])
    keys, values = project(picked, w_key, w_value, spans)
    return attend(other, w_key, w_value, keys, values, queries, spans)


def exchange(encodings, owners, stored, capacity):
    wide_count = lax.axis_size("wide")
    requests = owners.shape[0]
    order = jnp.arange(requests, dtype=jnp.int32)
    earlier = (owners[:, None] == owners[None, :]) & (order[None, :] < order[:, None])
    rank = jnp.sum(earlier.astype(jnp.int32), axis=1)
    slot = owners * capacity + rank
    table = jnp.full((wide_count * capacity,), -1, jnp.int32).at[slot].set(stored)
    table = table.reshape(wide_count, capacity)
    asked = lax.all_to_all(table, "wide", split_axis=0, concat_axis=0, tiled=True)
    wanted = jnp.maximum(asked, 0)
    picked = encodings[wanted]
    returned = lax.all_to_all(picked, "wide", split_axis=0, concat_axis=0, tiled=True)
    return returned.reshape(wide_count * capacity, encodings.shape[1])[slot]


def exchanged_plan(queries, encodings, w_key, w_value, owners, stored, capacity):
    fetched = exchange(encodings, owners, stored, capacity)
    channels = w_key.shape[0]
    source = fetched.reshape(-1, channels)
    keys = jnp.dot(source, w_key, preferred_element_type=jnp.float32).astype(jnp.bfloat16)
    values = jnp.dot(source, w_value, preferred_element_type=jnp.float32).astype(jnp.bfloat16)
    span_count = queries.shape[0] // SPAN
    heads_local = w_key.shape[1] // HD
    keys = keys.reshape(span_count, -1, heads_local, HD)
    values = values.reshape(span_count, -1, heads_local, HD)
    query_part = queries.reshape(span_count, SPAN, heads_local, HD)
    scores = jnp.einsum(
        "cqhd,ckhd->chqk", query_part, keys, preferred_element_type=jnp.float32
    ) * HD ** (-0.5)
    probs = jax.nn.softmax(scores, axis=-1).astype(jnp.bfloat16)
    mixed = jnp.einsum("chqk,ckhd->cqhd", probs, values, preferred_element_type=jnp.float32)
    return mixed.astype(jnp.bfloat16).reshape(queries.shape)


def on_device(queries, encodings, w_key, w_value, block_owner, block_row):
    wide_count = lax.axis_size("wide")
    owners = block_owner.reshape(-1)
    stored = block_row.reshape(-1)
    requests = owners.shape[0]
    capacity = 2 * ((requests + wide_count - 1) // wide_count)
    if encodings.shape[0] <= 2 * capacity:
        return gathered_plan(queries, encodings, w_key, w_value, owners, stored)
    return exchanged_plan(queries, encodings, w_key, w_value, owners, stored, capacity)


def solution(mesh):
    placed = (
        P(("groups", "wide"), "heads"),
        P(("groups", "wide"), None),
        P(None, "heads"),
        P(None, "heads"),
        P(("groups", "wide"), None, None),
        P(("groups", "wide"), None),
    )
    return jax.shard_map(
        on_device,
        mesh=mesh,
        in_specs=placed,
        out_specs=P(("groups", "wide"), "heads"),
        check_vma=False,
    )
```

```python
import functools

import jax
import jax.numpy as jnp
from jax import lax
from jax.experimental import pallas as pl
from jax.experimental.pallas import tpu as pltpu
from jax.sharding import PartitionSpec as P

HD = 128
SPAN = 64
SIDE = 2
LIMIT = 24 * 1024 * 1024
STREAMS = 2
EXPONENT = HD ** (-0.5) * 1.4426950408889634
VMEM = pl.BlockSpec(memory_space=pltpu.VMEM)


def params():
    return pltpu.CompilerParams(vmem_limit_bytes=LIMIT)


def half_kernel(enc_ref, *refs):
    outs, sems = refs[:-1], refs[-1]
    width = outs[0].shape[1]
    start = lax.axis_index("heads") * len(outs) * width
    copies = [
        pltpu.make_async_copy(enc_ref.at[:, pl.ds(pl.multiple_of(start + n * width, 128), width)], out, sems.at[n])
        for n, out in enumerate(outs)
    ]
    for copy in copies:
        copy.start()
    for copy in copies:
        copy.wait()


def half_columns(encodings):
    rows, columns = encodings.shape
    width = columns // lax.axis_size("heads") // STREAMS
    return pl.pallas_call(
        half_kernel,
        out_shape=[jax.ShapeDtypeStruct((rows, width), encodings.dtype)] * STREAMS,
        in_specs=[VMEM],
        out_specs=[VMEM] * STREAMS,
        scratch_shapes=[pltpu.SemaphoreType.DMA((STREAMS,))],
        compiler_params=params(),
    )(encodings)


def chosen_rows(index, sources, first):
    chunks = len(sources) // STREAMS
    rows = sources[0].shape[0]
    places = lax.broadcasted_iota(jnp.int32, (index.shape[0], chunks * rows), 1) + first
    chosen = jnp.where(places == index, 1.0, 0.0).astype(sources[0].dtype)
    parts = []
    for n in range(STREAMS):
        held = jnp.concatenate([ref[...] for ref in sources[n * chunks : (n + 1) * chunks]], axis=0)
        parts.append(jnp.dot(chosen, held, preferred_element_type=jnp.float32))
    return jnp.concatenate(parts, axis=1)


def ring_order(turns):
    return [0] + list(range(1, turns, 2)) + list(range(turns - 2 + turns % 2, 0, -2))


def ring_place(line, turns):
    return jnp.where(line % 2 == 1, (line + 1) // 2, jnp.where(line == 0, 0, turns - line // 2))


def wanted_rows(wide_count, rows, owner_ref, stored_ref):
    turns = wide_count // SIDE
    me = lax.axis_index("wide")
    columns = []
    for c in range(stored_ref.shape[0]):
        owner, stored = owner_ref[c], stored_ref[c : c + 1, :]
        back = ring_place(me // SIDE, turns) - ring_place(owner // SIDE, turns)
        back = jnp.where(back < 0, back + turns, back)
        straight = jnp.where(back == 0, 0, 2 * back - 1)
        crossed = jnp.where(back == turns - 1, wide_count - 1, 2 * back + 2)
        place = jnp.where(owner % SIDE == me % SIDE, straight, crossed) * rows + stored
        square = (place.shape[1], place.shape[1])
        own = lax.broadcasted_iota(jnp.int32, square, 0) == lax.broadcasted_iota(jnp.int32, square, 1)
        spread = jnp.where(own, jnp.broadcast_to(place.astype(jnp.float32), square), 0.0)
        columns.append(jnp.sum(spread, axis=1, keepdims=True))
    return jnp.concatenate(columns, axis=0).astype(jnp.int32)


def early_kernel(wide_count, owner_ref, stored_ref, *refs):
    sources, index_ref, out_ref = refs[:-2], refs[-2], refs[-1]
    index_ref[...] = wanted_rows(wide_count, sources[0].shape[0], owner_ref, stored_ref)
    out_ref[...] = chosen_rows(index_ref[...], sources, 0).astype(out_ref.dtype)


def early(owners, stored, streams):
    sources = [chunk for stream in streams for chunk in stream]
    rows, width = sources[0].shape
    requests = stored.size
    return pl.pallas_call(
        functools.partial(early_kernel, lax.axis_size("wide")),
        out_shape=(
            jax.ShapeDtypeStruct((requests, 1), jnp.int32),
            jax.ShapeDtypeStruct((requests, STREAMS * width), sources[0].dtype),
        ),
        in_specs=[VMEM] * (2 + len(sources)),
        out_specs=(VMEM, VMEM),
        compiler_params=params(),
        cost_estimate=pl.CostEstimate(
            flops=2 * requests * width * rows * len(sources),
            bytes_accessed=2 * requests * width * STREAMS,
            transcendentals=0,
        ),
    )(owners, stored, *sources)


def pick_kernel(first, index_ref, begun_ref, *refs):
    picked = chosen_rows(index_ref[...], refs[:-1], first)
    refs[-1][...] = (picked + begun_ref[...].astype(jnp.float32)).astype(begun_ref.dtype)


def pick(index, begun, streams, first):
    sources = [chunk for stream in streams for chunk in stream]
    return pl.pallas_call(
        functools.partial(pick_kernel, first),
        out_shape=jax.ShapeDtypeStruct(begun.shape, begun.dtype),
        in_specs=[VMEM] * (2 + len(sources)),
        out_specs=VMEM,
        compiler_params=params(),
    )(index, begun, *sources)


def by_span(picked, spans, channels):
    per = picked.shape[0] // spans
    parts = []
    for c in range(spans):
        for t in range(picked.shape[1] // channels):
            parts.append(picked[c * per : (c + 1) * per, t * channels : (t + 1) * channels])
    return jnp.concatenate(parts, axis=0)


def head_places(spans, columns):
    heads = columns // HD
    return [(c, slice(h * HD, (h + 1) * HD), c * heads + h) for c in range(spans) for h in range(heads)]


def score(spans, source, wk_ref, query_ref, scores_ref):
    keys = jnp.dot(source, wk_ref[...], preferred_element_type=jnp.float32).astype(jnp.bfloat16)
    per = keys.shape[0] // spans
    for c, lanes, n in head_places(spans, keys.shape[1]):
        scores_ref[n] = lax.dot_general(
            query_ref[c * SPAN : (c + 1) * SPAN, lanes],
            keys[c * per : (c + 1) * per, lanes],
            (((1,), (1,)), ((), ())),
            preferred_element_type=jnp.float32,
        )


def score_kernel(spans, picked_ref, wk_ref, query_ref, scores_ref):
    score(spans, by_span(picked_ref[...], spans, wk_ref.shape[0]), wk_ref, query_ref, scores_ref)


def scores_shape(picked, queries, channels, spans):
    return spans * (queries.shape[1] // HD), SPAN, picked.size // channels // spans


def own_scores(picked, w_key, queries, spans):
    return pl.pallas_call(
        functools.partial(score_kernel, spans),
        out_shape=jax.ShapeDtypeStruct(scores_shape(picked, queries, w_key.shape[0], spans), jnp.float32),
        in_specs=[VMEM] * 3,
        out_specs=VMEM,
        compiler_params=params(),
    )(picked, w_key, queries)


def attend_kernel(spans, own_ref, other_ref, wk_ref, wv_ref, query_ref, first_ref, out_ref, second_ref, probs_ref):
    channels = wk_ref.shape[0]
    other = by_span(other_ref[...], spans, channels)
    score(spans, other, wk_ref, query_ref, second_ref)
    per = other.shape[0] // spans
    own = by_span(own_ref[...], spans, channels)
    source = []
    for c in range(spans):
        source += [own[c * per : (c + 1) * per], other[c * per : (c + 1) * per]]
    source = jnp.concatenate(source, axis=0)
    values = jnp.dot(source, wv_ref[...], preferred_element_type=jnp.float32).astype(jnp.bfloat16)
    places = head_places(spans, values.shape[1])
    for c, lanes, n in places:
        scores = jnp.concatenate([first_ref[n], second_ref[n]], axis=1)
        raised = jnp.exp2((scores - jnp.max(scores, axis=-1, keepdims=True)) * EXPONENT)
        probs_ref[n] = (raised * (1.0 / jnp.sum(raised, axis=-1, keepdims=True))).astype(jnp.bfloat16)
    for c, lanes, n in places:
        mixed = jnp.dot(probs_ref[n], values[2 * c * per : 2 * (c + 1) * per, lanes], preferred_element_type=jnp.float32)
        out_ref[c * SPAN : (c + 1) * SPAN, lanes] = mixed.astype(out_ref.dtype)


def attend(picked, other, w_key, w_value, queries, first, spans):
    each = scores_shape(picked, queries, w_key.shape[0], spans)
    return pl.pallas_call(
        functools.partial(attend_kernel, spans),
        out_shape=jax.ShapeDtypeStruct(queries.shape, queries.dtype),
        in_specs=[VMEM] * 6,
        out_specs=VMEM,
        scratch_shapes=[pltpu.VMEM(each, jnp.float32), pltpu.VMEM(each[:2] + (2 * each[2],), jnp.bfloat16)],
        compiler_params=params(),
    )(picked, other, w_key, w_value, queries, first)


def gathered_plan(queries, encodings, w_key, w_value, block_owner, block_row):
    wide_count = lax.axis_size("wide")
    turns = wide_count // SIDE
    rows = encodings.shape[0]
    spans = queries.shape[0] // SPAN
    line = ring_order(turns)
    ring = [
        (here * SIDE + x, there * SIDE + x) for here, there in zip(line, line[1:] + line[:1]) for x in range(SIDE)
    ]
    across = [(n, n + 1 if n % SIDE == 0 else n - 1) for n in range(wide_count)]
    held = [[piece] for piece in half_columns(encodings)]
    crossed = [[] for _ in held]
    for k in range(turns - 1):
        for straight, side in zip(held, crossed):
            onward = lax.ppermute(straight[k], "wide", ring)
            aside = lax.ppermute(straight[k], "wide", across)
            onward, aside = lax.optimization_barrier((onward, aside))
            straight.append(onward)
            side.append(aside)
    last = [
        lax.ppermute(held[n][-1], "wide", across) if n % 2 == 0 else lax.ppermute(crossed[n][-1], "wide", ring)
        for n in range(STREAMS)
    ]
    order = [
        [straight[0]] + [chunk for pair in zip(straight[1:], side) for chunk in pair]
        for straight, side in zip(held, crossed)
    ]
    there = len(order[0]) - 2
    index, begun = early(jnp.transpose(block_owner, (0, 2, 1)), block_row, [chunks[:there] for chunks in order])
    picked = pick(index, begun, [chunks[there:] + [final] for chunks, final in zip(order, last)], there * rows)
    other = lax.ppermute(picked, "heads", [(0, 1), (1, 0)])
    first = own_scores(picked, w_key, queries, spans)
    return attend(picked, other, w_key, w_value, queries, first, spans)


def exchange(encodings, owners, stored, capacity):
    wide_count = lax.axis_size("wide")
    requests = owners.shape[0]
    order = jnp.arange(requests, dtype=jnp.int32)
    earlier = (owners[:, None] == owners[None, :]) & (order[None, :] < order[:, None])
    rank = jnp.sum(earlier.astype(jnp.int32), axis=1)
    slot = owners * capacity + rank
    table = jnp.full((wide_count * capacity,), -1, jnp.int32).at[slot].set(stored)
    table = table.reshape(wide_count, capacity)
    asked = lax.all_to_all(table, "wide", split_axis=0, concat_axis=0, tiled=True)
    wanted = jnp.maximum(asked, 0)
    picked = encodings[wanted]
    returned = lax.all_to_all(picked, "wide", split_axis=0, concat_axis=0, tiled=True)
    return returned.reshape(wide_count * capacity, encodings.shape[1])[slot]


def exchanged_plan(queries, encodings, w_key, w_value, owners, stored, capacity):
    fetched = exchange(encodings, owners, stored, capacity)
    channels = w_key.shape[0]
    source = fetched.reshape(-1, channels)
    keys = jnp.dot(source, w_key, preferred_element_type=jnp.float32).astype(jnp.bfloat16)
    values = jnp.dot(source, w_value, preferred_element_type=jnp.float32).astype(jnp.bfloat16)
    span_count = queries.shape[0] // SPAN
    heads_local = w_key.shape[1] // HD
    keys = keys.reshape(span_count, -1, heads_local, HD)
    values = values.reshape(span_count, -1, heads_local, HD)
    query_part = queries.reshape(span_count, SPAN, heads_local, HD)
    scores = jnp.einsum(
        "cqhd,ckhd->chqk", query_part, keys, preferred_element_type=jnp.float32
    ) * HD ** (-0.5)
    probs = jax.nn.softmax(scores, axis=-1).astype(jnp.bfloat16)
    mixed = jnp.einsum("chqk,ckhd->cqhd", probs, values, preferred_element_type=jnp.float32)
    return mixed.astype(jnp.bfloat16).reshape(queries.shape)


def on_device(queries, encodings, w_key, w_value, block_owner, block_row):
    wide_count = lax.axis_size("wide")
    requests = block_row.size
    capacity = 2 * ((requests + wide_count - 1) // wide_count)
    if encodings.shape[0] <= 2 * capacity:
        return gathered_plan(queries, encodings, w_key, w_value, block_owner, block_row)
    return exchanged_plan(
        queries, encodings, w_key, w_value, block_owner.reshape(-1), block_row.reshape(-1), capacity
    )


def solution(mesh):
    placed = (
        P(("groups", "wide"), "heads"),
        P(("groups", "wide"), None),
        P(None, "heads"),
        P(None, "heads"),
        P(("groups", "wide"), None, None),
        P(("groups", "wide"), None),
    )
    return jax.shard_map(
        on_device,
        mesh=mesh,
        in_specs=placed,
        out_specs=P(("groups", "wide"), "heads"),
        check_vma=False,
    )
```

```python
import functools

import jax
import jax.numpy as jnp
from jax import lax
from jax.experimental import pallas as pl
from jax.experimental.pallas import tpu as pltpu
from jax.sharding import PartitionSpec as P

HD = 128
SPAN = 64
SIDE = 2
LIMIT = 24 * 1024 * 1024
STREAMS = 2
EXPONENT = HD ** (-0.5) * 1.4426950408889634
VMEM = pl.BlockSpec(memory_space=pltpu.VMEM)


def params():
    return pltpu.CompilerParams(vmem_limit_bytes=LIMIT)


def half_kernel(enc_ref, *refs):
    outs, sems = refs[:-1], refs[-1]
    width = outs[0].shape[1]
    start = lax.axis_index("heads") * len(outs) * width
    copies = [
        pltpu.make_async_copy(enc_ref.at[:, pl.ds(pl.multiple_of(start + n * width, 128), width)], out, sems.at[n])
        for n, out in enumerate(outs)
    ]
    for copy in copies:
        copy.start()
    for copy in copies:
        copy.wait()


def half_columns(encodings):
    rows, columns = encodings.shape
    width = columns // lax.axis_size("heads") // STREAMS
    return pl.pallas_call(
        half_kernel,
        out_shape=[jax.ShapeDtypeStruct((rows, width), encodings.dtype)] * STREAMS,
        in_specs=[VMEM],
        out_specs=[VMEM] * STREAMS,
        scratch_shapes=[pltpu.SemaphoreType.DMA((STREAMS,))],
        compiler_params=params(),
    )(encodings)


def chosen_rows(index, sources, first):
    chunks = len(sources) // STREAMS
    rows = sources[0].shape[0]
    places = lax.broadcasted_iota(jnp.int32, (index.shape[0], chunks * rows), 1) + first
    chosen = jnp.where(places == index, 1.0, 0.0).astype(sources[0].dtype)
    parts = []
    for n in range(STREAMS):
        held = jnp.concatenate([ref[...] for ref in sources[n * chunks : (n + 1) * chunks]], axis=0)
        parts.append(jnp.dot(chosen, held, preferred_element_type=jnp.float32))
    return jnp.concatenate(parts, axis=1)


def ring_order(turns):
    return [0] + list(range(1, turns, 2)) + list(range(turns - 2 + turns % 2, 0, -2))


def ring_place(line, turns):
    return jnp.where(line % 2 == 1, (line + 1) // 2, jnp.where(line == 0, 0, turns - line // 2))


def wanted_rows(order, turns, rows, owner_ref, stored_ref):
    me = lax.axis_index("wide")
    columns = []
    for c in range(stored_ref.shape[0]):
        owner, stored = owner_ref[c], stored_ref[c : c + 1, :]
        back = ring_place(me // SIDE, turns) - ring_place(owner // SIDE, turns)
        back = jnp.where(back < 0, back + turns, back)
        beside = jnp.where(owner % SIDE == me % SIDE, 0, 1)
        place = jnp.zeros_like(stored)
        for n, chunk in enumerate(order):
            place = jnp.where(back * 2 + beside == chunk[0] * 2 + chunk[1], n, place)
        place = place * rows + stored
        square = (place.shape[1], place.shape[1])
        own = lax.broadcasted_iota(jnp.int32, square, 0) == lax.broadcasted_iota(jnp.int32, square, 1)
        spread = jnp.where(own, jnp.broadcast_to(place.astype(jnp.float32), square), 0.0)
        columns.append(jnp.sum(spread, axis=1, keepdims=True))
    return jnp.concatenate(columns, axis=0).astype(jnp.int32)


def early_kernel(order, turns, owner_ref, stored_ref, *refs):
    sources, index_ref, out_ref = refs[:-2], refs[-2], refs[-1]
    index_ref[...] = wanted_rows(order, turns, sources[0].shape[0], owner_ref, stored_ref)
    out_ref[...] = chosen_rows(index_ref[...], sources, 0).astype(out_ref.dtype)


def early(order, turns, owners, stored, streams):
    sources = [chunk for stream in streams for chunk in stream]
    rows, width = sources[0].shape
    requests = stored.size
    return pl.pallas_call(
        functools.partial(early_kernel, order, turns),
        out_shape=(
            jax.ShapeDtypeStruct((requests, 1), jnp.int32),
            jax.ShapeDtypeStruct((requests, STREAMS * width), sources[0].dtype),
        ),
        in_specs=[VMEM] * (2 + len(sources)),
        out_specs=(VMEM, VMEM),
        compiler_params=params(),
        cost_estimate=pl.CostEstimate(
            flops=2 * requests * width * rows * len(sources),
            bytes_accessed=2 * requests * width * STREAMS,
            transcendentals=0,
        ),
    )(owners, stored, *sources)


def pick_kernel(first, index_ref, begun_ref, *refs):
    picked = chosen_rows(index_ref[...], refs[:-1], first)
    refs[-1][...] = (picked + begun_ref[...].astype(jnp.float32)).astype(begun_ref.dtype)


def pick(index, begun, streams, first):
    sources = [chunk for stream in streams for chunk in stream]
    return pl.pallas_call(
        functools.partial(pick_kernel, first),
        out_shape=jax.ShapeDtypeStruct(begun.shape, begun.dtype),
        in_specs=[VMEM] * (2 + len(sources)),
        out_specs=VMEM,
        compiler_params=params(),
    )(index, begun, *sources)


def by_span(picked, spans, channels):
    per = picked.shape[0] // spans
    parts = []
    for c in range(spans):
        for t in range(picked.shape[1] // channels):
            parts.append(picked[c * per : (c + 1) * per, t * channels : (t + 1) * channels])
    return jnp.concatenate(parts, axis=0)


def head_places(spans, columns):
    heads = columns // HD
    return [(c, slice(h * HD, (h + 1) * HD), c * heads + h) for c in range(spans) for h in range(heads)]


def score(spans, source, wk_ref, query_ref, scores_ref):
    keys = jnp.dot(source, wk_ref[...], preferred_element_type=jnp.float32).astype(jnp.bfloat16)
    per = keys.shape[0] // spans
    for c, lanes, n in head_places(spans, keys.shape[1]):
        scores_ref[n] = lax.dot_general(
            query_ref[c * SPAN : (c + 1) * SPAN, lanes],
            keys[c * per : (c + 1) * per, lanes],
            (((1,), (1,)), ((), ())),
            preferred_element_type=jnp.float32,
        )


def score_kernel(spans, picked_ref, wk_ref, query_ref, scores_ref):
    score(spans, by_span(picked_ref[...], spans, wk_ref.shape[0]), wk_ref, query_ref, scores_ref)


def scores_shape(picked, queries, channels, spans):
    return spans * (queries.shape[1] // HD), SPAN, picked.size // channels // spans


def own_scores(picked, w_key, queries, spans):
    return pl.pallas_call(
        functools.partial(score_kernel, spans),
        out_shape=jax.ShapeDtypeStruct(scores_shape(picked, queries, w_key.shape[0], spans), jnp.float32),
        in_specs=[VMEM] * 3,
        out_specs=VMEM,
        compiler_params=params(),
    )(picked, w_key, queries)


def values_kernel(spans, picked_ref, wv_ref, values_ref):
    source = by_span(picked_ref[...], spans, wv_ref.shape[0])
    values_ref[...] = jnp.dot(source, wv_ref[...], preferred_element_type=jnp.float32).astype(values_ref.dtype)


def own_values(picked, w_value, spans):
    rows = picked.size // w_value.shape[0]
    return pl.pallas_call(
        functools.partial(values_kernel, spans),
        out_shape=jax.ShapeDtypeStruct((rows, w_value.shape[1]), picked.dtype),
        in_specs=[VMEM] * 2,
        out_specs=VMEM,
        compiler_params=params(),
    )(picked, w_value)


def attend_kernel(
    spans, other_ref, wk_ref, wv_ref, query_ref, first_ref, values_ref, out_ref, second_ref, probs_ref
):
    other = by_span(other_ref[...], spans, wk_ref.shape[0])
    score(spans, other, wk_ref, query_ref, second_ref)
    per = other.shape[0] // spans
    more = jnp.dot(other, wv_ref[...], preferred_element_type=jnp.float32).astype(jnp.bfloat16)
    places = head_places(spans, more.shape[1])
    for c, lanes, n in places:
        scores = jnp.concatenate([first_ref[n], second_ref[n]], axis=1)
        raised = jnp.exp2((scores - jnp.max(scores, axis=-1, keepdims=True)) * EXPONENT)
        probs_ref[n] = (raised * (1.0 / jnp.sum(raised, axis=-1, keepdims=True))).astype(jnp.bfloat16)
    for c, lanes, n in places:
        rows = slice(c * per, (c + 1) * per)
        values = jnp.concatenate([values_ref[rows, lanes], more[rows, lanes]], axis=0)
        mixed = jnp.dot(probs_ref[n], values, preferred_element_type=jnp.float32)
        out_ref[c * SPAN : (c + 1) * SPAN, lanes] = mixed.astype(out_ref.dtype)


def attend(other, w_key, w_value, queries, first, values, spans):
    each = scores_shape(other, queries, w_key.shape[0], spans)
    return pl.pallas_call(
        functools.partial(attend_kernel, spans),
        out_shape=jax.ShapeDtypeStruct(queries.shape, queries.dtype),
        in_specs=[VMEM] * 6,
        out_specs=VMEM,
        scratch_shapes=[pltpu.VMEM(each, jnp.float32), pltpu.VMEM(each[:2] + (2 * each[2],), jnp.bfloat16)],
        compiler_params=params(),
    )(other, w_key, w_value, queries, first, values)


def send(chunk, pairs):
    return lax.ppermute(chunk, "wide", pairs)


def gathered_plan(queries, encodings, w_key, w_value, block_owner, block_row):
    wide_count = lax.axis_size("wide")
    turns = wide_count // SIDE
    rows = encodings.shape[0]
    spans = queries.shape[0] // SPAN
    line = ring_order(turns)
    onward = [
        (here * SIDE + x, there * SIDE + x) for here, there in zip(line, line[1:] + line[:1]) for x in range(SIDE)
    ]
    backward = [(there, here) for here, there in onward]
    across = [(n, n + 1 if n % SIDE == 0 else n - 1) for n in range(wide_count)]
    ahead = turns // 2
    pieces = half_columns(encodings)
    streams = [{(0, 0): piece} for piece in pieces]
    for k in range(1, ahead + 1):
        for held in streams:
            held[k, 0], held[k - 1, 1] = lax.optimization_barrier(
                (send(held[k - 1, 0], onward), send(held[k - 1, 0], across))
            )
    for k in range(turns - 1, ahead, -1):
        for held in streams:
            source = held[(k + 1) % turns, 0]
            if k == turns - 1:
                source, streams[0][1, 0] = lax.optimization_barrier((source, streams[0][1, 0]))
            held[k, 0] = send(source, backward)
            if k < turns - 1:
                held[k + 1, 1] = send(source, across)
    for n, held in enumerate(streams):
        held[ahead, 1] = send(held[ahead, 0], across)
        k = ahead + 1
        held[k, 1] = send(held[k, 0], across) if n % 2 == 0 else send(held[(k + 1) % turns, 1], backward)
    late = [(ahead, 1), (ahead + 1, 1)]
    order = [chunk for chunk in streams[0] if chunk not in late] + late
    there = len(order) - len(late)
    index, begun = early(
        order,
        turns,
        jnp.transpose(block_owner, (0, 2, 1)),
        block_row,
        [[held[chunk] for chunk in order[:there]] for held in streams],
    )
    picked = pick(index, begun, [[held[chunk] for chunk in late] for held in streams], there * rows)
    other = lax.ppermute(picked, "heads", [(0, 1), (1, 0)])
    first = own_scores(picked, w_key, queries, spans)
    values = own_values(picked, w_value, spans)
    return attend(other, w_key, w_value, queries, first, values, spans)


def exchange(encodings, owners, stored, capacity):
    wide_count = lax.axis_size("wide")
    requests = owners.shape[0]
    order = jnp.arange(requests, dtype=jnp.int32)
    earlier = (owners[:, None] == owners[None, :]) & (order[None, :] < order[:, None])
    rank = jnp.sum(earlier.astype(jnp.int32), axis=1)
    slot = owners * capacity + rank
    table = jnp.full((wide_count * capacity,), -1, jnp.int32).at[slot].set(stored)
    table = table.reshape(wide_count, capacity)
    asked = lax.all_to_all(table, "wide", split_axis=0, concat_axis=0, tiled=True)
    wanted = jnp.maximum(asked, 0)
    picked = encodings[wanted]
    returned = lax.all_to_all(picked, "wide", split_axis=0, concat_axis=0, tiled=True)
    return returned.reshape(wide_count * capacity, encodings.shape[1])[slot]


def exchanged_plan(queries, encodings, w_key, w_value, owners, stored, capacity):
    fetched = exchange(encodings, owners, stored, capacity)
    channels = w_key.shape[0]
    source = fetched.reshape(-1, channels)
    keys = jnp.dot(source, w_key, preferred_element_type=jnp.float32).astype(jnp.bfloat16)
    values = jnp.dot(source, w_value, preferred_element_type=jnp.float32).astype(jnp.bfloat16)
    span_count = queries.shape[0] // SPAN
    heads_local = w_key.shape[1] // HD
    keys = keys.reshape(span_count, -1, heads_local, HD)
    values = values.reshape(span_count, -1, heads_local, HD)
    query_part = queries.reshape(span_count, SPAN, heads_local, HD)
    scores = jnp.einsum(
        "cqhd,ckhd->chqk", query_part, keys, preferred_element_type=jnp.float32
    ) * HD ** (-0.5)
    probs = jax.nn.softmax(scores, axis=-1).astype(jnp.bfloat16)
    mixed = jnp.einsum("chqk,ckhd->cqhd", probs, values, preferred_element_type=jnp.float32)
    return mixed.astype(jnp.bfloat16).reshape(queries.shape)


def on_device(queries, encodings, w_key, w_value, block_owner, block_row):
    wide_count = lax.axis_size("wide")
    requests = block_row.size
    capacity = 2 * ((requests + wide_count - 1) // wide_count)
    if encodings.shape[0] <= 2 * capacity:
        return gathered_plan(queries, encodings, w_key, w_value, block_owner, block_row)
    return exchanged_plan(
        queries, encodings, w_key, w_value, block_owner.reshape(-1), block_row.reshape(-1), capacity
    )


def solution(mesh):
    placed = (
        P(("groups", "wide"), "heads"),
        P(("groups", "wide"), None),
        P(None, "heads"),
        P(None, "heads"),
        P(("groups", "wide"), None, None),
        P(("groups", "wide"), None),
    )
    return jax.shard_map(
        on_device,
        mesh=mesh,
        in_specs=placed,
        out_specs=P(("groups", "wide"), "heads"),
        check_vma=False,
    )
```

```python
import functools

import jax
import jax.numpy as jnp
from jax import lax
from jax.experimental import pallas as pl
from jax.experimental.pallas import tpu as pltpu
from jax.sharding import PartitionSpec as P

HD = 128
SPAN = 64
SIDE = 2
LIMIT = 24 * 1024 * 1024
STREAMS = 2
EXPONENT = HD ** (-0.5) * 1.4426950408889634
VMEM = pl.BlockSpec(memory_space=pltpu.VMEM)


def params():
    return pltpu.CompilerParams(vmem_limit_bytes=LIMIT)


def half_kernel(enc_ref, *refs):
    outs, sems = refs[:-1], refs[-1]
    width = outs[0].shape[1]
    start = lax.axis_index("heads") * len(outs) * width
    copies = [
        pltpu.make_async_copy(enc_ref.at[:, pl.ds(pl.multiple_of(start + n * width, 128), width)], out, sems.at[n])
        for n, out in enumerate(outs)
    ]
    for copy in copies:
        copy.start()
    for copy in copies:
        copy.wait()


def half_columns(encodings):
    rows, columns = encodings.shape
    width = columns // lax.axis_size("heads") // STREAMS
    return pl.pallas_call(
        half_kernel,
        out_shape=[jax.ShapeDtypeStruct((rows, width), encodings.dtype)] * STREAMS,
        in_specs=[VMEM],
        out_specs=[VMEM] * STREAMS,
        scratch_shapes=[pltpu.SemaphoreType.DMA((STREAMS,))],
        compiler_params=params(),
    )(encodings)


def chosen_rows(index, sources, first):
    chunks = len(sources) // STREAMS
    rows = sources[0].shape[0]
    places = lax.broadcasted_iota(jnp.int32, (index.shape[0], chunks * rows), 1) + first
    chosen = jnp.where(places == index, 1.0, 0.0).astype(sources[0].dtype)
    parts = []
    for n in range(STREAMS):
        held = jnp.concatenate([ref[...] for ref in sources[n * chunks : (n + 1) * chunks]], axis=0)
        parts.append(jnp.dot(chosen, held, preferred_element_type=jnp.float32))
    return jnp.concatenate(parts, axis=1)


def ring_order(turns):
    return [0] + list(range(1, turns, 2)) + list(range(turns - 2 + turns % 2, 0, -2))


def ring_place(line, turns):
    return jnp.where(line % 2 == 1, (line + 1) // 2, jnp.where(line == 0, 0, turns - line // 2))


def wanted_rows(order, turns, rows, owner_ref, stored_ref):
    me = lax.axis_index("wide")
    columns = []
    for c in range(stored_ref.shape[0]):
        owner, stored = owner_ref[c], stored_ref[c : c + 1, :]
        back = ring_place(me // SIDE, turns) - ring_place(owner // SIDE, turns)
        back = jnp.where(back < 0, back + turns, back)
        beside = jnp.where(owner % SIDE == me % SIDE, 0, 1)
        place = jnp.zeros_like(stored)
        for n, chunk in enumerate(order):
            place = jnp.where(back * 2 + beside == chunk[0] * 2 + chunk[1], n, place)
        place = place * rows + stored
        square = (place.shape[1], place.shape[1])
        own = lax.broadcasted_iota(jnp.int32, square, 0) == lax.broadcasted_iota(jnp.int32, square, 1)
        spread = jnp.where(own, jnp.broadcast_to(place.astype(jnp.float32), square), 0.0)
        columns.append(jnp.sum(spread, axis=1, keepdims=True))
    return jnp.concatenate(columns, axis=0).astype(jnp.int32)


def early_kernel(order, turns, owner_ref, stored_ref, *refs):
    sources, index_ref, out_ref = refs[:-2], refs[-2], refs[-1]
    index_ref[...] = wanted_rows(order, turns, sources[0].shape[0], owner_ref, stored_ref)
    out_ref[...] = chosen_rows(index_ref[...], sources, 0).astype(out_ref.dtype)


def early(order, turns, owners, stored, streams):
    sources = [chunk for stream in streams for chunk in stream]
    rows, width = sources[0].shape
    requests = stored.size
    return pl.pallas_call(
        functools.partial(early_kernel, order, turns),
        out_shape=(
            jax.ShapeDtypeStruct((requests, 1), jnp.int32),
            jax.ShapeDtypeStruct((requests, STREAMS * width), sources[0].dtype),
        ),
        in_specs=[VMEM] * (2 + len(sources)),
        out_specs=(VMEM, VMEM),
        compiler_params=params(),
        cost_estimate=pl.CostEstimate(
            flops=2 * requests * width * rows * len(sources),
            bytes_accessed=2 * requests * width * STREAMS,
            transcendentals=0,
        ),
    )(owners, stored, *sources)


def pick_kernel(first, index_ref, begun_ref, *refs):
    picked = chosen_rows(index_ref[...], refs[:-1], first)
    refs[-1][...] = (picked + begun_ref[...].astype(jnp.float32)).astype(begun_ref.dtype)


def pick(index, begun, streams, first):
    sources = [chunk for stream in streams for chunk in stream]
    return pl.pallas_call(
        functools.partial(pick_kernel, first),
        out_shape=jax.ShapeDtypeStruct(begun.shape, begun.dtype),
        in_specs=[VMEM] * (2 + len(sources)),
        out_specs=VMEM,
        compiler_params=params(),
    )(index, begun, *sources)


def by_span(picked, spans, channels):
    per = picked.shape[0] // spans
    parts = []
    for c in range(spans):
        for t in range(picked.shape[1] // channels):
            parts.append(picked[c * per : (c + 1) * per, t * channels : (t + 1) * channels])
    return jnp.concatenate(parts, axis=0)


def head_places(spans, columns):
    heads = columns // HD
    return [(c, slice(h * HD, (h + 1) * HD), c * heads + h) for c in range(spans) for h in range(heads)]


def score(spans, source, wk_ref, query_ref, scores_ref):
    keys = jnp.dot(source, wk_ref[...], preferred_element_type=jnp.float32).astype(jnp.bfloat16)
    per = keys.shape[0] // spans
    for c, lanes, n in head_places(spans, keys.shape[1]):
        scores_ref[n] = lax.dot_general(
            query_ref[c * SPAN : (c + 1) * SPAN, lanes],
            keys[c * per : (c + 1) * per, lanes],
            (((1,), (1,)), ((), ())),
            preferred_element_type=jnp.float32,
        )


def score_kernel(spans, picked_ref, wk_ref, query_ref, scores_ref):
    score(spans, by_span(picked_ref[...], spans, wk_ref.shape[0]), wk_ref, query_ref, scores_ref)


def scores_shape(picked, queries, channels, spans):
    return spans * (queries.shape[1] // HD), SPAN, picked.size // channels // spans


def own_scores(picked, w_key, queries, spans):
    return pl.pallas_call(
        functools.partial(score_kernel, spans),
        out_shape=jax.ShapeDtypeStruct(scores_shape(picked, queries, w_key.shape[0], spans), jnp.float32),
        in_specs=[VMEM] * 3,
        out_specs=VMEM,
        compiler_params=params(),
    )(picked, w_key, queries)


def values_kernel(spans, picked_ref, wv_ref, values_ref):
    source = by_span(picked_ref[...], spans, wv_ref.shape[0])
    values_ref[...] = jnp.dot(source, wv_ref[...], preferred_element_type=jnp.float32).astype(values_ref.dtype)


def own_values(picked, w_value, spans):
    rows = picked.size // w_value.shape[0]
    return pl.pallas_call(
        functools.partial(values_kernel, spans),
        out_shape=jax.ShapeDtypeStruct((rows, w_value.shape[1]), picked.dtype),
        in_specs=[VMEM] * 2,
        out_specs=VMEM,
        compiler_params=params(),
    )(picked, w_value)


def attend_kernel(
    spans, other_ref, wk_ref, wv_ref, query_ref, first_ref, values_ref, out_ref, second_ref, probs_ref
):
    other = by_span(other_ref[...], spans, wk_ref.shape[0])
    score(spans, other, wk_ref, query_ref, second_ref)
    per = other.shape[0] // spans
    more = jnp.dot(other, wv_ref[...], preferred_element_type=jnp.float32).astype(jnp.bfloat16)
    places = head_places(spans, more.shape[1])
    for c, lanes, n in places:
        scores = jnp.concatenate([first_ref[n], second_ref[n]], axis=1)
        raised = jnp.exp2((scores - jnp.max(scores, axis=-1, keepdims=True)) * EXPONENT)
        probs_ref[n] = (raised * (1.0 / jnp.sum(raised, axis=-1, keepdims=True))).astype(jnp.bfloat16)
    for c, lanes, n in places:
        rows = slice(c * per, (c + 1) * per)
        values = jnp.concatenate([values_ref[rows, lanes], more[rows, lanes]], axis=0)
        mixed = jnp.dot(probs_ref[n], values, preferred_element_type=jnp.float32)
        out_ref[c * SPAN : (c + 1) * SPAN, lanes] = mixed.astype(out_ref.dtype)


def attend(other, w_key, w_value, queries, first, values, spans):
    each = scores_shape(other, queries, w_key.shape[0], spans)
    return pl.pallas_call(
        functools.partial(attend_kernel, spans),
        out_shape=jax.ShapeDtypeStruct(queries.shape, queries.dtype),
        in_specs=[VMEM] * 6,
        out_specs=VMEM,
        scratch_shapes=[pltpu.VMEM(each, jnp.float32), pltpu.VMEM(each[:2] + (2 * each[2],), jnp.bfloat16)],
        compiler_params=params(),
    )(other, w_key, w_value, queries, first, values)


def send(chunk, pairs):
    return lax.ppermute(chunk, "wide", pairs)


def gathered_plan(queries, encodings, w_key, w_value, block_owner, block_row):
    wide_count = lax.axis_size("wide")
    turns = wide_count // SIDE
    rows = encodings.shape[0]
    spans = queries.shape[0] // SPAN
    line = ring_order(turns)
    onward = [
        (here * SIDE + x, there * SIDE + x) for here, there in zip(line, line[1:] + line[:1]) for x in range(SIDE)
    ]
    across = [(n, n + 1 if n % SIDE == 0 else n - 1) for n in range(wide_count)]
    streams = [{(0, 0): piece} for piece in half_columns(encodings)]
    for k in range(1, turns):
        for held in streams:
            held[k, 0] = send(held[k - 1, 0], onward)
            held[k - 1, 1] = send(held[k - 1, 0], across)
            if k > 1:
                held[k, 0], held[k - 2, 1] = lax.optimization_barrier((held[k, 0], held[k - 2, 1]))
    for n, held in enumerate(streams):
        held[turns - 1, 1] = send(held[turns - 1, 0], across) if n % 2 == 0 else send(held[turns - 2, 1], onward)
    late = [(turns - 1, 0), (turns - 2, 1), (turns - 1, 1)]
    order = [chunk for chunk in streams[0] if chunk not in late] + late
    there = len(order) - len(late)
    index, begun = early(
        order,
        turns,
        jnp.transpose(block_owner, (0, 2, 1)),
        block_row,
        [[held[chunk] for chunk in order[:there]] for held in streams],
    )
    picked = pick(index, begun, [[held[chunk] for chunk in late] for held in streams], there * rows)
    other = lax.ppermute(picked, "heads", [(0, 1), (1, 0)])
    first = own_scores(picked, w_key, queries, spans)
    values = own_values(picked, w_value, spans)
    return attend(other, w_key, w_value, queries, first, values, spans)


def exchange(encodings, owners, stored, capacity):
    wide_count = lax.axis_size("wide")
    requests = owners.shape[0]
    order = jnp.arange(requests, dtype=jnp.int32)
    earlier = (owners[:, None] == owners[None, :]) & (order[None, :] < order[:, None])
    rank = jnp.sum(earlier.astype(jnp.int32), axis=1)
    slot = owners * capacity + rank
    table = jnp.full((wide_count * capacity,), -1, jnp.int32).at[slot].set(stored)
    table = table.reshape(wide_count, capacity)
    asked = lax.all_to_all(table, "wide", split_axis=0, concat_axis=0, tiled=True)
    wanted = jnp.maximum(asked, 0)
    picked = encodings[wanted]
    returned = lax.all_to_all(picked, "wide", split_axis=0, concat_axis=0, tiled=True)
    return returned.reshape(wide_count * capacity, encodings.shape[1])[slot]


def exchanged_plan(queries, encodings, w_key, w_value, owners, stored, capacity):
    fetched = exchange(encodings, owners, stored, capacity)
    channels = w_key.shape[0]
    source = fetched.reshape(-1, channels)
    keys = jnp.dot(source, w_key, preferred_element_type=jnp.float32).astype(jnp.bfloat16)
    values = jnp.dot(source, w_value, preferred_element_type=jnp.float32).astype(jnp.bfloat16)
    span_count = queries.shape[0] // SPAN
    heads_local = w_key.shape[1] // HD
    keys = keys.reshape(span_count, -1, heads_local, HD)
    values = values.reshape(span_count, -1, heads_local, HD)
    query_part = queries.reshape(span_count, SPAN, heads_local, HD)
    scores = jnp.einsum(
        "cqhd,ckhd->chqk", query_part, keys, preferred_element_type=jnp.float32
    ) * HD ** (-0.5)
    probs = jax.nn.softmax(scores, axis=-1).astype(jnp.bfloat16)
    mixed = jnp.einsum("chqk,ckhd->cqhd", probs, values, preferred_element_type=jnp.float32)
    return mixed.astype(jnp.bfloat16).reshape(queries.shape)


def on_device(queries, encodings, w_key, w_value, block_owner, block_row):
    wide_count = lax.axis_size("wide")
    requests = block_row.size
    capacity = 2 * ((requests + wide_count - 1) // wide_count)
    if encodings.shape[0] <= 2 * capacity:
        return gathered_plan(queries, encodings, w_key, w_value, block_owner, block_row)
    return exchanged_plan(
        queries, encodings, w_key, w_value, block_owner.reshape(-1), block_row.reshape(-1), capacity
    )


def solution(mesh):
    placed = (
        P(("groups", "wide"), "heads"),
        P(("groups", "wide"), None),
        P(None, "heads"),
        P(None, "heads"),
        P(("groups", "wide"), None, None),
        P(("groups", "wide"), None),
    )
    return jax.shard_map(
        on_device,
        mesh=mesh,
        in_specs=placed,
        out_specs=P(("groups", "wide"), "heads"),
        check_vma=False,
    )
```

```python
import functools

import jax
import jax.numpy as jnp
from jax import lax
from jax.experimental import pallas as pl
from jax.experimental.pallas import tpu as pltpu
from jax.sharding import PartitionSpec as P

HD = 128
SPAN = 64
SIDE = 2
LIMIT = 24 * 1024 * 1024
STREAMS = 2
EXPONENT = HD ** (-0.5) * 1.4426950408889634
VMEM = pl.BlockSpec(memory_space=pltpu.VMEM)


def params():
    return pltpu.CompilerParams(vmem_limit_bytes=LIMIT)


def half_kernel(enc_ref, *refs):
    outs, sems = refs[:-1], refs[-1]
    width = outs[0].shape[1]
    start = lax.axis_index("heads") * len(outs) * width
    copies = [
        pltpu.make_async_copy(enc_ref.at[:, pl.ds(pl.multiple_of(start + n * width, 128), width)], out, sems.at[n])
        for n, out in enumerate(outs)
    ]
    for copy in copies:
        copy.start()
    for copy in copies:
        copy.wait()


def half_columns(encodings):
    rows, columns = encodings.shape
    width = columns // lax.axis_size("heads") // STREAMS
    return pl.pallas_call(
        half_kernel,
        out_shape=[jax.ShapeDtypeStruct((rows, width), encodings.dtype)] * STREAMS,
        in_specs=[VMEM],
        out_specs=[VMEM] * STREAMS,
        scratch_shapes=[pltpu.SemaphoreType.DMA((STREAMS,))],
        compiler_params=params(),
    )(encodings)


def chosen_rows(index, sources, first):
    chunks = len(sources) // STREAMS
    rows = sources[0].shape[0]
    places = lax.broadcasted_iota(jnp.int32, (index.shape[0], chunks * rows), 1) + first
    chosen = jnp.where(places == index, 1.0, 0.0).astype(sources[0].dtype)
    parts = []
    for n in range(STREAMS):
        held = jnp.concatenate([ref[...] for ref in sources[n * chunks : (n + 1) * chunks]], axis=0)
        parts.append(jnp.dot(chosen, held, preferred_element_type=jnp.float32))
    return jnp.concatenate(parts, axis=1)


def ring_order(turns):
    return [0] + list(range(1, turns, 2)) + list(range(turns - 2 + turns % 2, 0, -2))


def ring_place(line, turns):
    return jnp.where(line % 2 == 1, (line + 1) // 2, jnp.where(line == 0, 0, turns - line // 2))


def wanted_rows(order, turns, rows, owner_ref, stored_ref):
    me = lax.axis_index("wide")
    columns = []
    for c in range(stored_ref.shape[0]):
        owner, stored = owner_ref[c], stored_ref[c : c + 1, :]
        back = ring_place(me // SIDE, turns) - ring_place(owner // SIDE, turns)
        back = jnp.where(back < 0, back + turns, back)
        beside = jnp.where(owner % SIDE == me % SIDE, 0, 1)
        place = jnp.zeros_like(stored)
        for n, chunk in enumerate(order):
            place = jnp.where(back * 2 + beside == chunk[0] * 2 + chunk[1], n, place)
        place = place * rows + stored
        square = (place.shape[1], place.shape[1])
        own = lax.broadcasted_iota(jnp.int32, square, 0) == lax.broadcasted_iota(jnp.int32, square, 1)
        spread = jnp.where(own, jnp.broadcast_to(place.astype(jnp.float32), square), 0.0)
        columns.append(jnp.sum(spread, axis=1, keepdims=True))
    return jnp.concatenate(columns, axis=0).astype(jnp.int32)


def early_kernel(order, turns, owner_ref, stored_ref, *refs):
    sources, index_ref, out_ref = refs[:-2], refs[-2], refs[-1]
    index_ref[...] = wanted_rows(order, turns, sources[0].shape[0], owner_ref, stored_ref)
    out_ref[...] = chosen_rows(index_ref[...], sources, 0).astype(out_ref.dtype)


def early(order, turns, owners, stored, streams):
    sources = [chunk for stream in streams for chunk in stream]
    rows, width = sources[0].shape
    requests = stored.size
    return pl.pallas_call(
        functools.partial(early_kernel, order, turns),
        out_shape=(
            jax.ShapeDtypeStruct((requests, 1), jnp.int32),
            jax.ShapeDtypeStruct((requests, STREAMS * width), sources[0].dtype),
        ),
        in_specs=[VMEM] * (2 + len(sources)),
        out_specs=(VMEM, VMEM),
        compiler_params=params(),
        cost_estimate=pl.CostEstimate(
            flops=2 * requests * width * rows * len(sources),
            bytes_accessed=2 * requests * width * STREAMS,
            transcendentals=0,
        ),
    )(owners, stored, *sources)


def pick_kernel(first, index_ref, begun_ref, *refs):
    picked = chosen_rows(index_ref[...], refs[:-1], first)
    refs[-1][...] = (picked + begun_ref[...].astype(jnp.float32)).astype(begun_ref.dtype)


def pick(index, begun, streams, first):
    sources = [chunk for stream in streams for chunk in stream]
    return pl.pallas_call(
        functools.partial(pick_kernel, first),
        out_shape=jax.ShapeDtypeStruct(begun.shape, begun.dtype),
        in_specs=[VMEM] * (2 + len(sources)),
        out_specs=VMEM,
        compiler_params=params(),
    )(index, begun, *sources)


def by_span(picked, spans, channels):
    per = picked.shape[0] // spans
    parts = []
    for c in range(spans):
        for t in range(picked.shape[1] // channels):
            parts.append(picked[c * per : (c + 1) * per, t * channels : (t + 1) * channels])
    return jnp.concatenate(parts, axis=0)


def head_places(spans, columns):
    heads = columns // HD
    return [(c, slice(h * HD, (h + 1) * HD), c * heads + h) for c in range(spans) for h in range(heads)]


def score(spans, source, wk_ref, query_ref, scores_ref):
    keys = jnp.dot(source, wk_ref[...], preferred_element_type=jnp.float32).astype(jnp.bfloat16)
    per = keys.shape[0] // spans
    for c, lanes, n in head_places(spans, keys.shape[1]):
        scores_ref[n] = lax.dot_general(
            query_ref[c * SPAN : (c + 1) * SPAN, lanes],
            keys[c * per : (c + 1) * per, lanes],
            (((1,), (1,)), ((), ())),
            preferred_element_type=jnp.float32,
        )


def score_kernel(spans, picked_ref, wk_ref, query_ref, scores_ref):
    score(spans, by_span(picked_ref[...], spans, wk_ref.shape[0]), wk_ref, query_ref, scores_ref)


def scores_shape(picked, queries, channels, spans):
    return spans * (queries.shape[1] // HD), SPAN, picked.size // channels // spans


def own_scores(picked, w_key, queries, spans):
    return pl.pallas_call(
        functools.partial(score_kernel, spans),
        out_shape=jax.ShapeDtypeStruct(scores_shape(picked, queries, w_key.shape[0], spans), jnp.float32),
        in_specs=[VMEM] * 3,
        out_specs=VMEM,
        compiler_params=params(),
    )(picked, w_key, queries)


def values_kernel(spans, picked_ref, wv_ref, values_ref):
    source = by_span(picked_ref[...], spans, wv_ref.shape[0])
    values_ref[...] = jnp.dot(source, wv_ref[...], preferred_element_type=jnp.float32).astype(values_ref.dtype)


def own_values(picked, w_value, spans):
    rows = picked.size // w_value.shape[0]
    return pl.pallas_call(
        functools.partial(values_kernel, spans),
        out_shape=jax.ShapeDtypeStruct((rows, w_value.shape[1]), picked.dtype),
        in_specs=[VMEM] * 2,
        out_specs=VMEM,
        compiler_params=params(),
    )(picked, w_value)


def attend_kernel(
    spans, other_ref, wk_ref, wv_ref, query_ref, first_ref, values_ref, out_ref, second_ref, probs_ref
):
    other = by_span(other_ref[...], spans, wk_ref.shape[0])
    score(spans, other, wk_ref, query_ref, second_ref)
    per = other.shape[0] // spans
    more = jnp.dot(other, wv_ref[...], preferred_element_type=jnp.float32).astype(jnp.bfloat16)
    places = head_places(spans, more.shape[1])
    for c, lanes, n in places:
        scores = jnp.concatenate([first_ref[n], second_ref[n]], axis=1)
        raised = jnp.exp2((scores - jnp.max(scores, axis=-1, keepdims=True)) * EXPONENT)
        probs_ref[n] = (raised * (1.0 / jnp.sum(raised, axis=-1, keepdims=True))).astype(jnp.bfloat16)
    for c, lanes, n in places:
        rows = slice(c * per, (c + 1) * per)
        values = jnp.concatenate([values_ref[rows, lanes], more[rows, lanes]], axis=0)
        mixed = jnp.dot(probs_ref[n], values, preferred_element_type=jnp.float32)
        out_ref[c * SPAN : (c + 1) * SPAN, lanes] = mixed.astype(out_ref.dtype)


def attend(other, w_key, w_value, queries, first, values, spans):
    each = scores_shape(other, queries, w_key.shape[0], spans)
    return pl.pallas_call(
        functools.partial(attend_kernel, spans),
        out_shape=jax.ShapeDtypeStruct(queries.shape, queries.dtype),
        in_specs=[VMEM] * 6,
        out_specs=VMEM,
        scratch_shapes=[pltpu.VMEM(each, jnp.float32), pltpu.VMEM(each[:2] + (2 * each[2],), jnp.bfloat16)],
        compiler_params=params(),
    )(other, w_key, w_value, queries, first, values)


def send(chunk, pairs):
    return lax.ppermute(chunk, "wide", pairs)


def gathered_plan(queries, encodings, w_key, w_value, block_owner, block_row):
    wide_count = lax.axis_size("wide")
    turns = wide_count // SIDE
    rows = encodings.shape[0]
    spans = queries.shape[0] // SPAN
    line = ring_order(turns)
    onward = [
        (here * SIDE + x, there * SIDE + x) for here, there in zip(line, line[1:] + line[:1]) for x in range(SIDE)
    ]
    across = [(n, n + 1 if n % SIDE == 0 else n - 1) for n in range(wide_count)]
    streams = [{(0, 0): piece} for piece in half_columns(encodings)]
    for k in range(1, turns):
        for n, held in enumerate(streams):
            held[k, 0] = send(held[k - 1, 0], onward)
            held[k - 1, 1] = send(held[k - 1, 0], across)
            before, place = streams[n - 1], (k - 1 if n else k - 2, 1)
            if place in before:
                held[k, 0], before[place] = lax.optimization_barrier((held[k, 0], before[place]))
    for n, held in enumerate(streams):
        held[turns - 1, 1] = send(held[turns - 1, 0], across) if n % 2 == 0 else send(held[turns - 2, 1], onward)
    late = [(turns - 1, 0), (turns - 2, 1), (turns - 1, 1)]
    order = [chunk for chunk in streams[0] if chunk not in late] + late
    there = len(order) - len(late)
    index, begun = early(
        order,
        turns,
        jnp.transpose(block_owner, (0, 2, 1)),
        block_row,
        [[held[chunk] for chunk in order[:there]] for held in streams],
    )
    picked = pick(index, begun, [[held[chunk] for chunk in late] for held in streams], there * rows)
    other = lax.ppermute(picked, "heads", [(0, 1), (1, 0)])
    first = own_scores(picked, w_key, queries, spans)
    values = own_values(picked, w_value, spans)
    return attend(other, w_key, w_value, queries, first, values, spans)


def exchange(encodings, owners, stored, capacity):
    wide_count = lax.axis_size("wide")
    requests = owners.shape[0]
    order = jnp.arange(requests, dtype=jnp.int32)
    earlier = (owners[:, None] == owners[None, :]) & (order[None, :] < order[:, None])
    rank = jnp.sum(earlier.astype(jnp.int32), axis=1)
    slot = owners * capacity + rank
    table = jnp.full((wide_count * capacity,), -1, jnp.int32).at[slot].set(stored)
    table = table.reshape(wide_count, capacity)
    asked = lax.all_to_all(table, "wide", split_axis=0, concat_axis=0, tiled=True)
    wanted = jnp.maximum(asked, 0)
    picked = encodings[wanted]
    returned = lax.all_to_all(picked, "wide", split_axis=0, concat_axis=0, tiled=True)
    return returned.reshape(wide_count * capacity, encodings.shape[1])[slot]


def exchanged_plan(queries, encodings, w_key, w_value, owners, stored, capacity):
    fetched = exchange(encodings, owners, stored, capacity)
    channels = w_key.shape[0]
    source = fetched.reshape(-1, channels)
    keys = jnp.dot(source, w_key, preferred_element_type=jnp.float32).astype(jnp.bfloat16)
    values = jnp.dot(source, w_value, preferred_element_type=jnp.float32).astype(jnp.bfloat16)
    span_count = queries.shape[0] // SPAN
    heads_local = w_key.shape[1] // HD
    keys = keys.reshape(span_count, -1, heads_local, HD)
    values = values.reshape(span_count, -1, heads_local, HD)
    query_part = queries.reshape(span_count, SPAN, heads_local, HD)
    scores = jnp.einsum(
        "cqhd,ckhd->chqk", query_part, keys, preferred_element_type=jnp.float32
    ) * HD ** (-0.5)
    probs = jax.nn.softmax(scores, axis=-1).astype(jnp.bfloat16)
    mixed = jnp.einsum("chqk,ckhd->cqhd", probs, values, preferred_element_type=jnp.float32)
    return mixed.astype(jnp.bfloat16).reshape(queries.shape)


def on_device(queries, encodings, w_key, w_value, block_owner, block_row):
    wide_count = lax.axis_size("wide")
    requests = block_row.size
    capacity = 2 * ((requests + wide_count - 1) // wide_count)
    if encodings.shape[0] <= 2 * capacity:
        return gathered_plan(queries, encodings, w_key, w_value, block_owner, block_row)
    return exchanged_plan(
        queries, encodings, w_key, w_value, block_owner.reshape(-1), block_row.reshape(-1), capacity
    )


def solution(mesh):
    placed = (
        P(("groups", "wide"), "heads"),
        P(("groups", "wide"), None),
        P(None, "heads"),
        P(None, "heads"),
        P(("groups", "wide"), None, None),
        P(("groups", "wide"), None),
    )
    return jax.shard_map(
        on_device,
        mesh=mesh,
        in_specs=placed,
        out_specs=P(("groups", "wide"), "heads"),
        check_vma=False,
    )
```

```python
import functools

import jax
import jax.numpy as jnp
from jax import lax
from jax.experimental import pallas as pl
from jax.experimental.pallas import tpu as pltpu
from jax.sharding import PartitionSpec as P

HD = 128
SPAN = 64
SIDE = 2
LIMIT = 24 * 1024 * 1024
EXPONENT = HD ** (-0.5) * 1.4426950408889634
VMEM = pl.BlockSpec(memory_space=pltpu.VMEM)


def params():
    return pltpu.CompilerParams(vmem_limit_bytes=LIMIT)


def half_kernel(enc_ref, out_ref, sem):
    width = out_ref.shape[1]
    start = pl.multiple_of(lax.axis_index("heads") * width, 128)
    copy = pltpu.make_async_copy(enc_ref.at[:, pl.ds(start, width)], out_ref, sem)
    copy.start()
    copy.wait()


def half_columns(encodings):
    rows, columns = encodings.shape
    width = columns // lax.axis_size("heads")
    return pl.pallas_call(
        half_kernel,
        out_shape=jax.ShapeDtypeStruct((rows, width), encodings.dtype),
        in_specs=[VMEM],
        out_specs=VMEM,
        scratch_shapes=[pltpu.SemaphoreType.DMA],
        compiler_params=params(),
    )(encodings)


def chosen_rows(index, sources, first):
    held = jnp.concatenate([ref[...] for ref in sources], axis=0)
    places = lax.broadcasted_iota(jnp.int32, (index.shape[0], held.shape[0]), 1) + first
    chosen = jnp.where(places == index, 1.0, 0.0).astype(held.dtype)
    return jnp.dot(chosen, held, preferred_element_type=jnp.float32)


def ring_order(turns):
    return [0] + list(range(1, turns, 2)) + list(range(turns - 2 + turns % 2, 0, -2))


def ring_place(line, turns):
    return jnp.where(line % 2 == 1, (line + 1) // 2, jnp.where(line == 0, 0, turns - line // 2))


def wanted_rows(orders, turns, rows, owner_ref, stored_ref):
    me = lax.axis_index("wide")
    core = lax.axis_index("heads")
    columns = []
    for c in range(stored_ref.shape[0]):
        owner, stored = owner_ref[c], stored_ref[c : c + 1, :]
        back = ring_place(me // SIDE, turns) - ring_place(owner // SIDE, turns)
        back = jnp.where(back < 0, back + turns, back)
        chunk = back * 2 + jnp.where(owner % SIDE == me % SIDE, 0, 1)
        place = jnp.zeros_like(stored)
        for n, choices in enumerate(zip(*orders)):
            here = jnp.where(core == 0, *[there * 2 + beside for there, beside in choices])
            place = jnp.where(chunk == here, n, place)
        place = place * rows + stored
        square = (place.shape[1], place.shape[1])
        own = lax.broadcasted_iota(jnp.int32, square, 0) == lax.broadcasted_iota(jnp.int32, square, 1)
        spread = jnp.where(own, jnp.broadcast_to(place.astype(jnp.float32), square), 0.0)
        columns.append(jnp.sum(spread, axis=1, keepdims=True))
    return jnp.concatenate(columns, axis=0).astype(jnp.int32)


def early_kernel(orders, turns, owner_ref, stored_ref, *refs):
    sources, index_ref, out_ref = refs[:-2], refs[-2], refs[-1]
    index_ref[...] = wanted_rows(orders, turns, sources[0].shape[0], owner_ref, stored_ref)
    out_ref[...] = chosen_rows(index_ref[...], sources, 0).astype(out_ref.dtype)


def early(orders, turns, owners, stored, sources):
    rows, width = sources[0].shape
    requests = stored.size
    return pl.pallas_call(
        functools.partial(early_kernel, orders, turns),
        out_shape=(
            jax.ShapeDtypeStruct((requests, 1), jnp.int32),
            jax.ShapeDtypeStruct((requests, width), sources[0].dtype),
        ),
        in_specs=[VMEM] * (2 + len(sources)),
        out_specs=(VMEM, VMEM),
        compiler_params=params(),
        cost_estimate=pl.CostEstimate(
            flops=2 * requests * width * rows * len(sources),
            bytes_accessed=2 * requests * width,
            transcendentals=0,
        ),
    )(owners, stored, *sources)


def pick_kernel(first, index_ref, begun_ref, last_ref, out_ref):
    picked = chosen_rows(index_ref[...], [last_ref], first)
    out_ref[...] = (picked + begun_ref[...].astype(jnp.float32)).astype(out_ref.dtype)


def pick(index, begun, last, first):
    return pl.pallas_call(
        functools.partial(pick_kernel, first),
        out_shape=jax.ShapeDtypeStruct(begun.shape, begun.dtype),
        in_specs=[VMEM] * 3,
        out_specs=VMEM,
        compiler_params=params(),
    )(index, begun, last)


def by_span(picked, spans, channels):
    per = picked.shape[0] // spans
    parts = []
    for c in range(spans):
        for t in range(picked.shape[1] // channels):
            parts.append(picked[c * per : (c + 1) * per, t * channels : (t + 1) * channels])
    return jnp.concatenate(parts, axis=0)


def head_places(spans, columns):
    heads = columns // HD
    return [(c, slice(h * HD, (h + 1) * HD), c * heads + h) for c in range(spans) for h in range(heads)]


def score(spans, source, wk_ref, query_ref, scores_ref):
    keys = jnp.dot(source, wk_ref[...], preferred_element_type=jnp.float32).astype(jnp.bfloat16)
    per = keys.shape[0] // spans
    for c, lanes, n in head_places(spans, keys.shape[1]):
        scores_ref[n] = lax.dot_general(
            query_ref[c * SPAN : (c + 1) * SPAN, lanes],
            keys[c * per : (c + 1) * per, lanes],
            (((1,), (1,)), ((), ())),
            preferred_element_type=jnp.float32,
        )


def score_kernel(spans, picked_ref, wk_ref, query_ref, scores_ref):
    score(spans, by_span(picked_ref[...], spans, wk_ref.shape[0]), wk_ref, query_ref, scores_ref)


def scores_shape(picked, queries, channels, spans):
    return spans * (queries.shape[1] // HD), SPAN, picked.size // channels // spans


def own_scores(picked, w_key, queries, spans):
    return pl.pallas_call(
        functools.partial(score_kernel, spans),
        out_shape=jax.ShapeDtypeStruct(scores_shape(picked, queries, w_key.shape[0], spans), jnp.float32),
        in_specs=[VMEM] * 3,
        out_specs=VMEM,
        compiler_params=params(),
    )(picked, w_key, queries)


def values_kernel(spans, picked_ref, wv_ref, values_ref):
    source = by_span(picked_ref[...], spans, wv_ref.shape[0])
    values_ref[...] = jnp.dot(source, wv_ref[...], preferred_element_type=jnp.float32).astype(values_ref.dtype)


def own_values(picked, w_value, spans):
    rows = picked.size // w_value.shape[0]
    return pl.pallas_call(
        functools.partial(values_kernel, spans),
        out_shape=jax.ShapeDtypeStruct((rows, w_value.shape[1]), picked.dtype),
        in_specs=[VMEM] * 2,
        out_specs=VMEM,
        compiler_params=params(),
    )(picked, w_value)


def attend_kernel(
    spans, other_ref, wk_ref, wv_ref, query_ref, first_ref, values_ref, out_ref, second_ref, probs_ref
):
    other = by_span(other_ref[...], spans, wk_ref.shape[0])
    score(spans, other, wk_ref, query_ref, second_ref)
    per = other.shape[0] // spans
    more = jnp.dot(other, wv_ref[...], preferred_element_type=jnp.float32).astype(jnp.bfloat16)
    places = head_places(spans, more.shape[1])
    for c, lanes, n in places:
        scores = jnp.concatenate([first_ref[n], second_ref[n]], axis=1)
        raised = jnp.exp2((scores - jnp.max(scores, axis=-1, keepdims=True)) * EXPONENT)
        probs_ref[n] = (raised * (1.0 / jnp.sum(raised, axis=-1, keepdims=True))).astype(jnp.bfloat16)
    for c, lanes, n in places:
        rows = slice(c * per, (c + 1) * per)
        values = jnp.concatenate([values_ref[rows, lanes], more[rows, lanes]], axis=0)
        mixed = jnp.dot(probs_ref[n], values, preferred_element_type=jnp.float32)
        out_ref[c * SPAN : (c + 1) * SPAN, lanes] = mixed.astype(out_ref.dtype)


def attend(other, w_key, w_value, queries, first, values, spans):
    each = scores_shape(other, queries, w_key.shape[0], spans)
    return pl.pallas_call(
        functools.partial(attend_kernel, spans),
        out_shape=jax.ShapeDtypeStruct(queries.shape, queries.dtype),
        in_specs=[VMEM] * 6,
        out_specs=VMEM,
        scratch_shapes=[pltpu.VMEM(each, jnp.float32), pltpu.VMEM(each[:2] + (2 * each[2],), jnp.bfloat16)],
        compiler_params=params(),
    )(other, w_key, w_value, queries, first, values)


def gathered_plan(queries, encodings, w_key, w_value, block_owner, block_row):
    wide_count = lax.axis_size("wide")
    turns = wide_count // SIDE
    rows = encodings.shape[0]
    spans = queries.shape[0] // SPAN
    line = ring_order(turns)
    onward = [
        (here * SIDE + x, there * SIDE + x) for here, there in zip(line, line[1:] + line[:1]) for x in range(SIDE)
    ]
    across = [(n, n + 1 if n % SIDE == 0 else n - 1) for n in range(wide_count)]

    def send(chunk, *steps):
        pairs = [(2 * here + core, 2 * there + core) for core, step in enumerate(steps) for here, there in step]
        return lax.ppermute(chunk, ("wide", "heads"), sorted(pairs))

    ahead = half_columns(encodings)
    sources, orders = [ahead], ([(0, 0)], [(0, 0)])
    for k in range(1, turns):
        one = send(ahead, onward, across)
        two = send(ahead, across, onward)
        ahead = jnp.where(lax.axis_index("heads") == 0, one, two)
        sources += [one, two]
        orders[0].extend([(k, 0), (k - 1, 1)])
        orders[1].extend([(k - 1, 1), (k, 0)])
    last = send(sources[-2], across, onward)
    for order in orders:
        order.append((turns - 1, 1))
    index, begun = early(orders, turns, jnp.transpose(block_owner, (0, 2, 1)), block_row, sources)
    picked = pick(index, begun, last, len(sources) * rows)
    other = lax.ppermute(picked, "heads", [(0, 1), (1, 0)])
    first = own_scores(picked, w_key, queries, spans)
    values = own_values(picked, w_value, spans)
    return attend(other, w_key, w_value, queries, first, values, spans)


def exchange(encodings, owners, stored, capacity):
    wide_count = lax.axis_size("wide")
    requests = owners.shape[0]
    order = jnp.arange(requests, dtype=jnp.int32)
    earlier = (owners[:, None] == owners[None, :]) & (order[None, :] < order[:, None])
    rank = jnp.sum(earlier.astype(jnp.int32), axis=1)
    slot = owners * capacity + rank
    table = jnp.full((wide_count * capacity,), -1, jnp.int32).at[slot].set(stored)
    table = table.reshape(wide_count, capacity)
    asked = lax.all_to_all(table, "wide", split_axis=0, concat_axis=0, tiled=True)
    wanted = jnp.maximum(asked, 0)
    picked = encodings[wanted]
    returned = lax.all_to_all(picked, "wide", split_axis=0, concat_axis=0, tiled=True)
    return returned.reshape(wide_count * capacity, encodings.shape[1])[slot]


def exchanged_plan(queries, encodings, w_key, w_value, owners, stored, capacity):
    fetched = exchange(encodings, owners, stored, capacity)
    channels = w_key.shape[0]
    source = fetched.reshape(-1, channels)
    keys = jnp.dot(source, w_key, preferred_element_type=jnp.float32).astype(jnp.bfloat16)
    values = jnp.dot(source, w_value, preferred_element_type=jnp.float32).astype(jnp.bfloat16)
    span_count = queries.shape[0] // SPAN
    heads_local = w_key.shape[1] // HD
    keys = keys.reshape(span_count, -1, heads_local, HD)
    values = values.reshape(span_count, -1, heads_local, HD)
    query_part = queries.reshape(span_count, SPAN, heads_local, HD)
    scores = jnp.einsum(
        "cqhd,ckhd->chqk", query_part, keys, preferred_element_type=jnp.float32
    ) * HD ** (-0.5)
    probs = jax.nn.softmax(scores, axis=-1).astype(jnp.bfloat16)
    mixed = jnp.einsum("chqk,ckhd->cqhd", probs, values, preferred_element_type=jnp.float32)
    return mixed.astype(jnp.bfloat16).reshape(queries.shape)


def on_device(queries, encodings, w_key, w_value, block_owner, block_row):
    wide_count = lax.axis_size("wide")
    requests = block_row.size
    capacity = 2 * ((requests + wide_count - 1) // wide_count)
    if encodings.shape[0] <= 2 * capacity:
        return gathered_plan(queries, encodings, w_key, w_value, block_owner, block_row)
    return exchanged_plan(
        queries, encodings, w_key, w_value, block_owner.reshape(-1), block_row.reshape(-1), capacity
    )


def solution(mesh):
    placed = (
        P(("groups", "wide"), "heads"),
        P(("groups", "wide"), None),
        P(None, "heads"),
        P(None, "heads"),
        P(("groups", "wide"), None, None),
        P(("groups", "wide"), None),
    )
    return jax.shard_map(
        on_device,
        mesh=mesh,
        in_specs=placed,
        out_specs=P(("groups", "wide"), "heads"),
        check_vma=False,
    )
```

```python
import functools

import jax
import jax.numpy as jnp
from jax import lax
from jax.experimental import pallas as pl
from jax.experimental.pallas import tpu as pltpu
from jax.sharding import PartitionSpec as P

HD = 128
SPAN = 64
SIDE = 2
LIMIT = 24 * 1024 * 1024
STREAMS = 2
EXPONENT = HD ** (-0.5) * 1.4426950408889634
VMEM = pl.BlockSpec(memory_space=pltpu.VMEM)


def params():
    return pltpu.CompilerParams(vmem_limit_bytes=LIMIT)


def half_kernel(enc_ref, *refs):
    outs, sems = refs[:-1], refs[-1]
    first = lax.axis_index("heads") * outs[-1].shape[1]
    copies = []
    for n, out in enumerate(outs):
        width = out.shape[1]
        start = first + (n * width if n < STREAMS else 0)
        copies.append(pltpu.make_async_copy(enc_ref.at[:, pl.ds(pl.multiple_of(start, 128), width)], out, sems.at[n]))
    for copy in copies:
        copy.start()
    for copy in copies:
        copy.wait()


def half_columns(encodings):
    rows, columns = encodings.shape
    whole = columns // lax.axis_size("heads")
    widths = [whole // STREAMS] * STREAMS + [whole]
    return pl.pallas_call(
        half_kernel,
        out_shape=[jax.ShapeDtypeStruct((rows, width), encodings.dtype) for width in widths],
        in_specs=[VMEM],
        out_specs=[VMEM] * len(widths),
        scratch_shapes=[pltpu.SemaphoreType.DMA((len(widths),))],
        compiler_params=params(),
    )(encodings)


def chosen_rows(index, chunks, refs, first):
    rows = refs[0].shape[0]
    width = min(ref.shape[1] for ref in refs)
    places = lax.broadcasted_iota(jnp.int32, (index.shape[0], len(chunks) * rows), 1) + first
    chosen = jnp.where(places == index, 1.0, 0.0).astype(refs[0].dtype)
    starts = [sum(chunks[:n]) for n in range(len(chunks))]
    parts = []
    for n in range(STREAMS):
        held = [
            refs[at + n][...] if arrays > 1 else refs[at][:, n * width : (n + 1) * width]
            for at, arrays in zip(starts, chunks)
        ]
        parts.append(jnp.dot(chosen, jnp.concatenate(held, axis=0), preferred_element_type=jnp.float32))
    return jnp.concatenate(parts, axis=1)


def ring_order(turns):
    return [0] + list(range(1, turns, 2)) + list(range(turns - 2 + turns % 2, 0, -2))


def ring_place(line, turns):
    return jnp.where(line % 2 == 1, (line + 1) // 2, jnp.where(line == 0, 0, turns - line // 2))


def wanted_rows(order, turns, rows, owner_ref, stored_ref):
    me = lax.axis_index("wide")
    columns = []
    for c in range(stored_ref.shape[0]):
        owner, stored = owner_ref[c], stored_ref[c : c + 1, :]
        back = ring_place(me // SIDE, turns) - ring_place(owner // SIDE, turns)
        back = jnp.where(back < 0, back + turns, back)
        beside = jnp.where(owner % SIDE == me % SIDE, 0, 1)
        place = jnp.zeros_like(stored)
        for n, chunk in enumerate(order):
            place = jnp.where(back * 2 + beside == chunk[0] * 2 + chunk[1], n, place)
        place = place * rows + stored
        square = (place.shape[1], place.shape[1])
        own = lax.broadcasted_iota(jnp.int32, square, 0) == lax.broadcasted_iota(jnp.int32, square, 1)
        spread = jnp.where(own, jnp.broadcast_to(place.astype(jnp.float32), square), 0.0)
        columns.append(jnp.sum(spread, axis=1, keepdims=True))
    return jnp.concatenate(columns, axis=0).astype(jnp.int32)


def early_kernel(order, turns, chunks, owner_ref, stored_ref, *refs):
    sources, index_ref, out_ref = refs[:-2], refs[-2], refs[-1]
    index_ref[...] = wanted_rows(order, turns, sources[0].shape[0], owner_ref, stored_ref)
    out_ref[...] = chosen_rows(index_ref[...], chunks, sources, 0).astype(out_ref.dtype)


def early(order, turns, owners, stored, sources, width):
    rows = sources[0][0].shape[0]
    requests = stored.size
    arrays = [array for chunk in sources for array in chunk]
    return pl.pallas_call(
        functools.partial(early_kernel, order, turns, [len(chunk) for chunk in sources]),
        out_shape=(
            jax.ShapeDtypeStruct((requests, 1), jnp.int32),
            jax.ShapeDtypeStruct((requests, width), arrays[0].dtype),
        ),
        in_specs=[VMEM] * (2 + len(arrays)),
        out_specs=(VMEM, VMEM),
        compiler_params=params(),
        cost_estimate=pl.CostEstimate(
            flops=2 * requests * width * rows * len(sources),
            bytes_accessed=2 * requests * width,
            transcendentals=0,
        ),
    )(owners, stored, *arrays)


def pick_kernel(chunks, first, index_ref, begun_ref, *refs):
    picked = chosen_rows(index_ref[...], chunks, refs[:-1], first)
    refs[-1][...] = (picked + begun_ref[...].astype(jnp.float32)).astype(begun_ref.dtype)


def pick(index, begun, sources, first):
    arrays = [array for chunk in sources for array in chunk]
    return pl.pallas_call(
        functools.partial(pick_kernel, [len(chunk) for chunk in sources], first),
        out_shape=jax.ShapeDtypeStruct(begun.shape, begun.dtype),
        in_specs=[VMEM] * (2 + len(arrays)),
        out_specs=VMEM,
        compiler_params=params(),
    )(index, begun, *arrays)


def by_span(picked, spans, channels):
    per = picked.shape[0] // spans
    parts = []
    for c in range(spans):
        for t in range(picked.shape[1] // channels):
            parts.append(picked[c * per : (c + 1) * per, t * channels : (t + 1) * channels])
    return jnp.concatenate(parts, axis=0)


def head_places(spans, columns):
    heads = columns // HD
    return [(c, slice(h * HD, (h + 1) * HD), c * heads + h) for c in range(spans) for h in range(heads)]


def score(spans, source, wk_ref, query_ref, scores_ref):
    keys = jnp.dot(source, wk_ref[...], preferred_element_type=jnp.float32).astype(jnp.bfloat16)
    per = keys.shape[0] // spans
    for c, lanes, n in head_places(spans, keys.shape[1]):
        scores_ref[n] = lax.dot_general(
            query_ref[c * SPAN : (c + 1) * SPAN, lanes],
            keys[c * per : (c + 1) * per, lanes],
            (((1,), (1,)), ((), ())),
            preferred_element_type=jnp.float32,
        )


def score_kernel(spans, picked_ref, wk_ref, query_ref, scores_ref):
    score(spans, by_span(picked_ref[...], spans, wk_ref.shape[0]), wk_ref, query_ref, scores_ref)


def scores_shape(picked, queries, channels, spans):
    return spans * (queries.shape[1] // HD), SPAN, picked.size // channels // spans


def own_scores(picked, w_key, queries, spans):
    return pl.pallas_call(
        functools.partial(score_kernel, spans),
        out_shape=jax.ShapeDtypeStruct(scores_shape(picked, queries, w_key.shape[0], spans), jnp.float32),
        in_specs=[VMEM] * 3,
        out_specs=VMEM,
        compiler_params=params(),
    )(picked, w_key, queries)


def values_kernel(spans, picked_ref, wv_ref, values_ref):
    source = by_span(picked_ref[...], spans, wv_ref.shape[0])
    values_ref[...] = jnp.dot(source, wv_ref[...], preferred_element_type=jnp.float32).astype(values_ref.dtype)


def own_values(picked, w_value, spans):
    rows = picked.size // w_value.shape[0]
    return pl.pallas_call(
        functools.partial(values_kernel, spans),
        out_shape=jax.ShapeDtypeStruct((rows, w_value.shape[1]), picked.dtype),
        in_specs=[VMEM] * 2,
        out_specs=VMEM,
        compiler_params=params(),
    )(picked, w_value)


def attend_kernel(
    spans, other_ref, wk_ref, wv_ref, query_ref, first_ref, values_ref, out_ref, second_ref
):
    other = by_span(other_ref[...], spans, wk_ref.shape[0])
    per = other.shape[0] // spans
    columns = wk_ref.shape[1]
    heads = columns // HD
    group = 2 if heads % 2 == 0 else 1
    score(spans, other, wk_ref, query_ref, second_ref)
    for at in range(0, heads, group):
        lanes = slice(at * HD, (at + group) * HD)
        more = jnp.dot(other, wv_ref[:, lanes], preferred_element_type=jnp.float32).astype(jnp.bfloat16)
        for c in range(spans):
            rows = slice(c * per, (c + 1) * per)
            for h in range(group):
                n = c * heads + at + h
                scores = jnp.concatenate([first_ref[n], second_ref[n]], axis=1)
                raised = jnp.exp2((scores - jnp.max(scores, axis=-1, keepdims=True)) * EXPONENT)
                probs = (raised * (1.0 / jnp.sum(raised, axis=-1, keepdims=True))).astype(jnp.bfloat16)
                head = slice((at + h) * HD, (at + h + 1) * HD)
                values = jnp.concatenate([values_ref[rows, head], more[rows, h * HD : (h + 1) * HD]], axis=0)
                mixed = jnp.dot(probs, values, preferred_element_type=jnp.float32)
                out_ref[c * SPAN : (c + 1) * SPAN, head] = mixed.astype(out_ref.dtype)


def attend(other, w_key, w_value, queries, first, values, spans):
    each = scores_shape(other, queries, w_key.shape[0], spans)
    return pl.pallas_call(
        functools.partial(attend_kernel, spans),
        out_shape=jax.ShapeDtypeStruct(queries.shape, queries.dtype),
        in_specs=[VMEM] * 6,
        out_specs=VMEM,
        scratch_shapes=[pltpu.VMEM(each, jnp.float32)],
        compiler_params=params(),
    )(other, w_key, w_value, queries, first, values)


def send(chunk, pairs):
    return lax.ppermute(chunk, "wide", pairs)


def gathered_plan(queries, encodings, w_key, w_value, block_owner, block_row):
    wide_count = lax.axis_size("wide")
    turns = wide_count // SIDE
    rows = encodings.shape[0]
    spans = queries.shape[0] // SPAN
    line = ring_order(turns)
    onward = [
        (here * SIDE + x, there * SIDE + x) for here, there in zip(line, line[1:] + line[:1]) for x in range(SIDE)
    ]
    across = [(n, n + 1 if n % SIDE == 0 else n - 1) for n in range(wide_count)]
    *pieces, whole = half_columns(encodings)
    held = {(0, 0): pieces}
    for k in range(1, turns):
        behind = held[k - 1, 0]
        steps = [send(piece, onward) for piece in behind]
        joined = whole if k == 1 else jnp.concatenate(behind, axis=1)
        held[k - 1, 1] = [send(joined, across)]
        if k > 1:
            steps[0], held[k - 2, 1][0] = lax.optimization_barrier((steps[0], held[k - 2, 1][0]))
        held[k, 0] = steps
    held[turns - 1, 1] = [send(piece, across) for piece in held[turns - 1, 0]]
    late = [(turns - 1, 0), (turns - 2, 1), (turns - 1, 1)]
    order = [chunk for chunk in held if chunk not in late] + late
    there = len(order) - len(late)
    index, begun = early(
        order,
        turns,
        jnp.transpose(block_owner, (0, 2, 1)),
        block_row,
        [held[chunk] for chunk in order[:there]],
        whole.shape[1],
    )
    picked = pick(index, begun, [held[chunk] for chunk in late], there * rows)
    other = lax.ppermute(picked, "heads", [(0, 1), (1, 0)])
    first = own_scores(picked, w_key, queries, spans)
    values = own_values(picked, w_value, spans)
    return attend(other, w_key, w_value, queries, first, values, spans)


def exchange(encodings, owners, stored, capacity):
    wide_count = lax.axis_size("wide")
    requests = owners.shape[0]
    order = jnp.arange(requests, dtype=jnp.int32)
    earlier = (owners[:, None] == owners[None, :]) & (order[None, :] < order[:, None])
    rank = jnp.sum(earlier.astype(jnp.int32), axis=1)
    slot = owners * capacity + rank
    table = jnp.full((wide_count * capacity,), -1, jnp.int32).at[slot].set(stored)
    table = table.reshape(wide_count, capacity)
    asked = lax.all_to_all(table, "wide", split_axis=0, concat_axis=0, tiled=True)
    wanted = jnp.maximum(asked, 0)
    picked = encodings[wanted]
    returned = lax.all_to_all(picked, "wide", split_axis=0, concat_axis=0, tiled=True)
    return returned.reshape(wide_count * capacity, encodings.shape[1])[slot]


def exchanged_plan(queries, encodings, w_key, w_value, owners, stored, capacity):
    fetched = exchange(encodings, owners, stored, capacity)
    channels = w_key.shape[0]
    source = fetched.reshape(-1, channels)
    keys = jnp.dot(source, w_key, preferred_element_type=jnp.float32).astype(jnp.bfloat16)
    values = jnp.dot(source, w_value, preferred_element_type=jnp.float32).astype(jnp.bfloat16)
    span_count = queries.shape[0] // SPAN
    heads_local = w_key.shape[1] // HD
    keys = keys.reshape(span_count, -1, heads_local, HD)
    values = values.reshape(span_count, -1, heads_local, HD)
    query_part = queries.reshape(span_count, SPAN, heads_local, HD)
    scores = jnp.einsum(
        "cqhd,ckhd->chqk", query_part, keys, preferred_element_type=jnp.float32
    ) * HD ** (-0.5)
    probs = jax.nn.softmax(scores, axis=-1).astype(jnp.bfloat16)
    mixed = jnp.einsum("chqk,ckhd->cqhd", probs, values, preferred_element_type=jnp.float32)
    return mixed.astype(jnp.bfloat16).reshape(queries.shape)


def on_device(queries, encodings, w_key, w_value, block_owner, block_row):
    wide_count = lax.axis_size("wide")
    requests = block_row.size
    capacity = 2 * ((requests + wide_count - 1) // wide_count)
    if encodings.shape[0] <= 2 * capacity:
        return gathered_plan(queries, encodings, w_key, w_value, block_owner, block_row)
    return exchanged_plan(
        queries, encodings, w_key, w_value, block_owner.reshape(-1), block_row.reshape(-1), capacity
    )


def solution(mesh):
    placed = (
        P(("groups", "wide"), "heads"),
        P(("groups", "wide"), None),
        P(None, "heads"),
        P(None, "heads"),
        P(("groups", "wide"), None, None),
        P(("groups", "wide"), None),
    )
    return jax.shard_map(
        on_device,
        mesh=mesh,
        in_specs=placed,
        out_specs=P(("groups", "wide"), "heads"),
        check_vma=False,
    )
```

```python
import functools

import jax
import jax.numpy as jnp
from jax import lax
from jax.experimental import pallas as pl
from jax.experimental.pallas import tpu as pltpu
from jax.sharding import PartitionSpec as P

HD = 128
SPAN = 64
SIDE = 2
LIMIT = 24 * 1024 * 1024
STREAMS = 2
EXPONENT = HD ** (-0.5) * 1.4426950408889634
VMEM = pl.BlockSpec(memory_space=pltpu.VMEM)


def params():
    return pltpu.CompilerParams(vmem_limit_bytes=LIMIT)


def half_kernel(enc_ref, *refs):
    outs, sems = refs[:-1], refs[-1]
    first = lax.axis_index("heads") * outs[-1].shape[1]
    copies = []
    for n, out in enumerate(outs):
        width = out.shape[1]
        start = first + (n * width if n < STREAMS else 0)
        copies.append(pltpu.make_async_copy(enc_ref.at[:, pl.ds(pl.multiple_of(start, 128), width)], out, sems.at[n]))
    for copy in copies:
        copy.start()
    for copy in copies:
        copy.wait()


def half_columns(encodings):
    rows, columns = encodings.shape
    whole = columns // lax.axis_size("heads")
    widths = [whole // STREAMS] * STREAMS + [whole]
    return pl.pallas_call(
        half_kernel,
        out_shape=[jax.ShapeDtypeStruct((rows, width), encodings.dtype) for width in widths],
        in_specs=[VMEM],
        out_specs=[VMEM] * len(widths),
        scratch_shapes=[pltpu.SemaphoreType.DMA((len(widths),))],
        compiler_params=params(),
    )(encodings)


def chosen_rows(index, chunks, refs, first):
    rows = refs[0].shape[0]
    width = min(ref.shape[1] for ref in refs)
    places = lax.broadcasted_iota(jnp.int32, (index.shape[0], len(chunks) * rows), 1) + first
    chosen = jnp.where(places == index, 1.0, 0.0).astype(refs[0].dtype)
    starts = [sum(chunks[:n]) for n in range(len(chunks))]
    parts = []
    for n in range(STREAMS):
        held = [
            refs[at + n][...] if arrays > 1 else refs[at][:, n * width : (n + 1) * width]
            for at, arrays in zip(starts, chunks)
        ]
        parts.append(jnp.dot(chosen, jnp.concatenate(held, axis=0), preferred_element_type=jnp.float32))
    return jnp.concatenate(parts, axis=1)


def ring_order(turns):
    return [0] + list(range(1, turns, 2)) + list(range(turns - 2 + turns % 2, 0, -2))


def ring_place(line, turns):
    return jnp.where(line % 2 == 1, (line + 1) // 2, jnp.where(line == 0, 0, turns - line // 2))


def wanted_rows(order, turns, rows, owner_ref, stored_ref):
    me = lax.axis_index("wide")
    columns = []
    for c in range(stored_ref.shape[0]):
        owner, stored = owner_ref[c], stored_ref[c : c + 1, :]
        back = ring_place(me // SIDE, turns) - ring_place(owner // SIDE, turns)
        back = jnp.where(back < 0, back + turns, back)
        beside = jnp.where(owner % SIDE == me % SIDE, 0, 1)
        place = jnp.zeros_like(stored)
        for n, chunk in enumerate(order):
            place = jnp.where(back * 2 + beside == chunk[0] * 2 + chunk[1], n, place)
        place = place * rows + stored
        square = (place.shape[1], place.shape[1])
        own = lax.broadcasted_iota(jnp.int32, square, 0) == lax.broadcasted_iota(jnp.int32, square, 1)
        spread = jnp.where(own, jnp.broadcast_to(place.astype(jnp.float32), square), 0.0)
        columns.append(jnp.sum(spread, axis=1, keepdims=True))
    return jnp.concatenate(columns, axis=0).astype(jnp.int32)


def places_kernel(order, turns, owner_ref, stored_ref, piece_ref, index_ref, piece_out, sem):
    copy = pltpu.make_async_copy(piece_ref, piece_out, sem)
    copy.start()
    index_ref[...] = wanted_rows(order, turns, piece_ref.shape[0], owner_ref, stored_ref)
    copy.wait()


def places(order, turns, owners, stored, piece):
    return pl.pallas_call(
        functools.partial(places_kernel, order, turns),
        out_shape=(
            jax.ShapeDtypeStruct((stored.size, 1), jnp.int32),
            jax.ShapeDtypeStruct(piece.shape, piece.dtype),
        ),
        in_specs=[VMEM] * 3,
        out_specs=(VMEM, VMEM),
        scratch_shapes=[pltpu.SemaphoreType.DMA],
        compiler_params=params(),
    )(owners, stored, piece)


def early_kernel(chunks, index_ref, *refs):
    refs[-1][...] = chosen_rows(index_ref[...], chunks, refs[:-1], 0).astype(refs[-1].dtype)


def early(index, sources, width):
    rows = sources[0][0].shape[0]
    requests = index.shape[0]
    arrays = [array for chunk in sources for array in chunk]
    return pl.pallas_call(
        functools.partial(early_kernel, [len(chunk) for chunk in sources]),
        out_shape=jax.ShapeDtypeStruct((requests, width), arrays[0].dtype),
        in_specs=[VMEM] * (1 + len(arrays)),
        out_specs=VMEM,
        compiler_params=params(),
        cost_estimate=pl.CostEstimate(
            flops=2 * requests * width * rows * len(sources),
            bytes_accessed=2 * requests * width,
            transcendentals=0,
        ),
    )(index, *arrays)


def pick_kernel(chunks, first, index_ref, begun_ref, *refs):
    picked = chosen_rows(index_ref[...], chunks, refs[:-1], first)
    refs[-1][...] = (picked + begun_ref[...].astype(jnp.float32)).astype(begun_ref.dtype)


def pick(index, begun, sources, first):
    arrays = [array for chunk in sources for array in chunk]
    return pl.pallas_call(
        functools.partial(pick_kernel, [len(chunk) for chunk in sources], first),
        out_shape=jax.ShapeDtypeStruct(begun.shape, begun.dtype),
        in_specs=[VMEM] * (2 + len(arrays)),
        out_specs=VMEM,
        compiler_params=params(),
    )(index, begun, *arrays)


def by_span(picked, spans, channels):
    per = picked.shape[0] // spans
    parts = []
    for c in range(spans):
        for t in range(picked.shape[1] // channels):
            parts.append(picked[c * per : (c + 1) * per, t * channels : (t + 1) * channels])
    return jnp.concatenate(parts, axis=0)


def head_places(spans, columns):
    heads = columns // HD
    return [(c, slice(h * HD, (h + 1) * HD), c * heads + h) for c in range(spans) for h in range(heads)]


def score(spans, source, wk_ref, query_ref, scores_ref):
    keys = jnp.dot(source, wk_ref[...], preferred_element_type=jnp.float32).astype(jnp.bfloat16)
    per = keys.shape[0] // spans
    for c, lanes, n in head_places(spans, keys.shape[1]):
        scores_ref[n] = lax.dot_general(
            query_ref[c * SPAN : (c + 1) * SPAN, lanes],
            keys[c * per : (c + 1) * per, lanes],
            (((1,), (1,)), ((), ())),
            preferred_element_type=jnp.float32,
        )


def score_kernel(spans, picked_ref, wk_ref, query_ref, scores_ref):
    score(spans, by_span(picked_ref[...], spans, wk_ref.shape[0]), wk_ref, query_ref, scores_ref)


def scores_shape(picked, queries, channels, spans):
    return spans * (queries.shape[1] // HD), SPAN, picked.size // channels // spans


def own_scores(picked, w_key, queries, spans):
    return pl.pallas_call(
        functools.partial(score_kernel, spans),
        out_shape=jax.ShapeDtypeStruct(scores_shape(picked, queries, w_key.shape[0], spans), jnp.float32),
        in_specs=[VMEM] * 3,
        out_specs=VMEM,
        compiler_params=params(),
    )(picked, w_key, queries)


def values_kernel(spans, picked_ref, wv_ref, values_ref):
    source = by_span(picked_ref[...], spans, wv_ref.shape[0])
    values_ref[...] = jnp.dot(source, wv_ref[...], preferred_element_type=jnp.float32).astype(values_ref.dtype)


def own_values(picked, w_value, spans):
    rows = picked.size // w_value.shape[0]
    return pl.pallas_call(
        functools.partial(values_kernel, spans),
        out_shape=jax.ShapeDtypeStruct((rows, w_value.shape[1]), picked.dtype),
        in_specs=[VMEM] * 2,
        out_specs=VMEM,
        compiler_params=params(),
    )(picked, w_value)


def attend_kernel(
    spans, other_ref, wk_ref, wv_ref, query_ref, first_ref, values_ref, out_ref, second_ref, probs_ref
):
    other = by_span(other_ref[...], spans, wk_ref.shape[0])
    score(spans, other, wk_ref, query_ref, second_ref)
    per = other.shape[0] // spans
    more = jnp.dot(other, wv_ref[...], preferred_element_type=jnp.float32).astype(jnp.bfloat16)
    places = head_places(spans, more.shape[1])
    for c, lanes, n in places:
        scores = jnp.concatenate([first_ref[n], second_ref[n]], axis=1)
        raised = jnp.exp2((scores - jnp.max(scores, axis=-1, keepdims=True)) * EXPONENT)
        probs_ref[n] = (raised * (1.0 / jnp.sum(raised, axis=-1, keepdims=True))).astype(jnp.bfloat16)
    for c, lanes, n in places:
        rows = slice(c * per, (c + 1) * per)
        values = jnp.concatenate([values_ref[rows, lanes], more[rows, lanes]], axis=0)
        mixed = jnp.dot(probs_ref[n], values, preferred_element_type=jnp.float32)
        out_ref[c * SPAN : (c + 1) * SPAN, lanes] = mixed.astype(out_ref.dtype)


def attend(other, w_key, w_value, queries, first, values, spans):
    each = scores_shape(other, queries, w_key.shape[0], spans)
    return pl.pallas_call(
        functools.partial(attend_kernel, spans),
        out_shape=jax.ShapeDtypeStruct(queries.shape, queries.dtype),
        in_specs=[VMEM] * 6,
        out_specs=VMEM,
        scratch_shapes=[pltpu.VMEM(each, jnp.float32), pltpu.VMEM(each[:2] + (2 * each[2],), jnp.bfloat16)],
        compiler_params=params(),
    )(other, w_key, w_value, queries, first, values)


def send(chunk, pairs):
    return lax.ppermute(chunk, "wide", pairs)


def gathered_plan(queries, encodings, w_key, w_value, block_owner, block_row):
    wide_count = lax.axis_size("wide")
    turns = wide_count // SIDE
    rows = encodings.shape[0]
    spans = queries.shape[0] // SPAN
    line = ring_order(turns)
    onward = [
        (here * SIDE + x, there * SIDE + x) for here, there in zip(line, line[1:] + line[:1]) for x in range(SIDE)
    ]
    across = [(n, n + 1 if n % SIDE == 0 else n - 1) for n in range(wide_count)]
    *pieces, whole = half_columns(encodings)
    order = [(0, 0)]
    for k in range(1, turns):
        order += [(k, 0), (k - 1, 1)]
    order.append((turns - 1, 1))
    index, pieces[-1] = places(order, turns, jnp.transpose(block_owner, (0, 2, 1)), block_row, pieces[-1])
    held = {(0, 0): pieces}
    for k in range(1, turns):
        behind = held[k - 1, 0]
        steps = [send(piece, onward) for piece in behind]
        joined = whole if k == 1 else jnp.concatenate(behind, axis=1)
        held[k - 1, 1] = [send(joined, across)]
        if k > 1:
            steps[0], held[k - 2, 1][0] = lax.optimization_barrier((steps[0], held[k - 2, 1][0]))
        held[k, 0] = steps
    held[turns - 1, 1] = [send(piece, across) for piece in held[turns - 1, 0]]
    late = 3
    sources = [held[chunk] for chunk in order]
    begun = early(index, sources[:-late], whole.shape[1])
    picked = pick(index, begun, sources[-late:], (len(order) - late) * rows)
    other = lax.ppermute(picked, "heads", [(0, 1), (1, 0)])
    first = own_scores(picked, w_key, queries, spans)
    values = own_values(picked, w_value, spans)
    return attend(other, w_key, w_value, queries, first, values, spans)


def exchange(encodings, owners, stored, capacity):
    wide_count = lax.axis_size("wide")
    requests = owners.shape[0]
    order = jnp.arange(requests, dtype=jnp.int32)
    earlier = (owners[:, None] == owners[None, :]) & (order[None, :] < order[:, None])
    rank = jnp.sum(earlier.astype(jnp.int32), axis=1)
    slot = owners * capacity + rank
    table = jnp.full((wide_count * capacity,), -1, jnp.int32).at[slot].set(stored)
    table = table.reshape(wide_count, capacity)
    asked = lax.all_to_all(table, "wide", split_axis=0, concat_axis=0, tiled=True)
    wanted = jnp.maximum(asked, 0)
    picked = encodings[wanted]
    returned = lax.all_to_all(picked, "wide", split_axis=0, concat_axis=0, tiled=True)
    return returned.reshape(wide_count * capacity, encodings.shape[1])[slot]


def exchanged_plan(queries, encodings, w_key, w_value, owners, stored, capacity):
    fetched = exchange(encodings, owners, stored, capacity)
    channels = w_key.shape[0]
    source = fetched.reshape(-1, channels)
    keys = jnp.dot(source, w_key, preferred_element_type=jnp.float32).astype(jnp.bfloat16)
    values = jnp.dot(source, w_value, preferred_element_type=jnp.float32).astype(jnp.bfloat16)
    span_count = queries.shape[0] // SPAN
    heads_local = w_key.shape[1] // HD
    keys = keys.reshape(span_count, -1, heads_local, HD)
    values = values.reshape(span_count, -1, heads_local, HD)
    query_part = queries.reshape(span_count, SPAN, heads_local, HD)
    scores = jnp.einsum(
        "cqhd,ckhd->chqk", query_part, keys, preferred_element_type=jnp.float32
    ) * HD ** (-0.5)
    probs = jax.nn.softmax(scores, axis=-1).astype(jnp.bfloat16)
    mixed = jnp.einsum("chqk,ckhd->cqhd", probs, values, preferred_element_type=jnp.float32)
    return mixed.astype(jnp.bfloat16).reshape(queries.shape)


def on_device(queries, encodings, w_key, w_value, block_owner, block_row):
    wide_count = lax.axis_size("wide")
    requests = block_row.size
    capacity = 2 * ((requests + wide_count - 1) // wide_count)
    if encodings.shape[0] <= 2 * capacity:
        return gathered_plan(queries, encodings, w_key, w_value, block_owner, block_row)
    return exchanged_plan(
        queries, encodings, w_key, w_value, block_owner.reshape(-1), block_row.reshape(-1), capacity
    )


def solution(mesh):
    placed = (
        P(("groups", "wide"), "heads"),
        P(("groups", "wide"), None),
        P(None, "heads"),
        P(None, "heads"),
        P(("groups", "wide"), None, None),
        P(("groups", "wide"), None),
    )
    return jax.shard_map(
        on_device,
        mesh=mesh,
        in_specs=placed,
        out_specs=P(("groups", "wide"), "heads"),
        check_vma=False,
    )
```

```python
import functools

import jax
import jax.numpy as jnp
from jax import lax
from jax.experimental import pallas as pl
from jax.experimental.pallas import tpu as pltpu
from jax.sharding import PartitionSpec as P

HD = 128
SPAN = 64
SIDE = 2
LIMIT = 24 * 1024 * 1024
STREAMS = 2
EXPONENT = HD ** (-0.5) * 1.4426950408889634
VMEM = pl.BlockSpec(memory_space=pltpu.VMEM)


def params():
    return pltpu.CompilerParams(vmem_limit_bytes=LIMIT)


def half_kernel(enc_ref, *refs):
    outs, sems = refs[:-1], refs[-1]
    first = lax.axis_index("heads") * outs[-1].shape[1]
    copies = []
    for n, out in enumerate(outs):
        width = out.shape[1]
        start = first + (n * width if n < STREAMS else 0)
        copies.append(pltpu.make_async_copy(enc_ref.at[:, pl.ds(pl.multiple_of(start, 128), width)], out, sems.at[n]))
    for copy in copies:
        copy.start()
    for copy in copies:
        copy.wait()


def half_columns(encodings):
    rows, columns = encodings.shape
    whole = columns // lax.axis_size("heads")
    widths = [whole // STREAMS] * STREAMS + [whole]
    return pl.pallas_call(
        half_kernel,
        out_shape=[jax.ShapeDtypeStruct((rows, width), encodings.dtype) for width in widths],
        in_specs=[VMEM],
        out_specs=[VMEM] * len(widths),
        scratch_shapes=[pltpu.SemaphoreType.DMA((len(widths),))],
        compiler_params=params(),
    )(encodings)


def chosen_rows(index, chunks, refs, first):
    rows = refs[0].shape[0]
    width = min(ref.shape[1] for ref in refs)
    places = lax.broadcasted_iota(jnp.int32, (index.shape[0], len(chunks) * rows), 1) + first
    chosen = jnp.where(places == index, 1.0, 0.0).astype(refs[0].dtype)
    starts = [sum(chunks[:n]) for n in range(len(chunks))]
    parts = []
    for n in range(STREAMS):
        held = [
            refs[at + n][...] if arrays > 1 else refs[at][:, n * width : (n + 1) * width]
            for at, arrays in zip(starts, chunks)
        ]
        parts.append(jnp.dot(chosen, jnp.concatenate(held, axis=0), preferred_element_type=jnp.float32))
    return jnp.concatenate(parts, axis=1)


def ring_order(turns):
    return [0] + list(range(1, turns, 2)) + list(range(turns - 2 + turns % 2, 0, -2))


def ring_place(line, turns):
    return jnp.where(line % 2 == 1, (line + 1) // 2, jnp.where(line == 0, 0, turns - line // 2))


def wanted_rows(order, turns, rows, owner_ref, stored_ref):
    me = lax.axis_index("wide")
    columns = []
    for c in range(stored_ref.shape[0]):
        owner, stored = owner_ref[c], stored_ref[c : c + 1, :]
        back = ring_place(me // SIDE, turns) - ring_place(owner // SIDE, turns)
        back = jnp.where(back < 0, back + turns, back)
        beside = jnp.where(owner % SIDE == me % SIDE, 0, 1)
        place = jnp.zeros_like(stored)
        for n, chunk in enumerate(order):
            place = jnp.where(back * 2 + beside == chunk[0] * 2 + chunk[1], n, place)
        place = place * rows + stored
        square = (place.shape[1], place.shape[1])
        own = lax.broadcasted_iota(jnp.int32, square, 0) == lax.broadcasted_iota(jnp.int32, square, 1)
        spread = jnp.where(own, jnp.broadcast_to(place.astype(jnp.float32), square), 0.0)
        columns.append(jnp.sum(spread, axis=1, keepdims=True))
    return jnp.concatenate(columns, axis=0).astype(jnp.int32)


def places_kernel(order, turns, owner_ref, stored_ref, piece_ref, index_ref, piece_out, sem):
    copy = pltpu.make_async_copy(piece_ref, piece_out, sem)
    copy.start()
    index_ref[...] = wanted_rows(order, turns, piece_ref.shape[0], owner_ref, stored_ref)
    copy.wait()


def places(order, turns, owners, stored, piece):
    return pl.pallas_call(
        functools.partial(places_kernel, order, turns),
        out_shape=(
            jax.ShapeDtypeStruct((stored.size, 1), jnp.int32),
            jax.ShapeDtypeStruct(piece.shape, piece.dtype),
        ),
        in_specs=[VMEM] * 3,
        out_specs=(VMEM, VMEM),
        scratch_shapes=[pltpu.SemaphoreType.DMA],
        compiler_params=params(),
    )(owners, stored, piece)


def early_kernel(chunks, index_ref, *refs):
    refs[-1][...] = chosen_rows(index_ref[...], chunks, refs[:-1], 0).astype(refs[-1].dtype)


def early(index, sources, width):
    rows = sources[0][0].shape[0]
    requests = index.shape[0]
    arrays = [array for chunk in sources for array in chunk]
    return pl.pallas_call(
        functools.partial(early_kernel, [len(chunk) for chunk in sources]),
        out_shape=jax.ShapeDtypeStruct((requests, width), arrays[0].dtype),
        in_specs=[VMEM] * (1 + len(arrays)),
        out_specs=VMEM,
        compiler_params=params(),
        cost_estimate=pl.CostEstimate(
            flops=2 * requests * width * rows * len(sources),
            bytes_accessed=2 * requests * width,
            transcendentals=0,
        ),
    )(index, *arrays)


def pick_kernel(chunks, first, index_ref, begun_ref, *refs):
    picked = chosen_rows(index_ref[...], chunks, refs[:-1], first)
    refs[-1][...] = (picked + begun_ref[...].astype(jnp.float32)).astype(begun_ref.dtype)


def pick(index, begun, sources, first):
    arrays = [array for chunk in sources for array in chunk]
    return pl.pallas_call(
        functools.partial(pick_kernel, [len(chunk) for chunk in sources], first),
        out_shape=jax.ShapeDtypeStruct(begun.shape, begun.dtype),
        in_specs=[VMEM] * (2 + len(arrays)),
        out_specs=VMEM,
        compiler_params=params(),
    )(index, begun, *arrays)


def by_span(picked, spans, channels):
    per = picked.shape[0] // spans
    parts = []
    for c in range(spans):
        for t in range(picked.shape[1] // channels):
            parts.append(picked[c * per : (c + 1) * per, t * channels : (t + 1) * channels])
    return jnp.concatenate(parts, axis=0)


def head_places(spans, columns):
    heads = columns // HD
    return [(c, slice(h * HD, (h + 1) * HD), c * heads + h) for c in range(spans) for h in range(heads)]


def score(spans, source, wk_ref, query_ref, scores_ref):
    keys = jnp.dot(source, wk_ref[...], preferred_element_type=jnp.float32).astype(jnp.bfloat16)
    per = keys.shape[0] // spans
    for c, lanes, n in head_places(spans, keys.shape[1]):
        scores_ref[n] = lax.dot_general(
            query_ref[c * SPAN : (c + 1) * SPAN, lanes],
            keys[c * per : (c + 1) * per, lanes],
            (((1,), (1,)), ((), ())),
            preferred_element_type=jnp.float32,
        )


def score_kernel(spans, picked_ref, wk_ref, query_ref, scores_ref):
    score(spans, by_span(picked_ref[...], spans, wk_ref.shape[0]), wk_ref, query_ref, scores_ref)


def scores_shape(picked, queries, channels, spans):
    return spans * (queries.shape[1] // HD), SPAN, picked.size // channels // spans


def own_scores(picked, w_key, queries, spans):
    return pl.pallas_call(
        functools.partial(score_kernel, spans),
        out_shape=jax.ShapeDtypeStruct(scores_shape(picked, queries, w_key.shape[0], spans), jnp.float32),
        in_specs=[VMEM] * 3,
        out_specs=VMEM,
        compiler_params=params(),
    )(picked, w_key, queries)


def values_kernel(spans, picked_ref, wv_ref, values_ref):
    source = by_span(picked_ref[...], spans, wv_ref.shape[0])
    values_ref[...] = jnp.dot(source, wv_ref[...], preferred_element_type=jnp.float32).astype(values_ref.dtype)


def own_values(picked, w_value, spans):
    rows = picked.size // w_value.shape[0]
    return pl.pallas_call(
        functools.partial(values_kernel, spans),
        out_shape=jax.ShapeDtypeStruct((rows, w_value.shape[1]), picked.dtype),
        in_specs=[VMEM] * 2,
        out_specs=VMEM,
        compiler_params=params(),
    )(picked, w_value)


def attend_kernel(
    spans, other_ref, wk_ref, wv_ref, query_ref, first_ref, values_ref, out_ref, second_ref, probs_ref
):
    other = by_span(other_ref[...], spans, wk_ref.shape[0])
    score(spans, other, wk_ref, query_ref, second_ref)
    per = other.shape[0] // spans
    more = jnp.dot(other, wv_ref[...], preferred_element_type=jnp.float32).astype(jnp.bfloat16)
    places = head_places(spans, more.shape[1])
    for c, lanes, n in places:
        scores = jnp.concatenate([first_ref[n], second_ref[n]], axis=1)
        raised = jnp.exp2((scores - jnp.max(scores, axis=-1, keepdims=True)) * EXPONENT)
        probs_ref[n] = (raised * (1.0 / jnp.sum(raised, axis=-1, keepdims=True))).astype(jnp.bfloat16)
    for c, lanes, n in places:
        rows = slice(c * per, (c + 1) * per)
        values = jnp.concatenate([values_ref[rows, lanes], more[rows, lanes]], axis=0)
        mixed = jnp.dot(probs_ref[n], values, preferred_element_type=jnp.float32)
        out_ref[c * SPAN : (c + 1) * SPAN, lanes] = mixed.astype(out_ref.dtype)


def attend(other, w_key, w_value, queries, first, values, spans):
    each = scores_shape(other, queries, w_key.shape[0], spans)
    return pl.pallas_call(
        functools.partial(attend_kernel, spans),
        out_shape=jax.ShapeDtypeStruct(queries.shape, queries.dtype),
        in_specs=[VMEM] * 6,
        out_specs=VMEM,
        scratch_shapes=[pltpu.VMEM(each, jnp.float32), pltpu.VMEM(each[:2] + (2 * each[2],), jnp.bfloat16)],
        compiler_params=params(),
    )(other, w_key, w_value, queries, first, values)


def send(chunk, pairs):
    return lax.ppermute(chunk, "wide", pairs)


def gathered_plan(queries, encodings, w_key, w_value, block_owner, block_row):
    wide_count = lax.axis_size("wide")
    turns = wide_count // SIDE
    rows = encodings.shape[0]
    spans = queries.shape[0] // SPAN
    line = ring_order(turns)
    onward = [
        (here * SIDE + x, there * SIDE + x) for here, there in zip(line, line[1:] + line[:1]) for x in range(SIDE)
    ]
    across = [(n, n + 1 if n % SIDE == 0 else n - 1) for n in range(wide_count)]
    *pieces, whole = half_columns(encodings)
    order = [(0, 0)]
    for k in range(1, turns):
        order += [(k, 0), (k - 1, 1)]
    order.append((turns - 1, 1))
    index, pieces[-1] = places(order, turns, jnp.transpose(block_owner, (0, 2, 1)), block_row, pieces[-1])
    held = {(0, 0): pieces}
    for k in range(1, turns):
        behind = held[k - 1, 0]
        steps = [send(piece, onward) for piece in behind]
        if k < turns - 1:
            held[k - 1, 1] = [send(whole if k == 1 else jnp.concatenate(behind, axis=1), across)]
        else:
            held[k - 1, 1] = [send(piece, across) for piece in behind]
        held[k, 0] = steps
    held[turns - 1, 1] = [send(piece, across) for piece in held[turns - 1, 0]]
    late = 3
    sources = [held[chunk] for chunk in order]
    begun = early(index, sources[:-late], whole.shape[1])
    picked = pick(index, begun, sources[-late:], (len(order) - late) * rows)
    other = lax.ppermute(picked, "heads", [(0, 1), (1, 0)])
    first = own_scores(picked, w_key, queries, spans)
    values = own_values(picked, w_value, spans)
    return attend(other, w_key, w_value, queries, first, values, spans)


def exchange(encodings, owners, stored, capacity):
    wide_count = lax.axis_size("wide")
    requests = owners.shape[0]
    order = jnp.arange(requests, dtype=jnp.int32)
    earlier = (owners[:, None] == owners[None, :]) & (order[None, :] < order[:, None])
    rank = jnp.sum(earlier.astype(jnp.int32), axis=1)
    slot = owners * capacity + rank
    table = jnp.full((wide_count * capacity,), -1, jnp.int32).at[slot].set(stored)
    table = table.reshape(wide_count, capacity)
    asked = lax.all_to_all(table, "wide", split_axis=0, concat_axis=0, tiled=True)
    wanted = jnp.maximum(asked, 0)
    picked = encodings[wanted]
    returned = lax.all_to_all(picked, "wide", split_axis=0, concat_axis=0, tiled=True)
    return returned.reshape(wide_count * capacity, encodings.shape[1])[slot]


def exchanged_plan(queries, encodings, w_key, w_value, owners, stored, capacity):
    fetched = exchange(encodings, owners, stored, capacity)
    channels = w_key.shape[0]
    source = fetched.reshape(-1, channels)
    keys = jnp.dot(source, w_key, preferred_element_type=jnp.float32).astype(jnp.bfloat16)
    values = jnp.dot(source, w_value, preferred_element_type=jnp.float32).astype(jnp.bfloat16)
    span_count = queries.shape[0] // SPAN
    heads_local = w_key.shape[1] // HD
    keys = keys.reshape(span_count, -1, heads_local, HD)
    values = values.reshape(span_count, -1, heads_local, HD)
    query_part = queries.reshape(span_count, SPAN, heads_local, HD)
    scores = jnp.einsum(
        "cqhd,ckhd->chqk", query_part, keys, preferred_element_type=jnp.float32
    ) * HD ** (-0.5)
    probs = jax.nn.softmax(scores, axis=-1).astype(jnp.bfloat16)
    mixed = jnp.einsum("chqk,ckhd->cqhd", probs, values, preferred_element_type=jnp.float32)
    return mixed.astype(jnp.bfloat16).reshape(queries.shape)


def on_device(queries, encodings, w_key, w_value, block_owner, block_row):
    wide_count = lax.axis_size("wide")
    requests = block_row.size
    capacity = 2 * ((requests + wide_count - 1) // wide_count)
    if encodings.shape[0] <= 2 * capacity:
        return gathered_plan(queries, encodings, w_key, w_value, block_owner, block_row)
    return exchanged_plan(
        queries, encodings, w_key, w_value, block_owner.reshape(-1), block_row.reshape(-1), capacity
    )


def solution(mesh):
    placed = (
        P(("groups", "wide"), "heads"),
        P(("groups", "wide"), None),
        P(None, "heads"),
        P(None, "heads"),
        P(("groups", "wide"), None, None),
        P(("groups", "wide"), None),
    )
    return jax.shard_map(
        on_device,
        mesh=mesh,
        in_specs=placed,
        out_specs=P(("groups", "wide"), "heads"),
        check_vma=False,
    )
```

```python
import functools

import jax
import jax.numpy as jnp
from jax import lax
from jax.experimental import pallas as pl
from jax.experimental.pallas import tpu as pltpu
from jax.sharding import PartitionSpec as P

HD = 128
SPAN = 64
SIDE = 2
LIMIT = 24 * 1024 * 1024
STREAMS = 2
EXPONENT = HD ** (-0.5) * 1.4426950408889634
VMEM = pl.BlockSpec(memory_space=pltpu.VMEM)


def params():
    return pltpu.CompilerParams(vmem_limit_bytes=LIMIT)


def half_kernel(enc_ref, *refs):
    outs, sems = refs[:-1], refs[-1]
    first = lax.axis_index("heads") * outs[-1].shape[1]
    copies = []
    for n, out in enumerate(outs):
        width = out.shape[1]
        start = first + (n * width if n < STREAMS else 0)
        copies.append(pltpu.make_async_copy(enc_ref.at[:, pl.ds(pl.multiple_of(start, 128), width)], out, sems.at[n]))
    for copy in copies:
        copy.start()
    for copy in copies:
        copy.wait()


def half_columns(encodings):
    rows, columns = encodings.shape
    whole = columns // lax.axis_size("heads")
    widths = [whole // STREAMS] * STREAMS + [whole]
    return pl.pallas_call(
        half_kernel,
        out_shape=[jax.ShapeDtypeStruct((rows, width), encodings.dtype) for width in widths],
        in_specs=[VMEM],
        out_specs=[VMEM] * len(widths),
        scratch_shapes=[pltpu.SemaphoreType.DMA((len(widths),))],
        compiler_params=params(),
    )(encodings)


def chosen_rows(index, chunks, refs, first):
    rows = refs[0].shape[0]
    width = min(ref.shape[1] for ref in refs)
    places = lax.broadcasted_iota(jnp.int32, (index.shape[0], len(chunks) * rows), 1) + first
    chosen = jnp.where(places == index, 1.0, 0.0).astype(refs[0].dtype)
    starts = [sum(chunks[:n]) for n in range(len(chunks))]
    parts = []
    for n in range(STREAMS):
        held = [
            refs[at + n][...] if arrays > 1 else refs[at][:, n * width : (n + 1) * width]
            for at, arrays in zip(starts, chunks)
        ]
        parts.append(jnp.dot(chosen, jnp.concatenate(held, axis=0), preferred_element_type=jnp.float32))
    return jnp.concatenate(parts, axis=1)


def ring_order(turns):
    return [0] + list(range(1, turns, 2)) + list(range(turns - 2 + turns % 2, 0, -2))


def ring_place(line, turns):
    return jnp.where(line % 2 == 1, (line + 1) // 2, jnp.where(line == 0, 0, turns - line // 2))


def wanted_rows(order, turns, rows, owner_ref, stored_ref):
    me = lax.axis_index("wide")
    columns = []
    for c in range(stored_ref.shape[0]):
        owner, stored = owner_ref[c], stored_ref[c : c + 1, :]
        back = ring_place(me // SIDE, turns) - ring_place(owner // SIDE, turns)
        back = jnp.where(back < 0, back + turns, back)
        beside = jnp.where(owner % SIDE == me % SIDE, 0, 1)
        place = jnp.zeros_like(stored)
        for n, chunk in enumerate(order):
            place = jnp.where(back * 2 + beside == chunk[0] * 2 + chunk[1], n, place)
        place = place * rows + stored
        square = (place.shape[1], place.shape[1])
        own = lax.broadcasted_iota(jnp.int32, square, 0) == lax.broadcasted_iota(jnp.int32, square, 1)
        spread = jnp.where(own, jnp.broadcast_to(place.astype(jnp.float32), square), 0.0)
        columns.append(jnp.sum(spread, axis=1, keepdims=True))
    return jnp.concatenate(columns, axis=0).astype(jnp.int32)


def places_kernel(order, turns, rows, owner_ref, stored_ref, index_ref):
    index_ref[...] = wanted_rows(order, turns, rows, owner_ref, stored_ref)


def places(order, turns, rows, owners, stored):
    return pl.pallas_call(
        functools.partial(places_kernel, order, turns, rows),
        out_shape=jax.ShapeDtypeStruct((stored.size, 1), jnp.int32),
        in_specs=[VMEM] * 2,
        out_specs=VMEM,
        compiler_params=params(),
    )(owners, stored)


def early_kernel(chunks, index_ref, *refs):
    refs[-1][...] = chosen_rows(index_ref[...], chunks, refs[:-1], 0).astype(refs[-1].dtype)


def early(index, sources, width):
    rows = sources[0][0].shape[0]
    requests = index.shape[0]
    arrays = [array for chunk in sources for array in chunk]
    return pl.pallas_call(
        functools.partial(early_kernel, [len(chunk) for chunk in sources]),
        out_shape=jax.ShapeDtypeStruct((requests, width), arrays[0].dtype),
        in_specs=[VMEM] * (1 + len(arrays)),
        out_specs=VMEM,
        compiler_params=params(),
        cost_estimate=pl.CostEstimate(
            flops=2 * requests * width * rows * len(sources),
            bytes_accessed=2 * requests * width,
            transcendentals=0,
        ),
    )(index, *arrays)


def pick_kernel(chunks, first, index_ref, begun_ref, *refs):
    picked = chosen_rows(index_ref[...], chunks, refs[:-1], first)
    refs[-1][...] = (picked + begun_ref[...].astype(jnp.float32)).astype(begun_ref.dtype)


def pick(index, begun, sources, first):
    arrays = [array for chunk in sources for array in chunk]
    return pl.pallas_call(
        functools.partial(pick_kernel, [len(chunk) for chunk in sources], first),
        out_shape=jax.ShapeDtypeStruct(begun.shape, begun.dtype),
        in_specs=[VMEM] * (2 + len(arrays)),
        out_specs=VMEM,
        compiler_params=params(),
    )(index, begun, *arrays)


def by_span(picked, spans, channels):
    per = picked.shape[0] // spans
    parts = []
    for c in range(spans):
        for t in range(picked.shape[1] // channels):
            parts.append(picked[c * per : (c + 1) * per, t * channels : (t + 1) * channels])
    return jnp.concatenate(parts, axis=0)


def head_places(spans, columns):
    heads = columns // HD
    return [(c, slice(h * HD, (h + 1) * HD), c * heads + h) for c in range(spans) for h in range(heads)]


def score(spans, source, wk_ref, query_ref, scores_ref):
    keys = jnp.dot(source, wk_ref[...], preferred_element_type=jnp.float32).astype(jnp.bfloat16)
    per = keys.shape[0] // spans
    for c, lanes, n in head_places(spans, keys.shape[1]):
        scores_ref[n] = lax.dot_general(
            query_ref[c * SPAN : (c + 1) * SPAN, lanes],
            keys[c * per : (c + 1) * per, lanes],
            (((1,), (1,)), ((), ())),
            preferred_element_type=jnp.float32,
        )


def score_kernel(spans, picked_ref, wk_ref, query_ref, scores_ref):
    score(spans, by_span(picked_ref[...], spans, wk_ref.shape[0]), wk_ref, query_ref, scores_ref)


def scores_shape(picked, queries, channels, spans):
    return spans * (queries.shape[1] // HD), SPAN, picked.size // channels // spans


def own_scores(picked, w_key, queries, spans):
    return pl.pallas_call(
        functools.partial(score_kernel, spans),
        out_shape=jax.ShapeDtypeStruct(scores_shape(picked, queries, w_key.shape[0], spans), jnp.float32),
        in_specs=[VMEM] * 3,
        out_specs=VMEM,
        compiler_params=params(),
    )(picked, w_key, queries)


def values_kernel(spans, picked_ref, wv_ref, values_ref):
    source = by_span(picked_ref[...], spans, wv_ref.shape[0])
    values_ref[...] = jnp.dot(source, wv_ref[...], preferred_element_type=jnp.float32).astype(values_ref.dtype)


def own_values(picked, w_value, spans):
    rows = picked.size // w_value.shape[0]
    return pl.pallas_call(
        functools.partial(values_kernel, spans),
        out_shape=jax.ShapeDtypeStruct((rows, w_value.shape[1]), picked.dtype),
        in_specs=[VMEM] * 2,
        out_specs=VMEM,
        compiler_params=params(),
    )(picked, w_value)


def attend_kernel(
    spans, other_ref, wk_ref, wv_ref, query_ref, first_ref, values_ref, out_ref, second_ref, probs_ref
):
    other = by_span(other_ref[...], spans, wk_ref.shape[0])
    score(spans, other, wk_ref, query_ref, second_ref)
    per = other.shape[0] // spans
    more = jnp.dot(other, wv_ref[...], preferred_element_type=jnp.float32).astype(jnp.bfloat16)
    places = head_places(spans, more.shape[1])
    for c, lanes, n in places:
        scores = jnp.concatenate([first_ref[n], second_ref[n]], axis=1)
        raised = jnp.exp2((scores - jnp.max(scores, axis=-1, keepdims=True)) * EXPONENT)
        probs_ref[n] = (raised * (1.0 / jnp.sum(raised, axis=-1, keepdims=True))).astype(jnp.bfloat16)
    for c, lanes, n in places:
        rows = slice(c * per, (c + 1) * per)
        values = jnp.concatenate([values_ref[rows, lanes], more[rows, lanes]], axis=0)
        mixed = jnp.dot(probs_ref[n], values, preferred_element_type=jnp.float32)
        out_ref[c * SPAN : (c + 1) * SPAN, lanes] = mixed.astype(out_ref.dtype)


def attend(other, w_key, w_value, queries, first, values, spans):
    each = scores_shape(other, queries, w_key.shape[0], spans)
    return pl.pallas_call(
        functools.partial(attend_kernel, spans),
        out_shape=jax.ShapeDtypeStruct(queries.shape, queries.dtype),
        in_specs=[VMEM] * 6,
        out_specs=VMEM,
        scratch_shapes=[pltpu.VMEM(each, jnp.float32), pltpu.VMEM(each[:2] + (2 * each[2],), jnp.bfloat16)],
        compiler_params=params(),
    )(other, w_key, w_value, queries, first, values)


def send(chunk, pairs):
    return lax.ppermute(chunk, "wide", pairs)


def gathered_plan(queries, encodings, w_key, w_value, block_owner, block_row):
    wide_count = lax.axis_size("wide")
    turns = wide_count // SIDE
    rows = encodings.shape[0]
    spans = queries.shape[0] // SPAN
    line = ring_order(turns)
    onward = [
        (here * SIDE + x, there * SIDE + x) for here, there in zip(line, line[1:] + line[:1]) for x in range(SIDE)
    ]
    across = [(n, n + 1 if n % SIDE == 0 else n - 1) for n in range(wide_count)]
    backward = [(there, here) for here, there in onward]
    *pieces, whole = half_columns(encodings)
    held = {(0, 0): pieces}
    ahead = turns // 2
    for k in range(1, ahead + 1):
        held[k, 0] = [send(piece, onward) for piece in held[k - 1, 0]]
        joined = whole if k == 1 else jnp.concatenate(held[k - 1, 0], axis=1)
        held[k - 1, 1] = [send(joined, across)]
    returned = whole
    for k in range(turns - 1, ahead, -1):
        returned = send(returned, backward)
        held[k, 0], held[k, 1] = [returned], [send(returned, across)]
    held[ahead, 1] = [send(piece, across) for piece in held[ahead, 0]]
    last = [(ahead, 0), (ahead + 1, 1), (ahead, 1)]
    order = [chunk for chunk in held if chunk not in last] + last
    index = places(order, turns, rows, jnp.transpose(block_owner, (0, 2, 1)), block_row)
    late = 3
    sources = [held[chunk] for chunk in order]
    begun = early(index, sources[:-late], whole.shape[1])
    picked = pick(index, begun, sources[-late:], (len(order) - late) * rows)
    other = lax.ppermute(picked, "heads", [(0, 1), (1, 0)])
    first = own_scores(picked, w_key, queries, spans)
    values = own_values(picked, w_value, spans)
    return attend(other, w_key, w_value, queries, first, values, spans)


def exchange(encodings, owners, stored, capacity):
    wide_count = lax.axis_size("wide")
    requests = owners.shape[0]
    order = jnp.arange(requests, dtype=jnp.int32)
    earlier = (owners[:, None] == owners[None, :]) & (order[None, :] < order[:, None])
    rank = jnp.sum(earlier.astype(jnp.int32), axis=1)
    slot = owners * capacity + rank
    table = jnp.full((wide_count * capacity,), -1, jnp.int32).at[slot].set(stored)
    table = table.reshape(wide_count, capacity)
    asked = lax.all_to_all(table, "wide", split_axis=0, concat_axis=0, tiled=True)
    wanted = jnp.maximum(asked, 0)
    picked = encodings[wanted]
    returned = lax.all_to_all(picked, "wide", split_axis=0, concat_axis=0, tiled=True)
    return returned.reshape(wide_count * capacity, encodings.shape[1])[slot]


def exchanged_plan(queries, encodings, w_key, w_value, owners, stored, capacity):
    fetched = exchange(encodings, owners, stored, capacity)
    channels = w_key.shape[0]
    source = fetched.reshape(-1, channels)
    keys = jnp.dot(source, w_key, preferred_element_type=jnp.float32).astype(jnp.bfloat16)
    values = jnp.dot(source, w_value, preferred_element_type=jnp.float32).astype(jnp.bfloat16)
    span_count = queries.shape[0] // SPAN
    heads_local = w_key.shape[1] // HD
    keys = keys.reshape(span_count, -1, heads_local, HD)
    values = values.reshape(span_count, -1, heads_local, HD)
    query_part = queries.reshape(span_count, SPAN, heads_local, HD)
    scores = jnp.einsum(
        "cqhd,ckhd->chqk", query_part, keys, preferred_element_type=jnp.float32
    ) * HD ** (-0.5)
    probs = jax.nn.softmax(scores, axis=-1).astype(jnp.bfloat16)
    mixed = jnp.einsum("chqk,ckhd->cqhd", probs, values, preferred_element_type=jnp.float32)
    return mixed.astype(jnp.bfloat16).reshape(queries.shape)


def on_device(queries, encodings, w_key, w_value, block_owner, block_row):
    wide_count = lax.axis_size("wide")
    requests = block_row.size
    capacity = 2 * ((requests + wide_count - 1) // wide_count)
    if encodings.shape[0] <= 2 * capacity:
        return gathered_plan(queries, encodings, w_key, w_value, block_owner, block_row)
    return exchanged_plan(
        queries, encodings, w_key, w_value, block_owner.reshape(-1), block_row.reshape(-1), capacity
    )


def solution(mesh):
    placed = (
        P(("groups", "wide"), "heads"),
        P(("groups", "wide"), None),
        P(None, "heads"),
        P(None, "heads"),
        P(("groups", "wide"), None, None),
        P(("groups", "wide"), None),
    )
    return jax.shard_map(
        on_device,
        mesh=mesh,
        in_specs=placed,
        out_specs=P(("groups", "wide"), "heads"),
        check_vma=False,
    )
```

```python
import functools

import jax
import jax.numpy as jnp
from jax import lax
from jax.experimental import pallas as pl
from jax.experimental.pallas import tpu as pltpu
from jax.sharding import PartitionSpec as P

HD = 128
SPAN = 64
SIDE = 2
LIMIT = 24 * 1024 * 1024
STREAMS = 2
EXPONENT = HD ** (-0.5) * 1.4426950408889634
VMEM = pl.BlockSpec(memory_space=pltpu.VMEM)


def params():
    return pltpu.CompilerParams(vmem_limit_bytes=LIMIT)


def half_kernel(enc_ref, *refs):
    outs, sems = refs[:-1], refs[-1]
    first = lax.axis_index("heads") * outs[-1].shape[1]
    copies = []
    for n, out in enumerate(outs):
        width = out.shape[1]
        start = first + (n * width if n < STREAMS else 0)
        copies.append(pltpu.make_async_copy(enc_ref.at[:, pl.ds(pl.multiple_of(start, 128), width)], out, sems.at[n]))
    for copy in copies:
        copy.start()
    for copy in copies:
        copy.wait()


def half_columns(encodings):
    rows, columns = encodings.shape
    whole = columns // lax.axis_size("heads")
    widths = [whole // STREAMS] * STREAMS + [whole]
    return pl.pallas_call(
        half_kernel,
        out_shape=[jax.ShapeDtypeStruct((rows, width), encodings.dtype) for width in widths],
        in_specs=[VMEM],
        out_specs=[VMEM] * len(widths),
        scratch_shapes=[pltpu.SemaphoreType.DMA((len(widths),))],
        compiler_params=params(),
    )(encodings)


def chosen_rows(index, chunks, refs, first):
    rows = refs[0].shape[0]
    width = min(ref.shape[1] for ref in refs)
    places = lax.broadcasted_iota(jnp.int32, (index.shape[0], len(chunks) * rows), 1) + first
    chosen = jnp.where(places == index, 1.0, 0.0).astype(refs[0].dtype)
    starts = [sum(chunks[:n]) for n in range(len(chunks))]
    parts = []
    for n in range(STREAMS):
        held = [
            refs[at + n][...] if arrays > 1 else refs[at][:, n * width : (n + 1) * width]
            for at, arrays in zip(starts, chunks)
        ]
        parts.append(jnp.dot(chosen, jnp.concatenate(held, axis=0), preferred_element_type=jnp.float32))
    return jnp.concatenate(parts, axis=1)


def ring_order(turns):
    return [0] + list(range(1, turns, 2)) + list(range(turns - 2 + turns % 2, 0, -2))


def ring_place(line, turns):
    return jnp.where(line % 2 == 1, (line + 1) // 2, jnp.where(line == 0, 0, turns - line // 2))


def wanted_rows(order, turns, rows, owner_ref, stored_ref):
    me = lax.axis_index("wide")
    columns = []
    for c in range(stored_ref.shape[0]):
        owner, stored = owner_ref[c], stored_ref[c : c + 1, :]
        back = ring_place(me // SIDE, turns) - ring_place(owner // SIDE, turns)
        back = jnp.where(back < 0, back + turns, back)
        beside = jnp.where(owner % SIDE == me % SIDE, 0, 1)
        place = jnp.zeros_like(stored)
        for n, chunk in enumerate(order):
            place = jnp.where(back * 2 + beside == chunk[0] * 2 + chunk[1], n, place)
        place = place * rows + stored
        square = (place.shape[1], place.shape[1])
        own = lax.broadcasted_iota(jnp.int32, square, 0) == lax.broadcasted_iota(jnp.int32, square, 1)
        spread = jnp.where(own, jnp.broadcast_to(place.astype(jnp.float32), square), 0.0)
        columns.append(jnp.sum(spread, axis=1, keepdims=True))
    return jnp.concatenate(columns, axis=0).astype(jnp.int32)


def places_kernel(order, turns, rows, owner_ref, stored_ref, index_ref):
    index_ref[...] = wanted_rows(order, turns, rows, owner_ref, stored_ref)


def places(order, turns, rows, owners, stored):
    return pl.pallas_call(
        functools.partial(places_kernel, order, turns, rows),
        out_shape=jax.ShapeDtypeStruct((stored.size, 1), jnp.int32),
        in_specs=[VMEM] * 2,
        out_specs=VMEM,
        compiler_params=params(),
    )(owners, stored)


def early_kernel(chunks, index_ref, *refs):
    refs[-1][...] = chosen_rows(index_ref[...], chunks, refs[:-1], 0).astype(refs[-1].dtype)


def early(index, sources, width):
    rows = sources[0][0].shape[0]
    requests = index.shape[0]
    arrays = [array for chunk in sources for array in chunk]
    return pl.pallas_call(
        functools.partial(early_kernel, [len(chunk) for chunk in sources]),
        out_shape=jax.ShapeDtypeStruct((requests, width), arrays[0].dtype),
        in_specs=[VMEM] * (1 + len(arrays)),
        out_specs=VMEM,
        compiler_params=params(),
        cost_estimate=pl.CostEstimate(
            flops=2 * requests * width * rows * len(sources),
            bytes_accessed=2 * requests * width,
            transcendentals=0,
        ),
    )(index, *arrays)


def pick_kernel(chunks, first, index_ref, begun_ref, *refs):
    picked = chosen_rows(index_ref[...], chunks, refs[:-1], first)
    refs[-1][...] = (picked + begun_ref[...].astype(jnp.float32)).astype(begun_ref.dtype)


def pick(index, begun, sources, first):
    arrays = [array for chunk in sources for array in chunk]
    return pl.pallas_call(
        functools.partial(pick_kernel, [len(chunk) for chunk in sources], first),
        out_shape=jax.ShapeDtypeStruct(begun.shape, begun.dtype),
        in_specs=[VMEM] * (2 + len(arrays)),
        out_specs=VMEM,
        compiler_params=params(),
    )(index, begun, *arrays)


def by_span(picked, spans, channels):
    per = picked.shape[0] // spans
    parts = []
    for c in range(spans):
        for t in range(picked.shape[1] // channels):
            parts.append(picked[c * per : (c + 1) * per, t * channels : (t + 1) * channels])
    return jnp.concatenate(parts, axis=0)


PAIR = 2


def pair_places(spans, columns):
    pairs = columns // (PAIR * HD)
    return [
        (c, slice(p * PAIR * HD, (p + 1) * PAIR * HD), c * pairs + p) for c in range(spans) for p in range(pairs)
    ]


def apart(query):
    none = jnp.zeros((query.shape[0], HD), query.dtype)
    upper = jnp.concatenate([query[:, :HD], none], axis=1)
    lower = jnp.concatenate([none, query[:, HD:]], axis=1)
    return jnp.concatenate([upper, lower], axis=0)


def score(spans, source, wk_ref, query_ref, scores_ref):
    keys = jnp.dot(source, wk_ref[...], preferred_element_type=jnp.float32).astype(jnp.bfloat16)
    per = keys.shape[0] // spans
    for c, lanes, n in pair_places(spans, keys.shape[1]):
        scores_ref[n] = lax.dot_general(
            keys[c * per : (c + 1) * per, lanes],
            apart(query_ref[c * SPAN : (c + 1) * SPAN, lanes]),
            (((1,), (1,)), ((), ())),
            preferred_element_type=jnp.float32,
        )


def score_kernel(spans, picked_ref, wk_ref, query_ref, scores_ref):
    score(spans, by_span(picked_ref[...], spans, wk_ref.shape[0]), wk_ref, query_ref, scores_ref)


def scores_shape(picked, queries, channels, spans):
    return spans * (queries.shape[1] // (PAIR * HD)), picked.size // channels // spans, PAIR * SPAN


def own_scores(picked, w_key, queries, spans):
    return pl.pallas_call(
        functools.partial(score_kernel, spans),
        out_shape=jax.ShapeDtypeStruct(scores_shape(picked, queries, w_key.shape[0], spans), jnp.float32),
        in_specs=[VMEM] * 3,
        out_specs=VMEM,
        compiler_params=params(),
    )(picked, w_key, queries)


def values_kernel(spans, picked_ref, wv_ref, values_ref):
    source = by_span(picked_ref[...], spans, wv_ref.shape[0])
    values_ref[...] = jnp.dot(source, wv_ref[...], preferred_element_type=jnp.float32).astype(values_ref.dtype)


def own_values(picked, w_value, spans):
    rows = picked.size // w_value.shape[0]
    return pl.pallas_call(
        functools.partial(values_kernel, spans),
        out_shape=jax.ShapeDtypeStruct((rows, w_value.shape[1]), picked.dtype),
        in_specs=[VMEM] * 2,
        out_specs=VMEM,
        compiler_params=params(),
    )(picked, w_value)


def attend_kernel(
    spans, other_ref, wk_ref, wv_ref, query_ref, first_ref, values_ref, out_ref, second_ref, probs_ref
):
    other = by_span(other_ref[...], spans, wk_ref.shape[0])
    score(spans, other, wk_ref, query_ref, second_ref)
    per = other.shape[0] // spans
    more = jnp.dot(other, wv_ref[...], preferred_element_type=jnp.float32).astype(jnp.bfloat16)
    everything = pair_places(spans, more.shape[1])
    for c, lanes, n in everything:
        scores = jnp.concatenate([first_ref[n], second_ref[n]], axis=0)
        raised = jnp.exp2((scores - jnp.max(scores, axis=0, keepdims=True)) * EXPONENT)
        probs_ref[n] = (raised * (1.0 / jnp.sum(raised, axis=0, keepdims=True))).astype(jnp.bfloat16)
    for c, lanes, n in everything:
        rows = slice(c * per, (c + 1) * per)
        values = jnp.concatenate([values_ref[rows, lanes], more[rows, lanes]], axis=0)
        mixed = lax.dot_general(
            probs_ref[n], values, (((0,), (0,)), ((), ())), preferred_element_type=jnp.float32
        ).astype(out_ref.dtype)
        own = [mixed[h * SPAN : (h + 1) * SPAN, h * HD : (h + 1) * HD] for h in range(PAIR)]
        out_ref[c * SPAN : (c + 1) * SPAN, lanes] = jnp.concatenate(own, axis=1)


def attend(other, w_key, w_value, queries, first, values, spans):
    each = scores_shape(other, queries, w_key.shape[0], spans)
    return pl.pallas_call(
        functools.partial(attend_kernel, spans),
        out_shape=jax.ShapeDtypeStruct(queries.shape, queries.dtype),
        in_specs=[VMEM] * 6,
        out_specs=VMEM,
        scratch_shapes=[pltpu.VMEM(each, jnp.float32), pltpu.VMEM((each[0], 2 * each[1], each[2]), jnp.bfloat16)],
        compiler_params=params(),
    )(other, w_key, w_value, queries, first, values)


def send(chunk, pairs):
    return lax.ppermute(chunk, "wide", pairs)


def gathered_plan(queries, encodings, w_key, w_value, block_owner, block_row):
    wide_count = lax.axis_size("wide")
    turns = wide_count // SIDE
    rows = encodings.shape[0]
    spans = queries.shape[0] // SPAN
    line = ring_order(turns)
    onward = [
        (here * SIDE + x, there * SIDE + x) for here, there in zip(line, line[1:] + line[:1]) for x in range(SIDE)
    ]
    across = [(n, n + 1 if n % SIDE == 0 else n - 1) for n in range(wide_count)]
    *pieces, whole = half_columns(encodings)
    order = [(0, 0)]
    for k in range(1, turns):
        order += [(k, 0), (k - 1, 1)]
    order.append((turns - 1, 1))
    index = places(order, turns, rows, jnp.transpose(block_owner, (0, 2, 1)), block_row)
    held = {(0, 0): pieces}
    for k in range(1, turns):
        behind = held[k - 1, 0]
        steps = [send(piece, onward) for piece in behind]
        if k < turns - 1:
            held[k - 1, 1] = [send(whole if k == 1 else jnp.concatenate(behind, axis=1), across)]
        else:
            held[k - 1, 1] = [send(piece, across) for piece in behind]
        held[k, 0] = steps
    held[turns - 1, 1] = [send(piece, across) for piece in held[turns - 1, 0]]
    late = 3
    sources = [held[chunk] for chunk in order]
    begun = early(index, sources[:-late], whole.shape[1])
    picked = pick(index, begun, sources[-late:], (len(order) - late) * rows)
    other = lax.ppermute(picked, "heads", [(0, 1), (1, 0)])
    first = own_scores(picked, w_key, queries, spans)
    values = own_values(picked, w_value, spans)
    return attend(other, w_key, w_value, queries, first, values, spans)


def exchange(encodings, owners, stored, capacity):
    wide_count = lax.axis_size("wide")
    requests = owners.shape[0]
    order = jnp.arange(requests, dtype=jnp.int32)
    earlier = (owners[:, None] == owners[None, :]) & (order[None, :] < order[:, None])
    rank = jnp.sum(earlier.astype(jnp.int32), axis=1)
    slot = owners * capacity + rank
    table = jnp.full((wide_count * capacity,), -1, jnp.int32).at[slot].set(stored)
    table = table.reshape(wide_count, capacity)
    asked = lax.all_to_all(table, "wide", split_axis=0, concat_axis=0, tiled=True)
    wanted = jnp.maximum(asked, 0)
    picked = encodings[wanted]
    returned = lax.all_to_all(picked, "wide", split_axis=0, concat_axis=0, tiled=True)
    return returned.reshape(wide_count * capacity, encodings.shape[1])[slot]


def exchanged_plan(queries, encodings, w_key, w_value, owners, stored, capacity):
    fetched = exchange(encodings, owners, stored, capacity)
    channels = w_key.shape[0]
    source = fetched.reshape(-1, channels)
    keys = jnp.dot(source, w_key, preferred_element_type=jnp.float32).astype(jnp.bfloat16)
    values = jnp.dot(source, w_value, preferred_element_type=jnp.float32).astype(jnp.bfloat16)
    span_count = queries.shape[0] // SPAN
    heads_local = w_key.shape[1] // HD
    keys = keys.reshape(span_count, -1, heads_local, HD)
    values = values.reshape(span_count, -1, heads_local, HD)
    query_part = queries.reshape(span_count, SPAN, heads_local, HD)
    scores = jnp.einsum(
        "cqhd,ckhd->chqk", query_part, keys, preferred_element_type=jnp.float32
    ) * HD ** (-0.5)
    probs = jax.nn.softmax(scores, axis=-1).astype(jnp.bfloat16)
    mixed = jnp.einsum("chqk,ckhd->cqhd", probs, values, preferred_element_type=jnp.float32)
    return mixed.astype(jnp.bfloat16).reshape(queries.shape)


def on_device(queries, encodings, w_key, w_value, block_owner, block_row):
    wide_count = lax.axis_size("wide")
    requests = block_row.size
    capacity = 2 * ((requests + wide_count - 1) // wide_count)
    if encodings.shape[0] <= 2 * capacity:
        return gathered_plan(queries, encodings, w_key, w_value, block_owner, block_row)
    return exchanged_plan(
        queries, encodings, w_key, w_value, block_owner.reshape(-1), block_row.reshape(-1), capacity
    )


def solution(mesh):
    placed = (
        P(("groups", "wide"), "heads"),
        P(("groups", "wide"), None),
        P(None, "heads"),
        P(None, "heads"),
        P(("groups", "wide"), None, None),
        P(("groups", "wide"), None),
    )
    return jax.shard_map(
        on_device,
        mesh=mesh,
        in_specs=placed,
        out_specs=P(("groups", "wide"), "heads"),
        check_vma=False,
    )
```

```python
import functools

import jax
import jax.numpy as jnp
from jax import lax
from jax.experimental import pallas as pl
from jax.experimental.pallas import tpu as pltpu
from jax.sharding import PartitionSpec as P

HD = 128
SPAN = 64
SIDE = 2
LIMIT = 24 * 1024 * 1024
STREAMS = 3
EXPONENT = HD ** (-0.5) * 1.4426950408889634
VMEM = pl.BlockSpec(memory_space=pltpu.VMEM)


def params():
    return pltpu.CompilerParams(vmem_limit_bytes=LIMIT)


def shares(width):
    lots = width // 128
    widths = [128 * (lots // STREAMS + (n < lots % STREAMS)) for n in range(STREAMS)]
    return widths, [sum(widths[:n]) for n in range(STREAMS)]


def half_kernel(enc_ref, *refs):
    outs, sems = refs[:-1], refs[-1]
    width = outs[-1].shape[1]
    first = lax.axis_index("heads") * width
    copies = []
    for n, (out, start) in enumerate(zip(outs, shares(width)[1] + [0])):
        columns = pl.ds(pl.multiple_of(first + start, 128), out.shape[1])
        copies.append(pltpu.make_async_copy(enc_ref.at[:, columns], out, sems.at[n]))
    for copy in copies:
        copy.start()
    for copy in copies:
        copy.wait()


def half_columns(encodings):
    rows, columns = encodings.shape
    whole = columns // lax.axis_size("heads")
    widths = shares(whole)[0] + [whole]
    return pl.pallas_call(
        half_kernel,
        out_shape=[jax.ShapeDtypeStruct((rows, width), encodings.dtype) for width in widths],
        in_specs=[VMEM],
        out_specs=[VMEM] * len(widths),
        scratch_shapes=[pltpu.SemaphoreType.DMA((len(widths),))],
        compiler_params=params(),
    )(encodings)


def chosen_rows(index, chunks, width, refs, first):
    rows = refs[0].shape[0]
    places = lax.broadcasted_iota(jnp.int32, (index.shape[0], len(chunks) * rows), 1) + first
    chosen = jnp.where(places == index, 1.0, 0.0).astype(refs[0].dtype)
    starts = [sum(chunks[:n]) for n in range(len(chunks))]
    parts = []
    for n, (share, column) in enumerate(zip(*shares(width))):
        held = [
            refs[at + n][...] if arrays > 1 else refs[at][:, column : column + share]
            for at, arrays in zip(starts, chunks)
        ]
        parts.append(jnp.dot(chosen, jnp.concatenate(held, axis=0), preferred_element_type=jnp.float32))
    return jnp.concatenate(parts, axis=1)


def ring_order(turns):
    return [0] + list(range(1, turns, 2)) + list(range(turns - 2 + turns % 2, 0, -2))


def ring_place(line, turns):
    return jnp.where(line % 2 == 1, (line + 1) // 2, jnp.where(line == 0, 0, turns - line // 2))


def wanted_rows(order, turns, rows, owner_ref, stored_ref):
    me = lax.axis_index("wide")
    columns = []
    for c in range(stored_ref.shape[0]):
        owner, stored = owner_ref[c], stored_ref[c : c + 1, :]
        back = ring_place(me // SIDE, turns) - ring_place(owner // SIDE, turns)
        back = jnp.where(back < 0, back + turns, back)
        beside = jnp.where(owner % SIDE == me % SIDE, 0, 1)
        place = jnp.zeros_like(stored)
        for n, chunk in enumerate(order):
            place = jnp.where(back * 2 + beside == chunk[0] * 2 + chunk[1], n, place)
        place = place * rows + stored
        square = (place.shape[1], place.shape[1])
        own = lax.broadcasted_iota(jnp.int32, square, 0) == lax.broadcasted_iota(jnp.int32, square, 1)
        spread = jnp.where(own, jnp.broadcast_to(place.astype(jnp.float32), square), 0.0)
        columns.append(jnp.sum(spread, axis=1, keepdims=True))
    return jnp.concatenate(columns, axis=0).astype(jnp.int32)


def places_kernel(order, turns, rows, owner_ref, stored_ref, index_ref):
    index_ref[...] = wanted_rows(order, turns, rows, owner_ref, stored_ref)


def places(order, turns, rows, owners, stored):
    return pl.pallas_call(
        functools.partial(places_kernel, order, turns, rows),
        out_shape=jax.ShapeDtypeStruct((stored.size, 1), jnp.int32),
        in_specs=[VMEM] * 2,
        out_specs=VMEM,
        compiler_params=params(),
    )(owners, stored)


def early_kernel(chunks, index_ref, *refs):
    refs[-1][...] = chosen_rows(index_ref[...], chunks, refs[-1].shape[1], refs[:-1], 0).astype(refs[-1].dtype)


def early(index, sources, width):
    rows = sources[0][0].shape[0]
    requests = index.shape[0]
    arrays = [array for chunk in sources for array in chunk]
    return pl.pallas_call(
        functools.partial(early_kernel, [len(chunk) for chunk in sources]),
        out_shape=jax.ShapeDtypeStruct((requests, width), arrays[0].dtype),
        in_specs=[VMEM] * (1 + len(arrays)),
        out_specs=VMEM,
        compiler_params=params(),
        cost_estimate=pl.CostEstimate(
            flops=2 * requests * width * rows * len(sources),
            bytes_accessed=2 * requests * width,
            transcendentals=0,
        ),
    )(index, *arrays)


def pick_kernel(chunks, first, index_ref, begun_ref, *refs):
    picked = chosen_rows(index_ref[...], chunks, refs[-1].shape[1], refs[:-1], first)
    refs[-1][...] = (picked + begun_ref[...].astype(jnp.float32)).astype(begun_ref.dtype)


def pick(index, begun, sources, first):
    arrays = [array for chunk in sources for array in chunk]
    return pl.pallas_call(
        functools.partial(pick_kernel, [len(chunk) for chunk in sources], first),
        out_shape=jax.ShapeDtypeStruct(begun.shape, begun.dtype),
        in_specs=[VMEM] * (2 + len(arrays)),
        out_specs=VMEM,
        compiler_params=params(),
    )(index, begun, *arrays)


def by_span(picked, spans, channels):
    per = picked.shape[0] // spans
    parts = []
    for c in range(spans):
        for t in range(picked.shape[1] // channels):
            parts.append(picked[c * per : (c + 1) * per, t * channels : (t + 1) * channels])
    return jnp.concatenate(parts, axis=0)


PAIR = 2


def pair_places(spans, columns):
    pairs = columns // (PAIR * HD)
    return [
        (c, slice(p * PAIR * HD, (p + 1) * PAIR * HD), c * pairs + p) for c in range(spans) for p in range(pairs)
    ]


def apart(query):
    none = jnp.zeros((query.shape[0], HD), query.dtype)
    upper = jnp.concatenate([query[:, :HD], none], axis=1)
    lower = jnp.concatenate([none, query[:, HD:]], axis=1)
    return jnp.concatenate([upper, lower], axis=0)


def score(spans, source, wk_ref, query_ref, scores_ref):
    keys = jnp.dot(source, wk_ref[...], preferred_element_type=jnp.float32).astype(jnp.bfloat16)
    per = keys.shape[0] // spans
    for c, lanes, n in pair_places(spans, keys.shape[1]):
        scores_ref[n] = lax.dot_general(
            keys[c * per : (c + 1) * per, lanes],
            apart(query_ref[c * SPAN : (c + 1) * SPAN, lanes]),
            (((1,), (1,)), ((), ())),
            preferred_element_type=jnp.float32,
        )


def score_kernel(spans, picked_ref, wk_ref, query_ref, scores_ref):
    score(spans, by_span(picked_ref[...], spans, wk_ref.shape[0]), wk_ref, query_ref, scores_ref)


def scores_shape(picked, queries, channels, spans):
    return spans * (queries.shape[1] // (PAIR * HD)), picked.size // channels // spans, PAIR * SPAN


def own_scores(picked, w_key, queries, spans):
    return pl.pallas_call(
        functools.partial(score_kernel, spans),
        out_shape=jax.ShapeDtypeStruct(scores_shape(picked, queries, w_key.shape[0], spans), jnp.float32),
        in_specs=[VMEM] * 3,
        out_specs=VMEM,
        compiler_params=params(),
    )(picked, w_key, queries)


def values_kernel(spans, picked_ref, wv_ref, values_ref):
    source = by_span(picked_ref[...], spans, wv_ref.shape[0])
    values_ref[...] = jnp.dot(source, wv_ref[...], preferred_element_type=jnp.float32).astype(values_ref.dtype)


def own_values(picked, w_value, spans):
    rows = picked.size // w_value.shape[0]
    return pl.pallas_call(
        functools.partial(values_kernel, spans),
        out_shape=jax.ShapeDtypeStruct((rows, w_value.shape[1]), picked.dtype),
        in_specs=[VMEM] * 2,
        out_specs=VMEM,
        compiler_params=params(),
    )(picked, w_value)


def attend_kernel(
    spans, other_ref, wk_ref, wv_ref, query_ref, first_ref, values_ref, out_ref, second_ref, probs_ref
):
    other = by_span(other_ref[...], spans, wk_ref.shape[0])
    score(spans, other, wk_ref, query_ref, second_ref)
    per = other.shape[0] // spans
    more = jnp.dot(other, wv_ref[...], preferred_element_type=jnp.float32).astype(jnp.bfloat16)
    everything = pair_places(spans, more.shape[1])
    for c, lanes, n in everything:
        scores = jnp.concatenate([first_ref[n], second_ref[n]], axis=0)
        raised = jnp.exp2((scores - jnp.max(scores, axis=0, keepdims=True)) * EXPONENT)
        probs_ref[n] = (raised * (1.0 / jnp.sum(raised, axis=0, keepdims=True))).astype(jnp.bfloat16)
    for c, lanes, n in everything:
        rows = slice(c * per, (c + 1) * per)
        values = jnp.concatenate([values_ref[rows, lanes], more[rows, lanes]], axis=0)
        mixed = lax.dot_general(
            probs_ref[n], values, (((0,), (0,)), ((), ())), preferred_element_type=jnp.float32
        ).astype(out_ref.dtype)
        own = [mixed[h * SPAN : (h + 1) * SPAN, h * HD : (h + 1) * HD] for h in range(PAIR)]
        out_ref[c * SPAN : (c + 1) * SPAN, lanes] = jnp.concatenate(own, axis=1)


def attend(other, w_key, w_value, queries, first, values, spans):
    each = scores_shape(other, queries, w_key.shape[0], spans)
    return pl.pallas_call(
        functools.partial(attend_kernel, spans),
        out_shape=jax.ShapeDtypeStruct(queries.shape, queries.dtype),
        in_specs=[VMEM] * 6,
        out_specs=VMEM,
        scratch_shapes=[pltpu.VMEM(each, jnp.float32), pltpu.VMEM((each[0], 2 * each[1], each[2]), jnp.bfloat16)],
        compiler_params=params(),
    )(other, w_key, w_value, queries, first, values)


def send(chunk, pairs):
    return lax.ppermute(chunk, "wide", pairs)


def gathered_plan(queries, encodings, w_key, w_value, block_owner, block_row):
    wide_count = lax.axis_size("wide")
    turns = wide_count // SIDE
    rows = encodings.shape[0]
    spans = queries.shape[0] // SPAN
    line = ring_order(turns)
    onward = [
        (here * SIDE + x, there * SIDE + x) for here, there in zip(line, line[1:] + line[:1]) for x in range(SIDE)
    ]
    across = [(n, n + 1 if n % SIDE == 0 else n - 1) for n in range(wide_count)]
    *pieces, whole = half_columns(encodings)
    order = [(0, 0)]
    for k in range(1, turns):
        order += [(k, 0), (k - 1, 1)]
    order.append((turns - 1, 1))
    index = places(order, turns, rows, jnp.transpose(block_owner, (0, 2, 1)), block_row)
    held = {(0, 0): pieces}
    for k in range(1, turns):
        behind = held[k - 1, 0]
        steps = [send(piece, onward) for piece in behind]
        held[k - 1, 1] = [send(whole if k == 1 else jnp.concatenate(behind, axis=1), across)]
        held[k, 0] = steps
    held[turns - 1, 1] = [send(piece, across) for piece in held[turns - 1, 0]]
    late = 3
    sources = [held[chunk] for chunk in order]
    begun = early(index, sources[:-late], whole.shape[1])
    picked = pick(index, begun, sources[-late:], (len(order) - late) * rows)
    other = lax.ppermute(picked, "heads", [(0, 1), (1, 0)])
    first = own_scores(picked, w_key, queries, spans)
    values = own_values(picked, w_value, spans)
    return attend(other, w_key, w_value, queries, first, values, spans)


def exchange(encodings, owners, stored, capacity):
    wide_count = lax.axis_size("wide")
    requests = owners.shape[0]
    order = jnp.arange(requests, dtype=jnp.int32)
    earlier = (owners[:, None] == owners[None, :]) & (order[None, :] < order[:, None])
    rank = jnp.sum(earlier.astype(jnp.int32), axis=1)
    slot = owners * capacity + rank
    table = jnp.full((wide_count * capacity,), -1, jnp.int32).at[slot].set(stored)
    table = table.reshape(wide_count, capacity)
    asked = lax.all_to_all(table, "wide", split_axis=0, concat_axis=0, tiled=True)
    wanted = jnp.maximum(asked, 0)
    picked = encodings[wanted]
    returned = lax.all_to_all(picked, "wide", split_axis=0, concat_axis=0, tiled=True)
    return returned.reshape(wide_count * capacity, encodings.shape[1])[slot]


def exchanged_plan(queries, encodings, w_key, w_value, owners, stored, capacity):
    fetched = exchange(encodings, owners, stored, capacity)
    channels = w_key.shape[0]
    source = fetched.reshape(-1, channels)
    keys = jnp.dot(source, w_key, preferred_element_type=jnp.float32).astype(jnp.bfloat16)
    values = jnp.dot(source, w_value, preferred_element_type=jnp.float32).astype(jnp.bfloat16)
    span_count = queries.shape[0] // SPAN
    heads_local = w_key.shape[1] // HD
    keys = keys.reshape(span_count, -1, heads_local, HD)
    values = values.reshape(span_count, -1, heads_local, HD)
    query_part = queries.reshape(span_count, SPAN, heads_local, HD)
    scores = jnp.einsum(
        "cqhd,ckhd->chqk", query_part, keys, preferred_element_type=jnp.float32
    ) * HD ** (-0.5)
    probs = jax.nn.softmax(scores, axis=-1).astype(jnp.bfloat16)
    mixed = jnp.einsum("chqk,ckhd->cqhd", probs, values, preferred_element_type=jnp.float32)
    return mixed.astype(jnp.bfloat16).reshape(queries.shape)


def on_device(queries, encodings, w_key, w_value, block_owner, block_row):
    wide_count = lax.axis_size("wide")
    requests = block_row.size
    capacity = 2 * ((requests + wide_count - 1) // wide_count)
    if encodings.shape[0] <= 2 * capacity:
        return gathered_plan(queries, encodings, w_key, w_value, block_owner, block_row)
    return exchanged_plan(
        queries, encodings, w_key, w_value, block_owner.reshape(-1), block_row.reshape(-1), capacity
    )


def solution(mesh):
    placed = (
        P(("groups", "wide"), "heads"),
        P(("groups", "wide"), None),
        P(None, "heads"),
        P(None, "heads"),
        P(("groups", "wide"), None, None),
        P(("groups", "wide"), None),
    )
    return jax.shard_map(
        on_device,
        mesh=mesh,
        in_specs=placed,
        out_specs=P(("groups", "wide"), "heads"),
        check_vma=False,
    )
```

```python
import functools

import jax
import jax.numpy as jnp
from jax import lax
from jax.experimental import pallas as pl
from jax.experimental.pallas import tpu as pltpu
from jax.sharding import PartitionSpec as P

HD = 128
SPAN = 64
SIDE = 2
LIMIT = 24 * 1024 * 1024
STREAMS = 2
EXPONENT = HD ** (-0.5) * 1.4426950408889634
VMEM = pl.BlockSpec(memory_space=pltpu.VMEM)


def params():
    return pltpu.CompilerParams(vmem_limit_bytes=LIMIT)


def half_kernel(enc_ref, *refs):
    outs, sems = refs[:-1], refs[-1]
    first = lax.axis_index("heads") * outs[-1].shape[1]
    copies = []
    for n, out in enumerate(outs):
        width = out.shape[1]
        start = first + (n * width if n < STREAMS else 0)
        copies.append(pltpu.make_async_copy(enc_ref.at[:, pl.ds(pl.multiple_of(start, 128), width)], out, sems.at[n]))
    for copy in copies:
        copy.start()
    for copy in copies:
        copy.wait()


def half_columns(encodings):
    rows, columns = encodings.shape
    whole = columns // lax.axis_size("heads")
    widths = [whole // STREAMS] * STREAMS + [whole]
    return pl.pallas_call(
        half_kernel,
        out_shape=[jax.ShapeDtypeStruct((rows, width), encodings.dtype) for width in widths],
        in_specs=[VMEM],
        out_specs=[VMEM] * len(widths),
        scratch_shapes=[pltpu.SemaphoreType.DMA((len(widths),))],
        compiler_params=params(),
    )(encodings)


def chosen_rows(index, sources, first):
    held = jnp.concatenate(sources, axis=0)
    places = lax.broadcasted_iota(jnp.int32, (index.shape[0], held.shape[0]), 1) + first
    chosen = jnp.where(places == index, 1.0, 0.0).astype(held.dtype)
    return jnp.dot(chosen, held, preferred_element_type=jnp.float32)


def ring_order(turns):
    return [0] + list(range(1, turns, 2)) + list(range(turns - 2 + turns % 2, 0, -2))


def ring_place(line, turns):
    return jnp.where(line % 2 == 1, (line + 1) // 2, jnp.where(line == 0, 0, turns - line // 2))


def wanted_rows(order, turns, rows, owner_ref, stored_ref):
    me = lax.axis_index("wide")
    columns = []
    for c in range(stored_ref.shape[0]):
        owner, stored = owner_ref[c], stored_ref[c : c + 1, :]
        back = ring_place(me // SIDE, turns) - ring_place(owner // SIDE, turns)
        back = jnp.where(back < 0, back + turns, back)
        beside = jnp.where(owner % SIDE == me % SIDE, 0, 1)
        place = jnp.zeros_like(stored)
        for n, chunk in enumerate(order):
            place = jnp.where(back * 2 + beside == chunk[0] * 2 + chunk[1], n, place)
        place = place * rows + stored
        square = (place.shape[1], place.shape[1])
        own = lax.broadcasted_iota(jnp.int32, square, 0) == lax.broadcasted_iota(jnp.int32, square, 1)
        spread = jnp.where(own, jnp.broadcast_to(place.astype(jnp.float32), square), 0.0)
        columns.append(jnp.sum(spread, axis=1, keepdims=True))
    return jnp.concatenate(columns, axis=0).astype(jnp.int32)


def places_kernel(order, turns, rows, owner_ref, stored_ref, index_ref):
    index_ref[...] = wanted_rows(order, turns, rows, owner_ref, stored_ref)


def places(order, turns, rows, owners, stored):
    return pl.pallas_call(
        functools.partial(places_kernel, order, turns, rows),
        out_shape=jax.ShapeDtypeStruct((stored.size, 1), jnp.int32),
        in_specs=[VMEM] * 2,
        out_specs=VMEM,
        compiler_params=params(),
    )(owners, stored)


def early_kernel(chunks, index_ref, *refs):
    sources, outs = refs[:-STREAMS], refs[-STREAMS:]
    starts = [sum(chunks[:n]) for n in range(len(chunks))]
    for n, out in enumerate(outs):
        lanes = slice(n * out.shape[1], (n + 1) * out.shape[1])
        held = [
            sources[at + n][...] if arrays > 1 else sources[at][:, lanes] for at, arrays in zip(starts, chunks)
        ]
        out[...] = chosen_rows(index_ref[...], held, 0).astype(out.dtype)


def early(index, sources, width):
    rows = sources[0][0].shape[0]
    requests = index.shape[0]
    arrays = [array for chunk in sources for array in chunk]
    return pl.pallas_call(
        functools.partial(early_kernel, [len(chunk) for chunk in sources]),
        out_shape=[jax.ShapeDtypeStruct((requests, width // STREAMS), arrays[0].dtype)] * STREAMS,
        in_specs=[VMEM] * (1 + len(arrays)),
        out_specs=[VMEM] * STREAMS,
        compiler_params=params(),
        cost_estimate=pl.CostEstimate(
            flops=2 * requests * width * rows * len(sources),
            bytes_accessed=2 * requests * width,
            transcendentals=0,
        ),
    )(index, *arrays)


def pick_kernel(first, index_ref, begun_ref, last_ref, out_ref):
    picked = chosen_rows(index_ref[...], [last_ref[...]], first)
    out_ref[...] = (picked + begun_ref[...].astype(jnp.float32)).astype(out_ref.dtype)


def pick(index, begun, last, first):
    return pl.pallas_call(
        functools.partial(pick_kernel, first),
        out_shape=jax.ShapeDtypeStruct(begun.shape, begun.dtype),
        in_specs=[VMEM] * 3,
        out_specs=VMEM,
        compiler_params=params(),
    )(index, begun, last)


def by_span(picked, spans, channels):
    per = picked[0].shape[0] // spans
    parts = []
    for c in range(spans):
        for array in picked:
            for t in range(array.shape[1] // channels):
                parts.append(array[c * per : (c + 1) * per, t * channels : (t + 1) * channels])
    return jnp.concatenate(parts, axis=0)


PAIR = 2


def pair_places(spans, columns):
    pairs = columns // (PAIR * HD)
    return [
        (c, slice(p * PAIR * HD, (p + 1) * PAIR * HD), c * pairs + p) for c in range(spans) for p in range(pairs)
    ]


def apart(query):
    none = jnp.zeros((query.shape[0], HD), query.dtype)
    upper = jnp.concatenate([query[:, :HD], none], axis=1)
    lower = jnp.concatenate([none, query[:, HD:]], axis=1)
    return jnp.concatenate([upper, lower], axis=0)


def score(spans, source, wk_ref, query_ref, scores_ref):
    keys = jnp.dot(source, wk_ref[...], preferred_element_type=jnp.float32).astype(jnp.bfloat16)
    per = keys.shape[0] // spans
    for c, lanes, n in pair_places(spans, keys.shape[1]):
        scores_ref[n] = lax.dot_general(
            keys[c * per : (c + 1) * per, lanes],
            apart(query_ref[c * SPAN : (c + 1) * SPAN, lanes]),
            (((1,), (1,)), ((), ())),
            preferred_element_type=jnp.float32,
        )


def score_kernel(spans, *refs):
    *picked, wk_ref, query_ref, scores_ref = refs
    score(spans, by_span(picked, spans, wk_ref.shape[0]), wk_ref, query_ref, scores_ref)


def tokens(picked, channels):
    return sum(array.size for array in picked) // channels


def scores_shape(picked, queries, channels, spans):
    return spans * (queries.shape[1] // (PAIR * HD)), tokens(picked, channels) // spans, PAIR * SPAN


def own_scores(picked, w_key, queries, spans):
    return pl.pallas_call(
        functools.partial(score_kernel, spans),
        out_shape=jax.ShapeDtypeStruct(scores_shape(picked, queries, w_key.shape[0], spans), jnp.float32),
        in_specs=[VMEM] * (2 + len(picked)),
        out_specs=VMEM,
        compiler_params=params(),
    )(*picked, w_key, queries)


def values_kernel(spans, *refs):
    *picked, wv_ref, values_ref = refs
    source = by_span(picked, spans, wv_ref.shape[0])
    values_ref[...] = jnp.dot(source, wv_ref[...], preferred_element_type=jnp.float32).astype(values_ref.dtype)


def own_values(picked, w_value, spans):
    return pl.pallas_call(
        functools.partial(values_kernel, spans),
        out_shape=jax.ShapeDtypeStruct((tokens(picked, w_value.shape[0]), w_value.shape[1]), picked[0].dtype),
        in_specs=[VMEM] * (1 + len(picked)),
        out_specs=VMEM,
        compiler_params=params(),
    )(*picked, w_value)


def attend_kernel(spans, *refs):
    *others, wk_ref, wv_ref, query_ref, first_ref, values_ref, out_ref, second_ref, probs_ref, held_ref, sems = refs
    other = by_span(others, spans, wk_ref.shape[0])
    score(spans, other, wk_ref, query_ref, second_ref)
    per = other.shape[0] // spans
    more = jnp.dot(other, wv_ref[...], preferred_element_type=jnp.float32).astype(jnp.bfloat16)
    everything = pair_places(spans, more.shape[1])
    for c, lanes, n in everything:
        scores = jnp.concatenate([first_ref[n], second_ref[n]], axis=0)
        raised = jnp.exp2((scores - jnp.max(scores, axis=0, keepdims=True)) * EXPONENT)
        probs_ref[n] = (raised * (1.0 / jnp.sum(raised, axis=0, keepdims=True))).astype(jnp.bfloat16)
    copies = []
    for c in range(spans):
        here = pl.ds(c * SPAN, SPAN)
        for at, lanes, n in everything:
            if at != c:
                continue
            rows = slice(c * per, (c + 1) * per)
            values = jnp.concatenate([values_ref[rows, lanes], more[rows, lanes]], axis=0)
            mixed = lax.dot_general(
                probs_ref[n], values, (((0,), (0,)), ((), ())), preferred_element_type=jnp.float32
            ).astype(out_ref.dtype)
            own = [mixed[h * SPAN : (h + 1) * SPAN, h * HD : (h + 1) * HD] for h in range(PAIR)]
            held_ref[here, lanes] = jnp.concatenate(own, axis=1)
        copies.append(pltpu.make_async_copy(held_ref.at[here, :], out_ref.at[here, :], sems.at[c]))
        copies[-1].start()
    for copy in copies:
        copy.wait()


def attend(others, w_key, w_value, queries, first, values, spans):
    each = scores_shape(others, queries, w_key.shape[0], spans)
    return pl.pallas_call(
        functools.partial(attend_kernel, spans),
        out_shape=jax.ShapeDtypeStruct(queries.shape, queries.dtype),
        in_specs=[VMEM] * (5 + len(others)),
        out_specs=pl.BlockSpec(memory_space=pl.ANY),
        scratch_shapes=[
            pltpu.VMEM(each, jnp.float32),
            pltpu.VMEM((each[0], 2 * each[1], each[2]), jnp.bfloat16),
            pltpu.VMEM(queries.shape, queries.dtype),
            pltpu.SemaphoreType.DMA((spans,)),
        ],
        compiler_params=params(),
    )(*others, w_key, w_value, queries, first, values)


def send(chunk, pairs):
    return lax.ppermute(chunk, "wide", pairs)


def gathered_plan(queries, encodings, w_key, w_value, block_owner, block_row):
    wide_count = lax.axis_size("wide")
    turns = wide_count // SIDE
    rows = encodings.shape[0]
    spans = queries.shape[0] // SPAN
    line = ring_order(turns)
    onward = [
        (here * SIDE + x, there * SIDE + x) for here, there in zip(line, line[1:] + line[:1]) for x in range(SIDE)
    ]
    across = [(n, n + 1 if n % SIDE == 0 else n - 1) for n in range(wide_count)]
    *pieces, whole = half_columns(encodings)
    order = [(0, 0)]
    for k in range(1, turns):
        order += [(k, 0), (k - 1, 1)]
    order.append((turns - 1, 1))
    index = places(order, turns, rows, jnp.transpose(block_owner, (0, 2, 1)), block_row)
    held = {(0, 0): pieces}
    for k in range(1, turns):
        behind = held[k - 1, 0]
        steps = [send(piece, onward) for piece in behind]
        if k < turns - 1:
            held[k - 1, 1] = [send(whole if k == 1 else jnp.concatenate(behind, axis=1), across)]
        else:
            held[k - 1, 1] = [send(piece, across) for piece in behind]
        held[k, 0] = steps
    held[turns - 1, 1] = [send(piece, across) for piece in held[turns - 1, 0]]
    sources = [held[chunk] for chunk in order]
    begun = early(index, sources[:-1], whole.shape[1])
    picked = [pick(index, *pieces, (len(order) - 1) * rows) for pieces in zip(begun, sources[-1])]
    others = [lax.ppermute(piece, "heads", [(0, 1), (1, 0)]) for piece in picked]
    first = own_scores(picked, w_key, queries, spans)
    values = own_values(picked, w_value, spans)
    return attend(others, w_key, w_value, queries, first, values, spans)


def exchange(encodings, owners, stored, capacity):
    wide_count = lax.axis_size("wide")
    requests = owners.shape[0]
    order = jnp.arange(requests, dtype=jnp.int32)
    earlier = (owners[:, None] == owners[None, :]) & (order[None, :] < order[:, None])
    rank = jnp.sum(earlier.astype(jnp.int32), axis=1)
    slot = owners * capacity + rank
    table = jnp.full((wide_count * capacity,), -1, jnp.int32).at[slot].set(stored)
    table = table.reshape(wide_count, capacity)
    asked = lax.all_to_all(table, "wide", split_axis=0, concat_axis=0, tiled=True)
    wanted = jnp.maximum(asked, 0)
    picked = encodings[wanted]
    returned = lax.all_to_all(picked, "wide", split_axis=0, concat_axis=0, tiled=True)
    return returned.reshape(wide_count * capacity, encodings.shape[1])[slot]


def exchanged_plan(queries, encodings, w_key, w_value, owners, stored, capacity):
    fetched = exchange(encodings, owners, stored, capacity)
    channels = w_key.shape[0]
    source = fetched.reshape(-1, channels)
    keys = jnp.dot(source, w_key, preferred_element_type=jnp.float32).astype(jnp.bfloat16)
    values = jnp.dot(source, w_value, preferred_element_type=jnp.float32).astype(jnp.bfloat16)
    span_count = queries.shape[0] // SPAN
    heads_local = w_key.shape[1] // HD
    keys = keys.reshape(span_count, -1, heads_local, HD)
    values = values.reshape(span_count, -1, heads_local, HD)
    query_part = queries.reshape(span_count, SPAN, heads_local, HD)
    scores = jnp.einsum(
        "cqhd,ckhd->chqk", query_part, keys, preferred_element_type=jnp.float32
    ) * HD ** (-0.5)
    probs = jax.nn.softmax(scores, axis=-1).astype(jnp.bfloat16)
    mixed = jnp.einsum("chqk,ckhd->cqhd", probs, values, preferred_element_type=jnp.float32)
    return mixed.astype(jnp.bfloat16).reshape(queries.shape)


def on_device(queries, encodings, w_key, w_value, block_owner, block_row):
    wide_count = lax.axis_size("wide")
    requests = block_row.size
    capacity = 2 * ((requests + wide_count - 1) // wide_count)
    if encodings.shape[0] <= 2 * capacity:
        return gathered_plan(queries, encodings, w_key, w_value, block_owner, block_row)
    return exchanged_plan(
        queries, encodings, w_key, w_value, block_owner.reshape(-1), block_row.reshape(-1), capacity
    )


def solution(mesh):
    placed = (
        P(("groups", "wide"), "heads"),
        P(("groups", "wide"), None),
        P(None, "heads"),
        P(None, "heads"),
        P(("groups", "wide"), None, None),
        P(("groups", "wide"), None),
    )
    return jax.shard_map(
        on_device,
        mesh=mesh,
        in_specs=placed,
        out_specs=P(("groups", "wide"), "heads"),
        check_vma=False,
    )
```

```python
import functools

import jax
import jax.numpy as jnp
from jax import lax
from jax.experimental import pallas as pl
from jax.experimental.pallas import tpu as pltpu
from jax.sharding import PartitionSpec as P

HD = 128
SPAN = 64
SIDE = 2
LIMIT = 24 * 1024 * 1024
STREAMS = 2
EXPONENT = HD ** (-0.5) * 1.4426950408889634
VMEM = pl.BlockSpec(memory_space=pltpu.VMEM)


def params():
    return pltpu.CompilerParams(vmem_limit_bytes=LIMIT)


def half_kernel(enc_ref, *refs):
    outs, sems = refs[:-1], refs[-1]
    first = lax.axis_index("heads") * outs[-1].shape[1]
    copies = []
    for n, out in enumerate(outs):
        width = out.shape[1]
        start = first + (n * width if n < STREAMS else 0)
        copies.append(pltpu.make_async_copy(enc_ref.at[:, pl.ds(pl.multiple_of(start, 128), width)], out, sems.at[n]))
    for copy in copies:
        copy.start()
    for copy in copies:
        copy.wait()


def half_columns(encodings):
    rows, columns = encodings.shape
    whole = columns // lax.axis_size("heads")
    widths = [whole // STREAMS] * STREAMS + [whole]
    return pl.pallas_call(
        half_kernel,
        out_shape=[jax.ShapeDtypeStruct((rows, width), encodings.dtype) for width in widths],
        in_specs=[VMEM],
        out_specs=[VMEM] * len(widths),
        scratch_shapes=[pltpu.SemaphoreType.DMA((len(widths),))],
        compiler_params=params(),
    )(encodings)


def chosen_rows(index, sources, first):
    held = jnp.concatenate(sources, axis=0)
    places = lax.broadcasted_iota(jnp.int32, (index.shape[0], held.shape[0]), 1) + first
    chosen = jnp.where(places == index, 1.0, 0.0).astype(held.dtype)
    return jnp.dot(chosen, held, preferred_element_type=jnp.float32)


def ring_order(turns):
    return [0] + list(range(1, turns, 2)) + list(range(turns - 2 + turns % 2, 0, -2))


def ring_place(line, turns):
    return jnp.where(line % 2 == 1, (line + 1) // 2, jnp.where(line == 0, 0, turns - line // 2))


def wanted_rows(order, turns, rows, owner_ref, stored_ref):
    me = lax.axis_index("wide")
    columns = []
    for c in range(stored_ref.shape[0]):
        owner, stored = owner_ref[c], stored_ref[c : c + 1, :]
        back = ring_place(me // SIDE, turns) - ring_place(owner // SIDE, turns)
        back = jnp.where(back < 0, back + turns, back)
        beside = jnp.where(owner % SIDE == me % SIDE, 0, 1)
        place = jnp.zeros_like(stored)
        for n, chunk in enumerate(order):
            place = jnp.where(back * 2 + beside == chunk[0] * 2 + chunk[1], n, place)
        place = place * rows + stored
        square = (place.shape[1], place.shape[1])
        own = lax.broadcasted_iota(jnp.int32, square, 0) == lax.broadcasted_iota(jnp.int32, square, 1)
        spread = jnp.where(own, jnp.broadcast_to(place.astype(jnp.float32), square), 0.0)
        columns.append(jnp.sum(spread, axis=1, keepdims=True))
    return jnp.concatenate(columns, axis=0).astype(jnp.int32)


def places_kernel(order, turns, rows, owner_ref, stored_ref, index_ref):
    index_ref[...] = wanted_rows(order, turns, rows, owner_ref, stored_ref)


def places(order, turns, rows, owners, stored):
    return pl.pallas_call(
        functools.partial(places_kernel, order, turns, rows),
        out_shape=jax.ShapeDtypeStruct((stored.size, 1), jnp.int32),
        in_specs=[VMEM] * 2,
        out_specs=VMEM,
        compiler_params=params(),
    )(owners, stored)


def early_kernel(chunks, index_ref, *refs):
    sources, outs = refs[:-STREAMS], refs[-STREAMS:]
    starts = [sum(chunks[:n]) for n in range(len(chunks))]
    for n, out in enumerate(outs):
        lanes = slice(n * out.shape[1], (n + 1) * out.shape[1])
        held = [
            sources[at + n][...] if arrays > 1 else sources[at][:, lanes] for at, arrays in zip(starts, chunks)
        ]
        out[...] = chosen_rows(index_ref[...], held, 0).astype(out.dtype)


def early(index, sources, width):
    rows = sources[0][0].shape[0]
    requests = index.shape[0]
    arrays = [array for chunk in sources for array in chunk]
    return pl.pallas_call(
        functools.partial(early_kernel, [len(chunk) for chunk in sources]),
        out_shape=[jax.ShapeDtypeStruct((requests, width // STREAMS), arrays[0].dtype)] * STREAMS,
        in_specs=[VMEM] * (1 + len(arrays)),
        out_specs=[VMEM] * STREAMS,
        compiler_params=params(),
        cost_estimate=pl.CostEstimate(
            flops=2 * requests * width * rows * len(sources),
            bytes_accessed=2 * requests * width,
            transcendentals=0,
        ),
    )(index, *arrays)


def pick_kernel(first, index_ref, begun_ref, last_ref, out_ref):
    picked = chosen_rows(index_ref[...], [last_ref[...]], first)
    out_ref[...] = (picked + begun_ref[...].astype(jnp.float32)).astype(out_ref.dtype)


def pick(index, begun, last, first):
    return pl.pallas_call(
        functools.partial(pick_kernel, first),
        out_shape=jax.ShapeDtypeStruct(begun.shape, begun.dtype),
        in_specs=[VMEM] * 3,
        out_specs=VMEM,
        compiler_params=params(),
    )(index, begun, last)


def by_span(picked, spans, channels):
    per = picked[0].shape[0] // spans
    parts = []
    for c in range(spans):
        for array in picked:
            for t in range(array.shape[1] // channels):
                parts.append(array[c * per : (c + 1) * per, t * channels : (t + 1) * channels])
    return jnp.concatenate(parts, axis=0)


PAIR = 2


def pair_places(spans, columns):
    pairs = columns // (PAIR * HD)
    return [
        (c, slice(p * PAIR * HD, (p + 1) * PAIR * HD), c * pairs + p) for c in range(spans) for p in range(pairs)
    ]


def apart(query):
    none = jnp.zeros((query.shape[0], HD), query.dtype)
    upper = jnp.concatenate([query[:, :HD], none], axis=1)
    lower = jnp.concatenate([none, query[:, HD:]], axis=1)
    return jnp.concatenate([upper, lower], axis=0)


def score(spans, source, wk_ref, query_ref, scores_ref):
    keys = jnp.dot(source, wk_ref[...], preferred_element_type=jnp.float32).astype(jnp.bfloat16)
    per = keys.shape[0] // spans
    for c, lanes, n in pair_places(spans, keys.shape[1]):
        scores_ref[n] = lax.dot_general(
            keys[c * per : (c + 1) * per, lanes],
            apart(query_ref[c * SPAN : (c + 1) * SPAN, lanes]),
            (((1,), (1,)), ((), ())),
            preferred_element_type=jnp.float32,
        )


def score_kernel(spans, *refs):
    *picked, wk_ref, query_ref, scores_ref = refs
    score(spans, by_span(picked, spans, wk_ref.shape[0]), wk_ref, query_ref, scores_ref)


def tokens(picked, channels):
    return sum(array.size for array in picked) // channels


def scores_shape(picked, queries, channels, spans):
    return spans * (queries.shape[1] // (PAIR * HD)), tokens(picked, channels) // spans, PAIR * SPAN


def own_scores(picked, w_key, queries, spans):
    return pl.pallas_call(
        functools.partial(score_kernel, spans),
        out_shape=jax.ShapeDtypeStruct(scores_shape(picked, queries, w_key.shape[0], spans), jnp.float32),
        in_specs=[VMEM] * (2 + len(picked)),
        out_specs=VMEM,
        compiler_params=params(),
    )(*picked, w_key, queries)


def values_kernel(spans, *refs):
    *picked, wv_ref, values_ref = refs
    source = by_span(picked, spans, wv_ref.shape[0])
    values_ref[...] = jnp.dot(source, wv_ref[...], preferred_element_type=jnp.float32).astype(values_ref.dtype)


def own_values(picked, w_value, spans):
    return pl.pallas_call(
        functools.partial(values_kernel, spans),
        out_shape=jax.ShapeDtypeStruct((tokens(picked, w_value.shape[0]), w_value.shape[1]), picked[0].dtype),
        in_specs=[VMEM] * (1 + len(picked)),
        out_specs=VMEM,
        compiler_params=params(),
    )(*picked, w_value)


def attend_kernel(spans, *refs):
    *others, wk_ref, wv_ref, query_ref, first_ref, values_ref, out_ref, second_ref, probs_ref, held_ref, sems = refs
    other = by_span(others, spans, wk_ref.shape[0])
    score(spans, other, wk_ref, query_ref, second_ref)
    per = other.shape[0] // spans
    more = jnp.dot(other, wv_ref[...], preferred_element_type=jnp.float32).astype(jnp.bfloat16)
    everything = pair_places(spans, more.shape[1])
    for c, lanes, n in everything:
        scores = jnp.concatenate([first_ref[n], second_ref[n]], axis=0)
        raised = jnp.exp2((scores - jnp.max(scores, axis=0, keepdims=True)) * EXPONENT)
        probs_ref[n] = (raised * (1.0 / jnp.sum(raised, axis=0, keepdims=True))).astype(jnp.bfloat16)
    copies = []
    for c in range(spans):
        here = pl.ds(c * SPAN, SPAN)
        for at, lanes, n in everything:
            if at != c:
                continue
            rows = slice(c * per, (c + 1) * per)
            values = jnp.concatenate([values_ref[rows, lanes], more[rows, lanes]], axis=0)
            mixed = lax.dot_general(
                probs_ref[n], values, (((0,), (0,)), ((), ())), preferred_element_type=jnp.float32
            ).astype(out_ref.dtype)
            own = [mixed[h * SPAN : (h + 1) * SPAN, h * HD : (h + 1) * HD] for h in range(PAIR)]
            held_ref[here, lanes] = jnp.concatenate(own, axis=1)
        copies.append(pltpu.make_async_copy(held_ref.at[here, :], out_ref.at[here, :], sems.at[c]))
        copies[-1].start()
    for copy in copies:
        copy.wait()


def attend(others, w_key, w_value, queries, first, values, spans):
    each = scores_shape(others, queries, w_key.shape[0], spans)
    return pl.pallas_call(
        functools.partial(attend_kernel, spans),
        out_shape=jax.ShapeDtypeStruct(queries.shape, queries.dtype),
        in_specs=[VMEM] * (5 + len(others)),
        out_specs=pl.BlockSpec(memory_space=pl.ANY),
        scratch_shapes=[
            pltpu.VMEM(each, jnp.float32),
            pltpu.VMEM((each[0], 2 * each[1], each[2]), jnp.bfloat16),
            pltpu.VMEM(queries.shape, queries.dtype),
            pltpu.SemaphoreType.DMA((spans,)),
        ],
        compiler_params=params(),
    )(*others, w_key, w_value, queries, first, values)


def send(chunk, pairs):
    return lax.ppermute(chunk, "wide", pairs)


def gathered_plan(queries, encodings, w_key, w_value, block_owner, block_row):
    wide_count = lax.axis_size("wide")
    turns = wide_count // SIDE
    rows = encodings.shape[0]
    spans = queries.shape[0] // SPAN
    line = ring_order(turns)
    onward = [
        (here * SIDE + x, there * SIDE + x) for here, there in zip(line, line[1:] + line[:1]) for x in range(SIDE)
    ]
    across = [(n, n + 1 if n % SIDE == 0 else n - 1) for n in range(wide_count)]
    *pieces, whole = half_columns(encodings)
    order = [(0, 0)]
    for k in range(1, turns):
        order += [(k, 0), (k - 1, 1)]
    order.append((turns - 1, 1))
    index = places(order, turns, rows, jnp.transpose(block_owner, (0, 2, 1)), block_row)
    held = {(0, 0): pieces}
    for k in range(1, turns):
        behind = held[k - 1, 0]
        steps = [send(piece, onward) for piece in behind]
        if k < turns - 1:
            held[k - 1, 1] = [send(whole if k == 1 else jnp.concatenate(behind, axis=1), across)]
        else:
            held[k - 1, 1] = [send(piece, across) for piece in behind]
        held[k, 0] = steps
    held[turns - 1, 1] = [send(piece, across) for piece in held[turns - 1, 0]]
    sources = [held[chunk] for chunk in order]
    begun = early(index, sources[:-1], whole.shape[1])
    picked = [pick(index, *pieces, (len(order) - 1) * rows) for pieces in zip(begun[::-1], sources[-1][::-1])]
    others = [lax.ppermute(piece, "heads", [(0, 1), (1, 0)]) for piece in picked]
    first = own_scores(picked, w_key, queries, spans)
    values = own_values(picked, w_value, spans)
    return attend(others, w_key, w_value, queries, first, values, spans)


def exchange(encodings, owners, stored, capacity):
    wide_count = lax.axis_size("wide")
    requests = owners.shape[0]
    order = jnp.arange(requests, dtype=jnp.int32)
    earlier = (owners[:, None] == owners[None, :]) & (order[None, :] < order[:, None])
    rank = jnp.sum(earlier.astype(jnp.int32), axis=1)
    slot = owners * capacity + rank
    table = jnp.full((wide_count * capacity,), -1, jnp.int32).at[slot].set(stored)
    table = table.reshape(wide_count, capacity)
    asked = lax.all_to_all(table, "wide", split_axis=0, concat_axis=0, tiled=True)
    wanted = jnp.maximum(asked, 0)
    picked = encodings[wanted]
    returned = lax.all_to_all(picked, "wide", split_axis=0, concat_axis=0, tiled=True)
    return returned.reshape(wide_count * capacity, encodings.shape[1])[slot]


def exchanged_plan(queries, encodings, w_key, w_value, owners, stored, capacity):
    fetched = exchange(encodings, owners, stored, capacity)
    channels = w_key.shape[0]
    source = fetched.reshape(-1, channels)
    keys = jnp.dot(source, w_key, preferred_element_type=jnp.float32).astype(jnp.bfloat16)
    values = jnp.dot(source, w_value, preferred_element_type=jnp.float32).astype(jnp.bfloat16)
    span_count = queries.shape[0] // SPAN
    heads_local = w_key.shape[1] // HD
    keys = keys.reshape(span_count, -1, heads_local, HD)
    values = values.reshape(span_count, -1, heads_local, HD)
    query_part = queries.reshape(span_count, SPAN, heads_local, HD)
    scores = jnp.einsum(
        "cqhd,ckhd->chqk", query_part, keys, preferred_element_type=jnp.float32
    ) * HD ** (-0.5)
    probs = jax.nn.softmax(scores, axis=-1).astype(jnp.bfloat16)
    mixed = jnp.einsum("chqk,ckhd->cqhd", probs, values, preferred_element_type=jnp.float32)
    return mixed.astype(jnp.bfloat16).reshape(queries.shape)


def on_device(queries, encodings, w_key, w_value, block_owner, block_row):
    wide_count = lax.axis_size("wide")
    requests = block_row.size
    capacity = 2 * ((requests + wide_count - 1) // wide_count)
    if encodings.shape[0] <= 2 * capacity:
        return gathered_plan(queries, encodings, w_key, w_value, block_owner, block_row)
    return exchanged_plan(
        queries, encodings, w_key, w_value, block_owner.reshape(-1), block_row.reshape(-1), capacity
    )


def solution(mesh):
    placed = (
        P(("groups", "wide"), "heads"),
        P(("groups", "wide"), None),
        P(None, "heads"),
        P(None, "heads"),
        P(("groups", "wide"), None, None),
        P(("groups", "wide"), None),
    )
    return jax.shard_map(
        on_device,
        mesh=mesh,
        in_specs=placed,
        out_specs=P(("groups", "wide"), "heads"),
        check_vma=False,
    )
```

```python
import functools

import jax
import jax.numpy as jnp
from jax import lax
from jax.experimental import pallas as pl
from jax.experimental.pallas import tpu as pltpu
from jax.sharding import PartitionSpec as P

HD = 128
SPAN = 64
SIDE = 2
LIMIT = 24 * 1024 * 1024
STREAMS = 2
EXPONENT = HD ** (-0.5) * 1.4426950408889634
VMEM = pl.BlockSpec(memory_space=pltpu.VMEM)


def params():
    return pltpu.CompilerParams(vmem_limit_bytes=LIMIT)


def half_kernel(enc_ref, *refs):
    outs, sems = refs[:-1], refs[-1]
    first = lax.axis_index("heads") * outs[-1].shape[1]
    copies = []
    for n, out in enumerate(outs):
        width = out.shape[1]
        start = first + (n * width if n < STREAMS else 0)
        copies.append(pltpu.make_async_copy(enc_ref.at[:, pl.ds(pl.multiple_of(start, 128), width)], out, sems.at[n]))
    for copy in copies:
        copy.start()
    for copy in copies:
        copy.wait()


def half_columns(encodings):
    rows, columns = encodings.shape
    whole = columns // lax.axis_size("heads")
    widths = [whole // STREAMS] * STREAMS + [whole]
    return pl.pallas_call(
        half_kernel,
        out_shape=[jax.ShapeDtypeStruct((rows, width), encodings.dtype) for width in widths],
        in_specs=[VMEM],
        out_specs=[VMEM] * len(widths),
        scratch_shapes=[pltpu.SemaphoreType.DMA((len(widths),))],
        compiler_params=params(),
    )(encodings)


def chosen_rows(index, sources, first):
    held = jnp.concatenate(sources, axis=0)
    places = lax.broadcasted_iota(jnp.int32, (index.shape[0], held.shape[0]), 1) + first
    chosen = jnp.where(places == index, 1.0, 0.0).astype(held.dtype)
    return jnp.dot(chosen, held, preferred_element_type=jnp.float32)


def ring_order(turns):
    return [0] + list(range(1, turns, 2)) + list(range(turns - 2 + turns % 2, 0, -2))


def ring_place(line, turns):
    return jnp.where(line % 2 == 1, (line + 1) // 2, jnp.where(line == 0, 0, turns - line // 2))


def wanted_rows(order, turns, rows, owner_ref, stored_ref):
    me = lax.axis_index("wide")
    columns = []
    for c in range(stored_ref.shape[0]):
        owner, stored = owner_ref[c], stored_ref[c : c + 1, :]
        back = ring_place(me // SIDE, turns) - ring_place(owner // SIDE, turns)
        back = jnp.where(back < 0, back + turns, back)
        beside = jnp.where(owner % SIDE == me % SIDE, 0, 1)
        place = jnp.zeros_like(stored)
        for n, chunk in enumerate(order):
            place = jnp.where(back * 2 + beside == chunk[0] * 2 + chunk[1], n, place)
        place = place * rows + stored
        square = (place.shape[1], place.shape[1])
        own = lax.broadcasted_iota(jnp.int32, square, 0) == lax.broadcasted_iota(jnp.int32, square, 1)
        spread = jnp.where(own, jnp.broadcast_to(place.astype(jnp.float32), square), 0.0)
        columns.append(jnp.sum(spread, axis=1, keepdims=True))
    return jnp.concatenate(columns, axis=0).astype(jnp.int32)


def places_kernel(order, turns, rows, owner_ref, stored_ref, index_ref):
    index_ref[...] = wanted_rows(order, turns, rows, owner_ref, stored_ref)


def places(order, turns, rows, owners, stored):
    return pl.pallas_call(
        functools.partial(places_kernel, order, turns, rows),
        out_shape=jax.ShapeDtypeStruct((stored.size, 1), jnp.int32),
        in_specs=[VMEM] * 2,
        out_specs=VMEM,
        compiler_params=params(),
    )(owners, stored)


def early_kernel(chunks, index_ref, *refs):
    sources, outs = refs[:-STREAMS], refs[-STREAMS:]
    starts = [sum(chunks[:n]) for n in range(len(chunks))]
    for n, out in enumerate(outs):
        lanes = slice(n * out.shape[1], (n + 1) * out.shape[1])
        held = [
            sources[at + n][...] if arrays > 1 else sources[at][:, lanes] for at, arrays in zip(starts, chunks)
        ]
        out[...] = chosen_rows(index_ref[...], held, 0).astype(out.dtype)


def early(index, sources, width):
    rows = sources[0][0].shape[0]
    requests = index.shape[0]
    arrays = [array for chunk in sources for array in chunk]
    return pl.pallas_call(
        functools.partial(early_kernel, [len(chunk) for chunk in sources]),
        out_shape=[jax.ShapeDtypeStruct((requests, width // STREAMS), arrays[0].dtype)] * STREAMS,
        in_specs=[VMEM] * (1 + len(arrays)),
        out_specs=[VMEM] * STREAMS,
        compiler_params=params(),
        cost_estimate=pl.CostEstimate(
            flops=2 * requests * width * rows * len(sources),
            bytes_accessed=2 * requests * width,
            transcendentals=0,
        ),
    )(index, *arrays)


def pick_kernel(first, index_ref, begun_ref, last_ref, out_ref):
    picked = chosen_rows(index_ref[...], [last_ref[...]], first)
    out_ref[...] = (picked + begun_ref[...].astype(jnp.float32)).astype(out_ref.dtype)


def pick(index, begun, last, first):
    return pl.pallas_call(
        functools.partial(pick_kernel, first),
        out_shape=jax.ShapeDtypeStruct(begun.shape, begun.dtype),
        in_specs=[VMEM] * 3,
        out_specs=VMEM,
        compiler_params=params(),
    )(index, begun, last)


def by_span(picked, spans, channels):
    per = picked[0].shape[0] // spans
    parts = []
    for c in range(spans):
        for array in picked:
            for t in range(array.shape[1] // channels):
                parts.append(array[c * per : (c + 1) * per, t * channels : (t + 1) * channels])
    return jnp.concatenate(parts, axis=0)


PAIR = 2


def pair_places(spans, columns):
    pairs = columns // (PAIR * HD)
    return [
        (c, slice(p * PAIR * HD, (p + 1) * PAIR * HD), c * pairs + p) for c in range(spans) for p in range(pairs)
    ]


def apart(query):
    none = jnp.zeros((query.shape[0], HD), query.dtype)
    upper = jnp.concatenate([query[:, :HD], none], axis=1)
    lower = jnp.concatenate([none, query[:, HD:]], axis=1)
    return jnp.concatenate([upper, lower], axis=0)


def score(spans, source, wk_ref, query_ref, scores_ref):
    keys = jnp.dot(source, wk_ref[...], preferred_element_type=jnp.float32).astype(jnp.bfloat16)
    per = keys.shape[0] // spans
    for c, lanes, n in pair_places(spans, keys.shape[1]):
        scores_ref[n] = lax.dot_general(
            keys[c * per : (c + 1) * per, lanes],
            apart(query_ref[c * SPAN : (c + 1) * SPAN, lanes]),
            (((1,), (1,)), ((), ())),
            preferred_element_type=jnp.float32,
        )


def score_kernel(spans, *refs):
    *picked, wk_ref, query_ref, scores_ref = refs
    score(spans, by_span(picked, spans, wk_ref.shape[0]), wk_ref, query_ref, scores_ref)


def tokens(picked, channels):
    return sum(array.size for array in picked) // channels


def scores_shape(picked, queries, channels, spans):
    return spans * (queries.shape[1] // (PAIR * HD)), tokens(picked, channels) // spans, PAIR * SPAN


def own_scores(picked, w_key, queries, spans):
    return pl.pallas_call(
        functools.partial(score_kernel, spans),
        out_shape=jax.ShapeDtypeStruct(scores_shape(picked, queries, w_key.shape[0], spans), jnp.float32),
        in_specs=[VMEM] * (2 + len(picked)),
        out_specs=VMEM,
        compiler_params=params(),
    )(*picked, w_key, queries)


def values_kernel(spans, *refs):
    *picked, wv_ref, values_ref = refs
    source = by_span(picked, spans, wv_ref.shape[0])
    values_ref[...] = jnp.dot(source, wv_ref[...], preferred_element_type=jnp.float32).astype(values_ref.dtype)


def own_values(picked, w_value, spans):
    return pl.pallas_call(
        functools.partial(values_kernel, spans),
        out_shape=jax.ShapeDtypeStruct((tokens(picked, w_value.shape[0]), w_value.shape[1]), picked[0].dtype),
        in_specs=[VMEM] * (1 + len(picked)),
        out_specs=VMEM,
        compiler_params=params(),
    )(*picked, w_value)


def attend_kernel(spans, *refs):
    *others, wk_ref, wv_ref, query_ref, first_ref, values_ref, out_ref, second_ref, probs_ref, held_ref, sems = refs
    other = by_span(others, spans, wk_ref.shape[0])
    score(spans, other, wk_ref, query_ref, second_ref)
    per = other.shape[0] // spans
    more = jnp.dot(other, wv_ref[...], preferred_element_type=jnp.float32).astype(jnp.bfloat16)
    everything = pair_places(spans, more.shape[1])
    for c, lanes, n in everything:
        scores = jnp.concatenate([first_ref[n], second_ref[n]], axis=0)
        raised = jnp.exp2((scores - jnp.max(scores, axis=0, keepdims=True)) * EXPONENT)
        probs_ref[n] = (raised * (1.0 / jnp.sum(raised, axis=0, keepdims=True))).astype(jnp.bfloat16)
    copies = []
    for c in range(spans):
        here = pl.ds(c * SPAN, SPAN)
        for at, lanes, n in everything:
            if at != c:
                continue
            rows = slice(c * per, (c + 1) * per)
            values = jnp.concatenate([values_ref[rows, lanes], more[rows, lanes]], axis=0)
            mixed = lax.dot_general(
                probs_ref[n], values, (((0,), (0,)), ((), ())), preferred_element_type=jnp.float32
            ).astype(out_ref.dtype)
            own = [mixed[h * SPAN : (h + 1) * SPAN, h * HD : (h + 1) * HD] for h in range(PAIR)]
            held_ref[here, lanes] = jnp.concatenate(own, axis=1)
        copies.append(pltpu.make_async_copy(held_ref.at[here, :], out_ref.at[here, :], sems.at[c]))
        copies[-1].start()
    for copy in copies:
        copy.wait()


def attend(others, w_key, w_value, queries, first, values, spans):
    each = scores_shape(others, queries, w_key.shape[0], spans)
    return pl.pallas_call(
        functools.partial(attend_kernel, spans),
        out_shape=jax.ShapeDtypeStruct(queries.shape, queries.dtype),
        in_specs=[VMEM] * (5 + len(others)),
        out_specs=pl.BlockSpec(memory_space=pl.ANY),
        scratch_shapes=[
            pltpu.VMEM(each, jnp.float32),
            pltpu.VMEM((each[0], 2 * each[1], each[2]), jnp.bfloat16),
            pltpu.VMEM(queries.shape, queries.dtype),
            pltpu.SemaphoreType.DMA((spans,)),
        ],
        compiler_params=params(),
    )(*others, w_key, w_value, queries, first, values)


def send(chunk, pairs):
    return lax.ppermute(chunk, "wide", pairs)


def gathered_plan(queries, encodings, w_key, w_value, block_owner, block_row):
    wide_count = lax.axis_size("wide")
    turns = wide_count // SIDE
    rows = encodings.shape[0]
    spans = queries.shape[0] // SPAN
    line = ring_order(turns)
    onward = [
        (here * SIDE + x, there * SIDE + x) for here, there in zip(line, line[1:] + line[:1]) for x in range(SIDE)
    ]
    across = [(n, n + 1 if n % SIDE == 0 else n - 1) for n in range(wide_count)]
    *pieces, whole = half_columns(encodings)
    order = [(0, 0)]
    for k in range(1, turns):
        order += [(k, 0), (k - 1, 1)]
    order.append((turns - 1, 1))
    index = places(order, turns, rows, jnp.transpose(block_owner, (0, 2, 1)), block_row)
    held = {(0, 0): pieces}
    for k in range(1, turns):
        behind = held[k - 1, 0]
        steps = [send(piece, onward) for piece in behind]
        if k < turns - 1:
            held[k - 1, 1] = [send(whole if k == 1 else jnp.concatenate(behind, axis=1), across)]
        else:
            held[k - 1, 1] = [send(piece, across) for piece in behind]
        held[k, 0] = steps
    straight, crossed = held[turns - 1, 0], held[turns - 2, 1]
    straight[0], crossed[0] = lax.optimization_barrier((straight[0], crossed[0]))
    held[turns - 1, 1] = [send(piece, across) for piece in held[turns - 1, 0]]
    sources = [held[chunk] for chunk in order]
    begun = early(index, sources[:-1], whole.shape[1])
    picked = [pick(index, *pieces, (len(order) - 1) * rows) for pieces in zip(begun[::-1], sources[-1][::-1])]
    others = [lax.ppermute(piece, "heads", [(0, 1), (1, 0)]) for piece in picked]
    first = own_scores(picked, w_key, queries, spans)
    values = own_values(picked, w_value, spans)
    return attend(others, w_key, w_value, queries, first, values, spans)


def exchange(encodings, owners, stored, capacity):
    wide_count = lax.axis_size("wide")
    requests = owners.shape[0]
    order = jnp.arange(requests, dtype=jnp.int32)
    earlier = (owners[:, None] == owners[None, :]) & (order[None, :] < order[:, None])
    rank = jnp.sum(earlier.astype(jnp.int32), axis=1)
    slot = owners * capacity + rank
    table = jnp.full((wide_count * capacity,), -1, jnp.int32).at[slot].set(stored)
    table = table.reshape(wide_count, capacity)
    asked = lax.all_to_all(table, "wide", split_axis=0, concat_axis=0, tiled=True)
    wanted = jnp.maximum(asked, 0)
    picked = encodings[wanted]
    returned = lax.all_to_all(picked, "wide", split_axis=0, concat_axis=0, tiled=True)
    return returned.reshape(wide_count * capacity, encodings.shape[1])[slot]


def exchanged_plan(queries, encodings, w_key, w_value, owners, stored, capacity):
    fetched = exchange(encodings, owners, stored, capacity)
    channels = w_key.shape[0]
    source = fetched.reshape(-1, channels)
    keys = jnp.dot(source, w_key, preferred_element_type=jnp.float32).astype(jnp.bfloat16)
    values = jnp.dot(source, w_value, preferred_element_type=jnp.float32).astype(jnp.bfloat16)
    span_count = queries.shape[0] // SPAN
    heads_local = w_key.shape[1] // HD
    keys = keys.reshape(span_count, -1, heads_local, HD)
    values = values.reshape(span_count, -1, heads_local, HD)
    query_part = queries.reshape(span_count, SPAN, heads_local, HD)
    scores = jnp.einsum(
        "cqhd,ckhd->chqk", query_part, keys, preferred_element_type=jnp.float32
    ) * HD ** (-0.5)
    probs = jax.nn.softmax(scores, axis=-1).astype(jnp.bfloat16)
    mixed = jnp.einsum("chqk,ckhd->cqhd", probs, values, preferred_element_type=jnp.float32)
    return mixed.astype(jnp.bfloat16).reshape(queries.shape)


def on_device(queries, encodings, w_key, w_value, block_owner, block_row):
    wide_count = lax.axis_size("wide")
    requests = block_row.size
    capacity = 2 * ((requests + wide_count - 1) // wide_count)
    if encodings.shape[0] <= 2 * capacity:
        return gathered_plan(queries, encodings, w_key, w_value, block_owner, block_row)
    return exchanged_plan(
        queries, encodings, w_key, w_value, block_owner.reshape(-1), block_row.reshape(-1), capacity
    )


def solution(mesh):
    placed = (
        P(("groups", "wide"), "heads"),
        P(("groups", "wide"), None),
        P(None, "heads"),
        P(None, "heads"),
        P(("groups", "wide"), None, None),
        P(("groups", "wide"), None),
    )
    return jax.shard_map(
        on_device,
        mesh=mesh,
        in_specs=placed,
        out_specs=P(("groups", "wide"), "heads"),
        check_vma=False,
    )
```

```python
import functools

import jax
import jax.numpy as jnp
from jax import lax
from jax.experimental import pallas as pl
from jax.experimental.pallas import tpu as pltpu
from jax.sharding import PartitionSpec as P

HD = 128
SPAN = 64
SIDE = 2
LIMIT = 24 * 1024 * 1024
STREAMS = 2
EXPONENT = HD ** (-0.5) * 1.4426950408889634
VMEM = pl.BlockSpec(memory_space=pltpu.VMEM)


def params():
    return pltpu.CompilerParams(vmem_limit_bytes=LIMIT)


def half_kernel(enc_ref, *refs):
    outs, sems = refs[:-1], refs[-1]
    first = lax.axis_index("heads") * outs[-1].shape[1]
    copies = []
    for n, out in enumerate(outs):
        width = out.shape[1]
        start = first + (n * width if n < STREAMS else 0)
        copies.append(pltpu.make_async_copy(enc_ref.at[:, pl.ds(pl.multiple_of(start, 128), width)], out, sems.at[n]))
    for copy in copies:
        copy.start()
    for copy in copies:
        copy.wait()


def half_columns(encodings):
    rows, columns = encodings.shape
    whole = columns // lax.axis_size("heads")
    widths = [whole // STREAMS] * STREAMS + [whole]
    return pl.pallas_call(
        half_kernel,
        out_shape=[jax.ShapeDtypeStruct((rows, width), encodings.dtype) for width in widths],
        in_specs=[VMEM],
        out_specs=[VMEM] * len(widths),
        scratch_shapes=[pltpu.SemaphoreType.DMA((len(widths),))],
        compiler_params=params(),
    )(encodings)


def chosen_rows(index, sources, first):
    held = jnp.concatenate(sources, axis=0)
    places = lax.broadcasted_iota(jnp.int32, (index.shape[0], held.shape[0]), 1) + first
    chosen = jnp.where(places == index, 1.0, 0.0).astype(held.dtype)
    return jnp.dot(chosen, held, preferred_element_type=jnp.float32)


def ring_order(turns):
    return [0] + list(range(1, turns, 2)) + list(range(turns - 2 + turns % 2, 0, -2))


def ring_place(line, turns):
    return jnp.where(line % 2 == 1, (line + 1) // 2, jnp.where(line == 0, 0, turns - line // 2))


def wanted_rows(order, turns, rows, owner_ref, stored_ref):
    me = lax.axis_index("wide")
    columns = []
    for c in range(stored_ref.shape[0]):
        owner, stored = owner_ref[c], stored_ref[c : c + 1, :]
        back = ring_place(me // SIDE, turns) - ring_place(owner // SIDE, turns)
        back = jnp.where(back < 0, back + turns, back)
        beside = jnp.where(owner % SIDE == me % SIDE, 0, 1)
        place = jnp.zeros_like(stored)
        for n, chunk in enumerate(order):
            place = jnp.where(back * 2 + beside == chunk[0] * 2 + chunk[1], n, place)
        place = place * rows + stored
        square = (place.shape[1], place.shape[1])
        own = lax.broadcasted_iota(jnp.int32, square, 0) == lax.broadcasted_iota(jnp.int32, square, 1)
        spread = jnp.where(own, jnp.broadcast_to(place.astype(jnp.float32), square), 0.0)
        columns.append(jnp.sum(spread, axis=1, keepdims=True))
    return jnp.concatenate(columns, axis=0).astype(jnp.int32)


def places_kernel(order, turns, rows, owner_ref, stored_ref, index_ref):
    index_ref[...] = wanted_rows(order, turns, rows, owner_ref, stored_ref)


def places(order, turns, rows, owners, stored):
    return pl.pallas_call(
        functools.partial(places_kernel, order, turns, rows),
        out_shape=jax.ShapeDtypeStruct((stored.size, 1), jnp.int32),
        in_specs=[VMEM] * 2,
        out_specs=VMEM,
        compiler_params=params(),
    )(owners, stored)


def early_kernel(chunks, index_ref, *refs):
    sources, outs = refs[:-STREAMS], refs[-STREAMS:]
    starts = [sum(chunks[:n]) for n in range(len(chunks))]
    for n, out in enumerate(outs):
        lanes = slice(n * out.shape[1], (n + 1) * out.shape[1])
        held = [
            sources[at + n][...] if arrays > 1 else sources[at][:, lanes] for at, arrays in zip(starts, chunks)
        ]
        out[...] = chosen_rows(index_ref[...], held, 0).astype(out.dtype)


def early(index, sources, width):
    rows = sources[0][0].shape[0]
    requests = index.shape[0]
    arrays = [array for chunk in sources for array in chunk]
    return pl.pallas_call(
        functools.partial(early_kernel, [len(chunk) for chunk in sources]),
        out_shape=[jax.ShapeDtypeStruct((requests, width // STREAMS), arrays[0].dtype)] * STREAMS,
        in_specs=[VMEM] * (1 + len(arrays)),
        out_specs=[VMEM] * STREAMS,
        compiler_params=params(),
        cost_estimate=pl.CostEstimate(
            flops=2 * requests * width * rows * len(sources),
            bytes_accessed=2 * requests * width,
            transcendentals=0,
        ),
    )(index, *arrays)


def pick_kernel(first, index_ref, begun_ref, last_ref, out_ref):
    picked = chosen_rows(index_ref[...], [last_ref[...]], first)
    out_ref[...] = (picked + begun_ref[...].astype(jnp.float32)).astype(out_ref.dtype)


def pick(index, begun, last, first):
    return pl.pallas_call(
        functools.partial(pick_kernel, first),
        out_shape=jax.ShapeDtypeStruct(begun.shape, begun.dtype),
        in_specs=[VMEM] * 3,
        out_specs=VMEM,
        compiler_params=params(),
    )(index, begun, last)


def by_span(picked, spans, channels):
    per = picked[0].shape[0] // spans
    parts = []
    for c in range(spans):
        for array in picked:
            for t in range(array.shape[1] // channels):
                parts.append(array[c * per : (c + 1) * per, t * channels : (t + 1) * channels])
    return jnp.concatenate(parts, axis=0)


PAIR = 2


def pair_places(spans, columns):
    pairs = columns // (PAIR * HD)
    return [
        (c, slice(p * PAIR * HD, (p + 1) * PAIR * HD), c * pairs + p) for c in range(spans) for p in range(pairs)
    ]


def apart(query):
    none = jnp.zeros((query.shape[0], HD), query.dtype)
    upper = jnp.concatenate([query[:, :HD], none], axis=1)
    lower = jnp.concatenate([none, query[:, HD:]], axis=1)
    return jnp.concatenate([upper, lower], axis=0)


def score(spans, source, wk_ref, query_ref, scores_ref):
    keys = jnp.dot(source, wk_ref[...], preferred_element_type=jnp.float32).astype(jnp.bfloat16)
    per = keys.shape[0] // spans
    for c, lanes, n in pair_places(spans, keys.shape[1]):
        scores_ref[n] = lax.dot_general(
            keys[c * per : (c + 1) * per, lanes],
            apart(query_ref[c * SPAN : (c + 1) * SPAN, lanes]),
            (((1,), (1,)), ((), ())),
            preferred_element_type=jnp.float32,
        )


def score_kernel(spans, *refs):
    *picked, wk_ref, query_ref, scores_ref = refs
    score(spans, by_span(picked, spans, wk_ref.shape[0]), wk_ref, query_ref, scores_ref)


def tokens(picked, channels):
    return sum(array.size for array in picked) // channels


def scores_shape(picked, queries, channels, spans):
    return spans * (queries.shape[1] // (PAIR * HD)), tokens(picked, channels) // spans, PAIR * SPAN


def own_scores(picked, w_key, queries, spans):
    return pl.pallas_call(
        functools.partial(score_kernel, spans),
        out_shape=jax.ShapeDtypeStruct(scores_shape(picked, queries, w_key.shape[0], spans), jnp.float32),
        in_specs=[VMEM] * (2 + len(picked)),
        out_specs=VMEM,
        compiler_params=params(),
    )(*picked, w_key, queries)


def values_kernel(spans, *refs):
    *picked, wv_ref, values_ref = refs
    source = by_span(picked, spans, wv_ref.shape[0])
    values_ref[...] = jnp.dot(source, wv_ref[...], preferred_element_type=jnp.float32).astype(values_ref.dtype)


def own_values(picked, w_value, spans):
    return pl.pallas_call(
        functools.partial(values_kernel, spans),
        out_shape=jax.ShapeDtypeStruct((tokens(picked, w_value.shape[0]), w_value.shape[1]), picked[0].dtype),
        in_specs=[VMEM] * (1 + len(picked)),
        out_specs=VMEM,
        compiler_params=params(),
    )(*picked, w_value)


def attend_kernel(spans, *refs):
    *others, wk_ref, wv_ref, query_ref, first_ref, values_ref, out_ref, second_ref, probs_ref, held_ref, sems = refs
    other = by_span(others, spans, wk_ref.shape[0])
    score(spans, other, wk_ref, query_ref, second_ref)
    per = other.shape[0] // spans
    more = jnp.dot(other, wv_ref[...], preferred_element_type=jnp.float32).astype(jnp.bfloat16)
    everything = pair_places(spans, more.shape[1])
    copies = []
    for c in range(spans):
        here = pl.ds(c * SPAN, SPAN)
        ours = [(lanes, n) for at, lanes, n in everything if at == c]
        for lanes, n in ours:
            scores = jnp.concatenate([first_ref[n], second_ref[n]], axis=0)
            raised = jnp.exp2((scores - jnp.max(scores, axis=0, keepdims=True)) * EXPONENT)
            probs_ref[n] = (raised * (1.0 / jnp.sum(raised, axis=0, keepdims=True))).astype(jnp.bfloat16)
        for lanes, n in ours:
            rows = slice(c * per, (c + 1) * per)
            values = jnp.concatenate([values_ref[rows, lanes], more[rows, lanes]], axis=0)
            mixed = lax.dot_general(
                probs_ref[n], values, (((0,), (0,)), ((), ())), preferred_element_type=jnp.float32
            ).astype(out_ref.dtype)
            own = [mixed[h * SPAN : (h + 1) * SPAN, h * HD : (h + 1) * HD] for h in range(PAIR)]
            held_ref[here, lanes] = jnp.concatenate(own, axis=1)
        copies.append(pltpu.make_async_copy(held_ref.at[here, :], out_ref.at[here, :], sems.at[c]))
        copies[-1].start()
    for copy in copies:
        copy.wait()


def attend(others, w_key, w_value, queries, first, values, spans):
    each = scores_shape(others, queries, w_key.shape[0], spans)
    return pl.pallas_call(
        functools.partial(attend_kernel, spans),
        out_shape=jax.ShapeDtypeStruct(queries.shape, queries.dtype),
        in_specs=[VMEM] * (5 + len(others)),
        out_specs=pl.BlockSpec(memory_space=pl.ANY),
        scratch_shapes=[
            pltpu.VMEM(each, jnp.float32),
            pltpu.VMEM((each[0], 2 * each[1], each[2]), jnp.bfloat16),
            pltpu.VMEM(queries.shape, queries.dtype),
            pltpu.SemaphoreType.DMA((spans,)),
        ],
        compiler_params=params(),
    )(*others, w_key, w_value, queries, first, values)


def send(chunk, pairs):
    return lax.ppermute(chunk, "wide", pairs)


def gathered_plan(queries, encodings, w_key, w_value, block_owner, block_row):
    wide_count = lax.axis_size("wide")
    turns = wide_count // SIDE
    rows = encodings.shape[0]
    spans = queries.shape[0] // SPAN
    line = ring_order(turns)
    onward = [
        (here * SIDE + x, there * SIDE + x) for here, there in zip(line, line[1:] + line[:1]) for x in range(SIDE)
    ]
    across = [(n, n + 1 if n % SIDE == 0 else n - 1) for n in range(wide_count)]
    *pieces, whole = half_columns(encodings)
    order = [(0, 0)]
    for k in range(1, turns):
        order += [(k, 0), (k - 1, 1)]
    order.append((turns - 1, 1))
    index = places(order, turns, rows, jnp.transpose(block_owner, (0, 2, 1)), block_row)
    held = {(0, 0): pieces}
    for k in range(1, turns):
        behind = held[k - 1, 0]
        steps = [send(piece, onward) for piece in behind]
        if k < turns - 1:
            held[k - 1, 1] = [send(whole if k == 1 else jnp.concatenate(behind, axis=1), across)]
        else:
            held[k - 1, 1] = [send(piece, across) for piece in behind]
        held[k, 0] = steps
    straight, crossed = held[turns - 1, 0], held[turns - 2, 1]
    straight[0], crossed[0] = lax.optimization_barrier((straight[0], crossed[0]))
    held[turns - 1, 1] = [send(piece, across) for piece in held[turns - 1, 0]]
    sources = [held[chunk] for chunk in order]
    begun = early(index, sources[:-1], whole.shape[1])
    picked = [pick(index, *pieces, (len(order) - 1) * rows) for pieces in zip(begun[::-1], sources[-1][::-1])]
    others = [lax.ppermute(piece, "heads", [(0, 1), (1, 0)]) for piece in picked]
    first = own_scores(picked, w_key, queries, spans)
    values = own_values(picked, w_value, spans)
    return attend(others, w_key, w_value, queries, first, values, spans)


def exchange(encodings, owners, stored, capacity):
    wide_count = lax.axis_size("wide")
    requests = owners.shape[0]
    order = jnp.arange(requests, dtype=jnp.int32)
    earlier = (owners[:, None] == owners[None, :]) & (order[None, :] < order[:, None])
    rank = jnp.sum(earlier.astype(jnp.int32), axis=1)
    slot = owners * capacity + rank
    table = jnp.full((wide_count * capacity,), -1, jnp.int32).at[slot].set(stored)
    table = table.reshape(wide_count, capacity)
    asked = lax.all_to_all(table, "wide", split_axis=0, concat_axis=0, tiled=True)
    wanted = jnp.maximum(asked, 0)
    picked = encodings[wanted]
    returned = lax.all_to_all(picked, "wide", split_axis=0, concat_axis=0, tiled=True)
    return returned.reshape(wide_count * capacity, encodings.shape[1])[slot]


def exchanged_plan(queries, encodings, w_key, w_value, owners, stored, capacity):
    fetched = exchange(encodings, owners, stored, capacity)
    channels = w_key.shape[0]
    source = fetched.reshape(-1, channels)
    keys = jnp.dot(source, w_key, preferred_element_type=jnp.float32).astype(jnp.bfloat16)
    values = jnp.dot(source, w_value, preferred_element_type=jnp.float32).astype(jnp.bfloat16)
    span_count = queries.shape[0] // SPAN
    heads_local = w_key.shape[1] // HD
    keys = keys.reshape(span_count, -1, heads_local, HD)
    values = values.reshape(span_count, -1, heads_local, HD)
    query_part = queries.reshape(span_count, SPAN, heads_local, HD)
    scores = jnp.einsum(
        "cqhd,ckhd->chqk", query_part, keys, preferred_element_type=jnp.float32
    ) * HD ** (-0.5)
    probs = jax.nn.softmax(scores, axis=-1).astype(jnp.bfloat16)
    mixed = jnp.einsum("chqk,ckhd->cqhd", probs, values, preferred_element_type=jnp.float32)
    return mixed.astype(jnp.bfloat16).reshape(queries.shape)


def on_device(queries, encodings, w_key, w_value, block_owner, block_row):
    wide_count = lax.axis_size("wide")
    requests = block_row.size
    capacity = 2 * ((requests + wide_count - 1) // wide_count)
    if encodings.shape[0] <= 2 * capacity:
        return gathered_plan(queries, encodings, w_key, w_value, block_owner, block_row)
    return exchanged_plan(
        queries, encodings, w_key, w_value, block_owner.reshape(-1), block_row.reshape(-1), capacity
    )


def solution(mesh):
    placed = (
        P(("groups", "wide"), "heads"),
        P(("groups", "wide"), None),
        P(None, "heads"),
        P(None, "heads"),
        P(("groups", "wide"), None, None),
        P(("groups", "wide"), None),
    )
    return jax.shard_map(
        on_device,
        mesh=mesh,
        in_specs=placed,
        out_specs=P(("groups", "wide"), "heads"),
        check_vma=False,
    )
```

```python
import functools

import jax
import jax.numpy as jnp
from jax import lax
from jax.experimental import pallas as pl
from jax.experimental.pallas import tpu as pltpu
from jax.sharding import PartitionSpec as P

HD = 128
SPAN = 64
SIDE = 2
LIMIT = 24 * 1024 * 1024
STREAMS = 2
EXPONENT = HD ** (-0.5) * 1.4426950408889634
VMEM = pl.BlockSpec(memory_space=pltpu.VMEM)


def params():
    return pltpu.CompilerParams(vmem_limit_bytes=LIMIT)


def half_kernel(enc_ref, *refs):
    outs, sems = refs[:-1], refs[-1]
    first = lax.axis_index("heads") * outs[-1].shape[1]
    copies = []
    for n, out in enumerate(outs):
        width = out.shape[1]
        start = first + (n * width if n < STREAMS else 0)
        copies.append(pltpu.make_async_copy(enc_ref.at[:, pl.ds(pl.multiple_of(start, 128), width)], out, sems.at[n]))
    for copy in copies:
        copy.start()
    for copy in copies:
        copy.wait()


def half_columns(encodings):
    rows, columns = encodings.shape
    whole = columns // lax.axis_size("heads")
    widths = [whole // STREAMS] * STREAMS + [whole]
    return pl.pallas_call(
        half_kernel,
        out_shape=[jax.ShapeDtypeStruct((rows, width), encodings.dtype) for width in widths],
        in_specs=[VMEM],
        out_specs=[VMEM] * len(widths),
        scratch_shapes=[pltpu.SemaphoreType.DMA((len(widths),))],
        compiler_params=params(),
    )(encodings)


def chosen_rows(index, sources, first):
    held = jnp.concatenate(sources, axis=0)
    places = lax.broadcasted_iota(jnp.int32, (index.shape[0], held.shape[0]), 1) + first
    chosen = jnp.where(places == index, 1.0, 0.0).astype(held.dtype)
    return jnp.dot(chosen, held, preferred_element_type=jnp.float32)


def ring_order(turns):
    return [0] + list(range(1, turns, 2)) + list(range(turns - 2 + turns % 2, 0, -2))


def ring_place(line, turns):
    return jnp.where(line % 2 == 1, (line + 1) // 2, jnp.where(line == 0, 0, turns - line // 2))


def wanted_rows(order, turns, rows, owner_ref, stored_ref):
    me = lax.axis_index("wide")
    columns = []
    for c in range(stored_ref.shape[0]):
        owner, stored = owner_ref[c], stored_ref[c : c + 1, :]
        back = ring_place(me // SIDE, turns) - ring_place(owner // SIDE, turns)
        back = jnp.where(back < 0, back + turns, back)
        beside = jnp.where(owner % SIDE == me % SIDE, 0, 1)
        place = jnp.zeros_like(stored)
        for n, chunk in enumerate(order):
            place = jnp.where(back * 2 + beside == chunk[0] * 2 + chunk[1], n, place)
        place = place * rows + stored
        square = (place.shape[1], place.shape[1])
        own = lax.broadcasted_iota(jnp.int32, square, 0) == lax.broadcasted_iota(jnp.int32, square, 1)
        spread = jnp.where(own, jnp.broadcast_to(place.astype(jnp.float32), square), 0.0)
        columns.append(jnp.sum(spread, axis=1, keepdims=True))
    return jnp.concatenate(columns, axis=0).astype(jnp.int32)


def places_kernel(order, turns, rows, owner_ref, stored_ref, index_ref):
    index_ref[...] = wanted_rows(order, turns, rows, owner_ref, stored_ref)


def places(order, turns, rows, owners, stored):
    return pl.pallas_call(
        functools.partial(places_kernel, order, turns, rows),
        out_shape=jax.ShapeDtypeStruct((stored.size, 1), jnp.int32),
        in_specs=[VMEM] * 2,
        out_specs=VMEM,
        compiler_params=params(),
    )(owners, stored)


def early_kernel(chunks, index_ref, *refs):
    sources, outs = refs[:-STREAMS], refs[-STREAMS:]
    starts = [sum(chunks[:n]) for n in range(len(chunks))]
    for n, out in enumerate(outs):
        lanes = slice(n * out.shape[1], (n + 1) * out.shape[1])
        held = [
            sources[at + n][...] if arrays > 1 else sources[at][:, lanes] for at, arrays in zip(starts, chunks)
        ]
        out[...] = chosen_rows(index_ref[...], held, 0).astype(out.dtype)


def early(index, sources, width):
    rows = sources[0][0].shape[0]
    requests = index.shape[0]
    arrays = [array for chunk in sources for array in chunk]
    return pl.pallas_call(
        functools.partial(early_kernel, [len(chunk) for chunk in sources]),
        out_shape=[jax.ShapeDtypeStruct((requests, width // STREAMS), arrays[0].dtype)] * STREAMS,
        in_specs=[VMEM] * (1 + len(arrays)),
        out_specs=[VMEM] * STREAMS,
        compiler_params=params(),
        cost_estimate=pl.CostEstimate(
            flops=2 * requests * width * rows * len(sources),
            bytes_accessed=2 * requests * width,
            transcendentals=0,
        ),
    )(index, *arrays)


def pick_kernel(first, index_ref, begun_ref, last_ref, out_ref):
    picked = chosen_rows(index_ref[...], [last_ref[...]], first)
    out_ref[...] = (picked + begun_ref[...].astype(jnp.float32)).astype(out_ref.dtype)


def pick(index, begun, last, first):
    return pl.pallas_call(
        functools.partial(pick_kernel, first),
        out_shape=jax.ShapeDtypeStruct(begun.shape, begun.dtype),
        in_specs=[VMEM] * 3,
        out_specs=VMEM,
        compiler_params=params(),
    )(index, begun, last)


def by_span(picked, spans, channels):
    per = picked[0].shape[0] // spans
    parts = []
    for c in range(spans):
        for array in picked:
            for t in range(array.shape[1] // channels):
                parts.append(array[c * per : (c + 1) * per, t * channels : (t + 1) * channels])
    return jnp.concatenate(parts, axis=0)


PAIR = 2


def pair_places(spans, columns):
    pairs = columns // (PAIR * HD)
    return [
        (c, slice(p * PAIR * HD, (p + 1) * PAIR * HD), c * pairs + p) for c in range(spans) for p in range(pairs)
    ]


def apart(query):
    none = jnp.zeros((query.shape[0], HD), query.dtype)
    upper = jnp.concatenate([query[:, :HD], none], axis=1)
    lower = jnp.concatenate([none, query[:, HD:]], axis=1)
    return jnp.concatenate([upper, lower], axis=0)


def score(spans, source, wk_ref, query_ref, scores_ref):
    keys = jnp.dot(source, wk_ref[...], preferred_element_type=jnp.float32).astype(jnp.bfloat16)
    per = keys.shape[0] // spans
    for c, lanes, n in pair_places(spans, keys.shape[1]):
        scores_ref[n] = lax.dot_general(
            keys[c * per : (c + 1) * per, lanes],
            apart(query_ref[c * SPAN : (c + 1) * SPAN, lanes]),
            (((1,), (1,)), ((), ())),
            preferred_element_type=jnp.float32,
        )


def score_kernel(spans, *refs):
    *picked, wk_ref, query_ref, scores_ref = refs
    score(spans, by_span(picked, spans, wk_ref.shape[0]), wk_ref, query_ref, scores_ref)


def tokens(picked, channels):
    return sum(array.size for array in picked) // channels


def scores_shape(picked, queries, channels, spans):
    return spans * (queries.shape[1] // (PAIR * HD)), tokens(picked, channels) // spans, PAIR * SPAN


def own_scores(picked, w_key, queries, spans):
    return pl.pallas_call(
        functools.partial(score_kernel, spans),
        out_shape=jax.ShapeDtypeStruct(scores_shape(picked, queries, w_key.shape[0], spans), jnp.float32),
        in_specs=[VMEM] * (2 + len(picked)),
        out_specs=VMEM,
        compiler_params=params(),
    )(*picked, w_key, queries)


def values_kernel(spans, *refs):
    *picked, wv_ref, values_ref = refs
    source = by_span(picked, spans, wv_ref.shape[0])
    values_ref[...] = jnp.dot(source, wv_ref[...], preferred_element_type=jnp.float32).astype(values_ref.dtype)


def own_values(picked, w_value, spans):
    return pl.pallas_call(
        functools.partial(values_kernel, spans),
        out_shape=jax.ShapeDtypeStruct((tokens(picked, w_value.shape[0]), w_value.shape[1]), picked[0].dtype),
        in_specs=[VMEM] * (1 + len(picked)),
        out_specs=VMEM,
        compiler_params=params(),
    )(*picked, w_value)


def attend_kernel(spans, *refs):
    others, refs = refs[:STREAMS], refs[STREAMS:]
    values_refs, refs = refs[:STREAMS], refs[STREAMS:]
    wk_ref, wv_ref, query_ref, first_ref, out_ref, second_ref, probs_ref, held_ref, sems = refs
    other = by_span(others, spans, wk_ref.shape[0])
    score(spans, other, wk_ref, query_ref, second_ref)
    per = other.shape[0] // spans
    more = jnp.dot(other, wv_ref[...], preferred_element_type=jnp.float32).astype(jnp.bfloat16)
    everything = pair_places(spans, more.shape[1])
    for c, lanes, n in everything:
        scores = jnp.concatenate([first_ref[n], second_ref[n]], axis=0)
        raised = jnp.exp2((scores - jnp.max(scores, axis=0, keepdims=True)) * EXPONENT)
        probs_ref[n] = (raised * (1.0 / jnp.sum(raised, axis=0, keepdims=True))).astype(jnp.bfloat16)
    copies = []
    for c in range(spans):
        here = pl.ds(c * SPAN, SPAN)
        for at, lanes, n in everything:
            if at != c:
                continue
            rows = slice(c * per, (c + 1) * per)
            owned = [ref[c * ref.shape[0] // spans : (c + 1) * ref.shape[0] // spans, lanes] for ref in values_refs]
            values = jnp.concatenate(owned + [more[rows, lanes]], axis=0)
            mixed = lax.dot_general(
                probs_ref[n], values, (((0,), (0,)), ((), ())), preferred_element_type=jnp.float32
            ).astype(out_ref.dtype)
            own = [mixed[h * SPAN : (h + 1) * SPAN, h * HD : (h + 1) * HD] for h in range(PAIR)]
            held_ref[here, lanes] = jnp.concatenate(own, axis=1)
        copies.append(pltpu.make_async_copy(held_ref.at[here, :], out_ref.at[here, :], sems.at[c]))
        copies[-1].start()
    for copy in copies:
        copy.wait()


def attend(others, w_key, w_value, queries, first, values, spans):
    each = scores_shape(others, queries, w_key.shape[0], spans)
    return pl.pallas_call(
        functools.partial(attend_kernel, spans),
        out_shape=jax.ShapeDtypeStruct(queries.shape, queries.dtype),
        in_specs=[VMEM] * (4 + len(others) + len(values)),
        out_specs=pl.BlockSpec(memory_space=pl.ANY),
        scratch_shapes=[
            pltpu.VMEM(each, jnp.float32),
            pltpu.VMEM((each[0], 2 * each[1], each[2]), jnp.bfloat16),
            pltpu.VMEM(queries.shape, queries.dtype),
            pltpu.SemaphoreType.DMA((spans,)),
        ],
        compiler_params=params(),
    )(*others, *values, w_key, w_value, queries, first)


def send(chunk, pairs):
    return lax.ppermute(chunk, "wide", pairs)


def gathered_plan(queries, encodings, w_key, w_value, block_owner, block_row):
    wide_count = lax.axis_size("wide")
    turns = wide_count // SIDE
    rows = encodings.shape[0]
    spans = queries.shape[0] // SPAN
    line = ring_order(turns)
    onward = [
        (here * SIDE + x, there * SIDE + x) for here, there in zip(line, line[1:] + line[:1]) for x in range(SIDE)
    ]
    across = [(n, n + 1 if n % SIDE == 0 else n - 1) for n in range(wide_count)]
    *pieces, whole = half_columns(encodings)
    order = [(0, 0)]
    for k in range(1, turns):
        order += [(k, 0), (k - 1, 1)]
    order.append((turns - 1, 1))
    index = places(order, turns, rows, jnp.transpose(block_owner, (0, 2, 1)), block_row)
    held = {(0, 0): pieces}
    for k in range(1, turns):
        behind = held[k - 1, 0]
        steps = [send(piece, onward) for piece in behind]
        if k < turns - 1:
            held[k - 1, 1] = [send(whole if k == 1 else jnp.concatenate(behind, axis=1), across)]
        else:
            held[k - 1, 1] = [send(piece, across) for piece in behind]
        held[k, 0] = steps
    straight, crossed = held[turns - 1, 0], held[turns - 2, 1]
    straight[0], crossed[0] = lax.optimization_barrier((straight[0], crossed[0]))
    held[turns - 1, 1] = [send(piece, across) for piece in held[turns - 1, 0]]
    sources = [held[chunk] for chunk in order]
    begun = early(index, sources[:-1], whole.shape[1])
    picked, values, others = [], [], []
    for piece, last in zip(begun, sources[-1]):
        if values:
            last, values[-1] = lax.optimization_barrier((last, values[-1]))
        picked.append(pick(index, piece, last, (len(order) - 1) * rows))
        others.append(lax.ppermute(picked[-1], "heads", [(0, 1), (1, 0)]))
        values.append(own_values(picked[-1:], w_value, spans))
    first = own_scores(picked, w_key, queries, spans)
    return attend(others, w_key, w_value, queries, first, values, spans)


def exchange(encodings, owners, stored, capacity):
    wide_count = lax.axis_size("wide")
    requests = owners.shape[0]
    order = jnp.arange(requests, dtype=jnp.int32)
    earlier = (owners[:, None] == owners[None, :]) & (order[None, :] < order[:, None])
    rank = jnp.sum(earlier.astype(jnp.int32), axis=1)
    slot = owners * capacity + rank
    table = jnp.full((wide_count * capacity,), -1, jnp.int32).at[slot].set(stored)
    table = table.reshape(wide_count, capacity)
    asked = lax.all_to_all(table, "wide", split_axis=0, concat_axis=0, tiled=True)
    wanted = jnp.maximum(asked, 0)
    picked = encodings[wanted]
    returned = lax.all_to_all(picked, "wide", split_axis=0, concat_axis=0, tiled=True)
    return returned.reshape(wide_count * capacity, encodings.shape[1])[slot]


def exchanged_plan(queries, encodings, w_key, w_value, owners, stored, capacity):
    fetched = exchange(encodings, owners, stored, capacity)
    channels = w_key.shape[0]
    source = fetched.reshape(-1, channels)
    keys = jnp.dot(source, w_key, preferred_element_type=jnp.float32).astype(jnp.bfloat16)
    values = jnp.dot(source, w_value, preferred_element_type=jnp.float32).astype(jnp.bfloat16)
    span_count = queries.shape[0] // SPAN
    heads_local = w_key.shape[1] // HD
    keys = keys.reshape(span_count, -1, heads_local, HD)
    values = values.reshape(span_count, -1, heads_local, HD)
    query_part = queries.reshape(span_count, SPAN, heads_local, HD)
    scores = jnp.einsum(
        "cqhd,ckhd->chqk", query_part, keys, preferred_element_type=jnp.float32
    ) * HD ** (-0.5)
    probs = jax.nn.softmax(scores, axis=-1).astype(jnp.bfloat16)
    mixed = jnp.einsum("chqk,ckhd->cqhd", probs, values, preferred_element_type=jnp.float32)
    return mixed.astype(jnp.bfloat16).reshape(queries.shape)


def on_device(queries, encodings, w_key, w_value, block_owner, block_row):
    wide_count = lax.axis_size("wide")
    requests = block_row.size
    capacity = 2 * ((requests + wide_count - 1) // wide_count)
    if encodings.shape[0] <= 2 * capacity:
        return gathered_plan(queries, encodings, w_key, w_value, block_owner, block_row)
    return exchanged_plan(
        queries, encodings, w_key, w_value, block_owner.reshape(-1), block_row.reshape(-1), capacity
    )


def solution(mesh):
    placed = (
        P(("groups", "wide"), "heads"),
        P(("groups", "wide"), None),
        P(None, "heads"),
        P(None, "heads"),
        P(("groups", "wide"), None, None),
        P(("groups", "wide"), None),
    )
    return jax.shard_map(
        on_device,
        mesh=mesh,
        in_specs=placed,
        out_specs=P(("groups", "wide"), "heads"),
        check_vma=False,
    )
```

```python
import functools

import jax
import jax.numpy as jnp
from jax import lax
from jax.experimental import pallas as pl
from jax.experimental.pallas import tpu as pltpu
from jax.sharding import PartitionSpec as P

HD = 128
SPAN = 64
SIDE = 2
LIMIT = 24 * 1024 * 1024
STREAMS = 2
EXPONENT = HD ** (-0.5) * 1.4426950408889634
VMEM = pl.BlockSpec(memory_space=pltpu.VMEM)


def params():
    return pltpu.CompilerParams(vmem_limit_bytes=LIMIT)


def half_kernel(enc_ref, *refs):
    outs, sems = refs[:-1], refs[-1]
    first = lax.axis_index("heads") * outs[-1].shape[1]
    copies = []
    for n, out in enumerate(outs):
        width = out.shape[1]
        start = first + (n * width if n < STREAMS else 0)
        copies.append(pltpu.make_async_copy(enc_ref.at[:, pl.ds(pl.multiple_of(start, 128), width)], out, sems.at[n]))
    for copy in copies:
        copy.start()
    for copy in copies:
        copy.wait()


def half_columns(encodings):
    rows, columns = encodings.shape
    whole = columns // lax.axis_size("heads")
    widths = [whole // STREAMS] * STREAMS + [whole]
    return pl.pallas_call(
        half_kernel,
        out_shape=[jax.ShapeDtypeStruct((rows, width), encodings.dtype) for width in widths],
        in_specs=[VMEM],
        out_specs=[VMEM] * len(widths),
        scratch_shapes=[pltpu.SemaphoreType.DMA((len(widths),))],
        compiler_params=params(),
    )(encodings)


def chosen_rows(index, sources, first):
    held = jnp.concatenate(sources, axis=0)
    places = lax.broadcasted_iota(jnp.int32, (index.shape[0], held.shape[0]), 1) + first
    chosen = jnp.where(places == index, 1.0, 0.0).astype(held.dtype)
    return jnp.dot(chosen, held, preferred_element_type=jnp.float32)


def ring_order(turns):
    return [0] + list(range(1, turns, 2)) + list(range(turns - 2 + turns % 2, 0, -2))


def ring_place(line, turns):
    return jnp.where(line % 2 == 1, (line + 1) // 2, jnp.where(line == 0, 0, turns - line // 2))


def wanted_rows(order, turns, rows, owner_ref, stored_ref):
    me = lax.axis_index("wide")
    columns = []
    for c in range(stored_ref.shape[0]):
        owner, stored = owner_ref[c], stored_ref[c : c + 1, :]
        back = ring_place(me // SIDE, turns) - ring_place(owner // SIDE, turns)
        back = jnp.where(back < 0, back + turns, back)
        beside = jnp.where(owner % SIDE == me % SIDE, 0, 1)
        place = jnp.zeros_like(stored)
        for n, chunk in enumerate(order):
            place = jnp.where(back * 2 + beside == chunk[0] * 2 + chunk[1], n, place)
        place = place * rows + stored
        square = (place.shape[1], place.shape[1])
        own = lax.broadcasted_iota(jnp.int32, square, 0) == lax.broadcasted_iota(jnp.int32, square, 1)
        spread = jnp.where(own, jnp.broadcast_to(place.astype(jnp.float32), square), 0.0)
        columns.append(jnp.sum(spread, axis=1, keepdims=True))
    return jnp.concatenate(columns, axis=0).astype(jnp.int32)


def places_kernel(order, turns, rows, owner_ref, stored_ref, index_ref):
    index_ref[...] = wanted_rows(order, turns, rows, owner_ref, stored_ref)


def places(order, turns, rows, owners, stored):
    return pl.pallas_call(
        functools.partial(places_kernel, order, turns, rows),
        out_shape=jax.ShapeDtypeStruct((stored.size, 1), jnp.int32),
        in_specs=[VMEM] * 2,
        out_specs=VMEM,
        compiler_params=params(),
    )(owners, stored)


def early_kernel(chunks, index_ref, *refs):
    sources, outs = refs[:-STREAMS], refs[-STREAMS:]
    starts = [sum(chunks[:n]) for n in range(len(chunks))]
    for n, out in enumerate(outs):
        lanes = slice(n * out.shape[1], (n + 1) * out.shape[1])
        held = [
            sources[at + n][...] if arrays > 1 else sources[at][:, lanes] for at, arrays in zip(starts, chunks)
        ]
        out[...] = chosen_rows(index_ref[...], held, 0).astype(out.dtype)


def early(index, sources, width):
    rows = sources[0][0].shape[0]
    requests = index.shape[0]
    arrays = [array for chunk in sources for array in chunk]
    return pl.pallas_call(
        functools.partial(early_kernel, [len(chunk) for chunk in sources]),
        out_shape=[jax.ShapeDtypeStruct((requests, width // STREAMS), arrays[0].dtype)] * STREAMS,
        in_specs=[VMEM] * (1 + len(arrays)),
        out_specs=[VMEM] * STREAMS,
        compiler_params=params(),
        cost_estimate=pl.CostEstimate(
            flops=2 * requests * width * rows * len(sources),
            bytes_accessed=2 * requests * width,
            transcendentals=0,
        ),
    )(index, *arrays)


def pick_kernel(first, index_ref, begun_ref, last_ref, out_ref):
    picked = chosen_rows(index_ref[...], [last_ref[...]], first)
    out_ref[...] = (picked + begun_ref[...].astype(jnp.float32)).astype(out_ref.dtype)


def pick(index, begun, last, first):
    return pl.pallas_call(
        functools.partial(pick_kernel, first),
        out_shape=jax.ShapeDtypeStruct(begun.shape, begun.dtype),
        in_specs=[VMEM] * 3,
        out_specs=VMEM,
        compiler_params=params(),
    )(index, begun, last)


def by_span(picked, spans, channels):
    per = picked[0].shape[0] // spans
    parts = []
    for c in range(spans):
        for array in picked:
            for t in range(array.shape[1] // channels):
                parts.append(array[c * per : (c + 1) * per, t * channels : (t + 1) * channels])
    return jnp.concatenate(parts, axis=0)


PAIR = 2


def pair_places(spans, columns):
    pairs = columns // (PAIR * HD)
    return [
        (c, slice(p * PAIR * HD, (p + 1) * PAIR * HD), c * pairs + p) for c in range(spans) for p in range(pairs)
    ]


def apart(query):
    none = jnp.zeros((query.shape[0], HD), query.dtype)
    upper = jnp.concatenate([query[:, :HD], none], axis=1)
    lower = jnp.concatenate([none, query[:, HD:]], axis=1)
    return jnp.concatenate([upper, lower], axis=0)


def score(spans, source, wk_ref, query_ref, scores_ref):
    keys = jnp.dot(source, wk_ref[...], preferred_element_type=jnp.float32).astype(jnp.bfloat16)
    per = keys.shape[0] // spans
    for c, lanes, n in pair_places(spans, keys.shape[1]):
        scores_ref[n] = lax.dot_general(
            keys[c * per : (c + 1) * per, lanes],
            apart(query_ref[c * SPAN : (c + 1) * SPAN, lanes]),
            (((1,), (1,)), ((), ())),
            preferred_element_type=jnp.float32,
        )


def score_kernel(spans, *refs):
    *picked, wk_ref, query_ref, scores_ref = refs
    score(spans, by_span(picked, spans, wk_ref.shape[0]), wk_ref, query_ref, scores_ref)


def tokens(picked, channels):
    return sum(array.size for array in picked) // channels


def scores_shape(picked, queries, channels, spans):
    return spans * (queries.shape[1] // (PAIR * HD)), tokens(picked, channels) // spans, PAIR * SPAN


def own_scores(picked, w_key, queries, spans):
    return pl.pallas_call(
        functools.partial(score_kernel, spans),
        out_shape=jax.ShapeDtypeStruct(scores_shape(picked, queries, w_key.shape[0], spans), jnp.float32),
        in_specs=[VMEM] * (2 + len(picked)),
        out_specs=VMEM,
        compiler_params=params(),
    )(*picked, w_key, queries)


def values_kernel(spans, *refs):
    *picked, wv_ref, values_ref = refs
    source = by_span(picked, spans, wv_ref.shape[0])
    values_ref[...] = jnp.dot(source, wv_ref[...], preferred_element_type=jnp.float32).astype(values_ref.dtype)


def own_values(picked, w_value, spans):
    return pl.pallas_call(
        functools.partial(values_kernel, spans),
        out_shape=jax.ShapeDtypeStruct((tokens(picked, w_value.shape[0]), w_value.shape[1]), picked[0].dtype),
        in_specs=[VMEM] * (1 + len(picked)),
        out_specs=VMEM,
        compiler_params=params(),
    )(*picked, w_value)


def attend_kernel(spans, *refs):
    others, refs = refs[:STREAMS], refs[STREAMS:]
    values_refs, refs = refs[:STREAMS], refs[STREAMS:]
    wk_ref, wv_ref, query_ref, first_ref, out_ref, second_ref, probs_ref, held_ref, sems = refs
    other = by_span(others, spans, wk_ref.shape[0])
    score(spans, other, wk_ref, query_ref, second_ref)
    per = other.shape[0] // spans
    more = jnp.dot(other, wv_ref[...], preferred_element_type=jnp.float32).astype(jnp.bfloat16)
    everything = pair_places(spans, more.shape[1])
    for c, lanes, n in everything:
        scores = jnp.concatenate([first_ref[n], second_ref[n]], axis=0)
        raised = jnp.exp2((scores - jnp.max(scores, axis=0, keepdims=True)) * EXPONENT)
        probs_ref[n] = (raised * (1.0 / jnp.sum(raised, axis=0, keepdims=True))).astype(jnp.bfloat16)
    copies = []
    for c in range(spans):
        here = pl.ds(c * SPAN, SPAN)
        for at, lanes, n in everything:
            if at != c:
                continue
            rows = slice(c * per, (c + 1) * per)
            owned = [ref[c * ref.shape[0] // spans : (c + 1) * ref.shape[0] // spans, lanes] for ref in values_refs]
            values = jnp.concatenate(owned + [more[rows, lanes]], axis=0)
            mixed = lax.dot_general(
                probs_ref[n], values, (((0,), (0,)), ((), ())), preferred_element_type=jnp.float32
            ).astype(out_ref.dtype)
            own = [mixed[h * SPAN : (h + 1) * SPAN, h * HD : (h + 1) * HD] for h in range(PAIR)]
            held_ref[here, lanes] = jnp.concatenate(own, axis=1)
        copies.append(pltpu.make_async_copy(held_ref.at[here, :], out_ref.at[here, :], sems.at[c]))
        copies[-1].start()
    for copy in copies:
        copy.wait()


def attend(others, w_key, w_value, queries, first, values, spans):
    each = scores_shape(others, queries, w_key.shape[0], spans)
    return pl.pallas_call(
        functools.partial(attend_kernel, spans),
        out_shape=jax.ShapeDtypeStruct(queries.shape, queries.dtype),
        in_specs=[VMEM] * (4 + len(others) + len(values)),
        out_specs=pl.BlockSpec(memory_space=pl.ANY),
        scratch_shapes=[
            pltpu.VMEM(each, jnp.float32),
            pltpu.VMEM((each[0], 2 * each[1], each[2]), jnp.bfloat16),
            pltpu.VMEM(queries.shape, queries.dtype),
            pltpu.SemaphoreType.DMA((spans,)),
        ],
        compiler_params=params(),
    )(*others, *values, w_key, w_value, queries, first)


def send(chunk, pairs):
    return lax.ppermute(chunk, "wide", pairs)


def gathered_plan(queries, encodings, w_key, w_value, block_owner, block_row):
    wide_count = lax.axis_size("wide")
    turns = wide_count // SIDE
    rows = encodings.shape[0]
    spans = queries.shape[0] // SPAN
    line = ring_order(turns)
    onward = [
        (here * SIDE + x, there * SIDE + x) for here, there in zip(line, line[1:] + line[:1]) for x in range(SIDE)
    ]
    across = [(n, n + 1 if n % SIDE == 0 else n - 1) for n in range(wide_count)]
    *pieces, whole = half_columns(encodings)
    order = [(0, 0)]
    for k in range(1, turns):
        order += [(k, 0), (k - 1, 1)]
    order.append((turns - 1, 1))
    index = places(order, turns, rows, jnp.transpose(block_owner, (0, 2, 1)), block_row)
    held = {(0, 0): pieces}
    for k in range(1, turns):
        behind = held[k - 1, 0]
        steps = [send(piece, onward) for piece in behind]
        if k < turns - 1:
            held[k - 1, 1] = [send(whole if k == 1 else jnp.concatenate(behind, axis=1), across)]
        else:
            held[k - 1, 1] = [send(piece, across) for piece in behind]
        held[k, 0] = steps
    straight, crossed = held[turns - 1, 0], held[turns - 2, 1]
    straight[0], crossed[0] = lax.optimization_barrier((straight[0], crossed[0]))
    held[turns - 1, 1] = [send(piece, across) for piece in held[turns - 1, 0]]
    sources = [held[chunk] for chunk in order]
    begun = early(index, sources[:-1], whole.shape[1])
    picked, values, others = [], [], []
    for piece, last in zip(begun, sources[-1]):
        if values:
            last, values[-1], others[-1] = lax.optimization_barrier((last, values[-1], others[-1]))
        picked.append(pick(index, piece, last, (len(order) - 1) * rows))
        others.append(lax.ppermute(picked[-1], "heads", [(0, 1), (1, 0)]))
        values.append(own_values(picked[-1:], w_value, spans))
    first = own_scores(picked, w_key, queries, spans)
    return attend(others, w_key, w_value, queries, first, values, spans)


def exchange(encodings, owners, stored, capacity):
    wide_count = lax.axis_size("wide")
    requests = owners.shape[0]
    order = jnp.arange(requests, dtype=jnp.int32)
    earlier = (owners[:, None] == owners[None, :]) & (order[None, :] < order[:, None])
    rank = jnp.sum(earlier.astype(jnp.int32), axis=1)
    slot = owners * capacity + rank
    table = jnp.full((wide_count * capacity,), -1, jnp.int32).at[slot].set(stored)
    table = table.reshape(wide_count, capacity)
    asked = lax.all_to_all(table, "wide", split_axis=0, concat_axis=0, tiled=True)
    wanted = jnp.maximum(asked, 0)
    picked = encodings[wanted]
    returned = lax.all_to_all(picked, "wide", split_axis=0, concat_axis=0, tiled=True)
    return returned.reshape(wide_count * capacity, encodings.shape[1])[slot]


def exchanged_plan(queries, encodings, w_key, w_value, owners, stored, capacity):
    fetched = exchange(encodings, owners, stored, capacity)
    channels = w_key.shape[0]
    source = fetched.reshape(-1, channels)
    keys = jnp.dot(source, w_key, preferred_element_type=jnp.float32).astype(jnp.bfloat16)
    values = jnp.dot(source, w_value, preferred_element_type=jnp.float32).astype(jnp.bfloat16)
    span_count = queries.shape[0] // SPAN
    heads_local = w_key.shape[1] // HD
    keys = keys.reshape(span_count, -1, heads_local, HD)
    values = values.reshape(span_count, -1, heads_local, HD)
    query_part = queries.reshape(span_count, SPAN, heads_local, HD)
    scores = jnp.einsum(
        "cqhd,ckhd->chqk", query_part, keys, preferred_element_type=jnp.float32
    ) * HD ** (-0.5)
    probs = jax.nn.softmax(scores, axis=-1).astype(jnp.bfloat16)
    mixed = jnp.einsum("chqk,ckhd->cqhd", probs, values, preferred_element_type=jnp.float32)
    return mixed.astype(jnp.bfloat16).reshape(queries.shape)


def on_device(queries, encodings, w_key, w_value, block_owner, block_row):
    wide_count = lax.axis_size("wide")
    requests = block_row.size
    capacity = 2 * ((requests + wide_count - 1) // wide_count)
    if encodings.shape[0] <= 2 * capacity:
        return gathered_plan(queries, encodings, w_key, w_value, block_owner, block_row)
    return exchanged_plan(
        queries, encodings, w_key, w_value, block_owner.reshape(-1), block_row.reshape(-1), capacity
    )


def solution(mesh):
    placed = (
        P(("groups", "wide"), "heads"),
        P(("groups", "wide"), None),
        P(None, "heads"),
        P(None, "heads"),
        P(("groups", "wide"), None, None),
        P(("groups", "wide"), None),
    )
    return jax.shard_map(
        on_device,
        mesh=mesh,
        in_specs=placed,
        out_specs=P(("groups", "wide"), "heads"),
        check_vma=False,
    )
```
